32 devices in a mesh: dp: 8 (over z, y), mp: 4 (over x, core).
Axes of the slice: x: 2, y: 2, z: 4, core: 2. Of those that a mesh axis runs over, the one named last changes fastest.
Arguments:
- layer_input: bfloat16 [8192, 1024], P('dp'), may hold values from -6 to 6
- output_cot: bfloat16 [8192, 1024], P('dp'), may hold values from -6 to 6
- score_cot: float32 [4, 16], replicated, may hold values from -24 to 24
- query_lengths: int32 [4, 16], replicated, may hold values from 1 to 128, 1024 in all within a row
- passage_lengths: int32 [4, 4], replicated, may hold values from 1 to 512, 1024 in all within a row
- pairing: int32 [4, 16], replicated, may hold values from 0 to 3
- match_offset: int32 [4, 1024], replicated, may hold values from 0 to 511
- block_order: int32 [4, 192], P('mp'), may hold values from 0 to 191, as said below
- block_master: float32 [768, 128, 128], P(('dp', 'mp'))
- block_first: float32 [768, 128, 128], P(('dp', 'mp'))
- block_second: float32 [768, 128, 128], P(('dp', 'mp')), as said below
- basis_left: float32 [768, 128, 128], P(('dp', 'mp')), as said below
- basis_right: float32 [768, 128, 128], P(('dp', 'mp')), as said below
- bias_state: float32 [3, 6144], P(None, 'mp'), as said below
- norm_state: float32 [3, 6, 1024], replicated, as said below
Outputs:
- output_rows: bfloat16 [8192, 1024], P('dp')
- scores: float32 [4, 16], replicated
- input_grad: bfloat16 [8192, 1024], P('dp')
- block_grad: float32 [768, 128, 128], P(('dp', 'mp'))
- block_first_new: float32 [768, 128, 128], P(('dp', 'mp'))
- block_second_new: float32 [768, 128, 128], P(('dp', 'mp'))
- block_master_new: float32 [768, 128, 128], P(('dp', 'mp'))
- bias_out: float32 [3, 6144], P(None, 'mp')
- norm_out: float32 [3, 6, 1024], replicated
- small_values: float32 [12288], P('mp')
The draws below stay inside these ranges and needn't reach their ends.
Inputs may be any that keep to these rules, and one draw needn't show every extreme that they name: `block_order`: each row is a permutation of the block ids of its shard; device (i, j) owns slots i * 24 to (i+1) * 24 - 1 of row j. `query_lengths`: each row sums to 1024 and its largest entry is 128. `passage_lengths`: each row sums to 1024 and its largest entry is 512. `basis_left`: each block is an orthogonal matrix. `basis_right`: each block is an orthogonal matrix. `block_second`: entries are positive. `bias_state`: row 2 is positive. `norm_state`: row 2 is positive.
All inputs are finite; a program needn't handle non-finite values.
Results may differ from the reference program's by a relative error of at most 0.017.
Values may be sent and summed in bfloat16 or wider, within the bound.
No kernel may reach another device: no remote copies, remote signals or barrier semaphores. Data moves between devices by JAX's collectives and lax.ppermute only.
A program may use at most 192 MiB of HBM per device.

```python
import math
import jax
import jax.numpy as jnp
import numpy as np
from jax import lax

D = 1024
H = 16
HD = 64
FF = 4096
ROW = 1024
NQ = 16
QMAX = 128
NP = 4
PMAX = 512
BLK = 128
STEP = 10
TOKENS = 8192
NPAIR = 4
LW = 256
FFL = 1024
SB = 1536
NB_MP = 192
NBLK = 768
N_DP = 8
N_MP = 4


def order_table(key):
    base_key = jax.random.fold_in(key, 101)
    return jnp.stack([jax.random.permutation(jax.random.fold_in(base_key, shard_index), NB_MP).astype(jnp.int32) for shard_index in range(N_MP)])


def slot_ids(key):
    owned_count = NB_MP // N_DP
    return jnp.swapaxes(order_table(key).reshape(N_MP, N_DP, owned_count), 0, 1).reshape(NBLK)


def block_scales(key):
    block_ids = slot_ids(key)
    row_blocks = D // BLK
    qkv_columns = 3 * LW // BLK
    qkv_count = row_blocks * qkv_columns
    out_count = LW // BLK * row_blocks
    up_count = row_blocks * (FFL // BLK)
    value_block = block_ids % qkv_columns >= 2 * (LW // BLK)
    in_qkv = block_ids < qkv_count
    in_out = block_ids < qkv_count + out_count
    in_up = block_ids < qkv_count + out_count + up_count
    weight_scale = jnp.where(in_qkv, D ** (-0.5), jnp.where(in_out, 4.0 * D ** (-0.5), jnp.where(in_up, D ** (-0.5), FF ** (-0.5))))
    grad_factor = jnp.where(in_qkv, jnp.where(value_block, 0.8, 0.15), jnp.where(in_out, 0.2, jnp.where(in_up, 0.3, 0.6)))
    return (weight_scale.astype(jnp.float32)[:, None, None], (grad_factor * TOKENS ** 0.5).astype(jnp.float32)[:, None, None])


def spread_factor(key, shape):
    return jnp.exp(jax.random.uniform(key, shape, jnp.float32, jnp.log(0.5), jnp.log(2.0)))


def draw_block_order(key, part):
    return order_table(key)


def draw_block_master(key, part):
    weight_scale, grad_scale = block_scales(key)
    return jax.random.normal(jax.random.fold_in(key, 202), (NBLK, BLK, BLK), jnp.float32) * weight_scale


def draw_block_first(key, part):
    weight_scale, grad_scale = block_scales(key)
    return jax.random.normal(jax.random.fold_in(key, 303), (NBLK, BLK, BLK), jnp.float32) * grad_scale * (0.1 / 0.9)


def draw_block_second(key, part):
    weight_scale, grad_scale = block_scales(key)
    return grad_scale * grad_scale * (0.001 / 0.999) * 2.0 * spread_factor(jax.random.fold_in(key, 404), (NBLK, BLK, BLK))


def draw_basis_left(key, part):
    basis, upper = jnp.linalg.qr(jax.random.normal(jax.random.fold_in(key, 505), (NBLK, BLK, BLK), jnp.float32))
    return basis


def draw_basis_right(key, part):
    basis, upper = jnp.linalg.qr(jax.random.normal(jax.random.fold_in(key, 606), (NBLK, BLK, BLK), jnp.float32))
    return basis


def draw_bias_state(key, part):
    position = jnp.arange(N_MP * SB, dtype=jnp.int32) % SB
    grad_scale = jnp.where(position < LW, 0.15, jnp.where(position < 2 * LW, 0.8, 0.3)).astype(jnp.float32) * TOKENS ** 0.5
    values = 0.3 * jax.random.normal(jax.random.fold_in(key, 707), (N_MP * SB,), jnp.float32)
    first_state = grad_scale * (0.1 / 0.9) * jax.random.normal(jax.random.fold_in(key, 708), (N_MP * SB,), jnp.float32)
    second_state = grad_scale * grad_scale * (0.001 / 0.999) * 2.0 * spread_factor(jax.random.fold_in(key, 709), (N_MP * SB,))
    return jnp.stack([values, first_state, second_state])


def draw_norm_state(key, part):
    row_kind = jnp.arange(6, dtype=jnp.int32)[:, None]
    is_gain = (row_kind == 2) | (row_kind == 4)
    noise = jax.random.normal(jax.random.fold_in(key, 801), (6, D), jnp.float32)
    values = jnp.where(is_gain, 1.0 + 0.1 * noise, 0.3 * noise)
    grad_scale = TOKENS ** 0.5
    first_state = grad_scale * (0.1 / 0.9) * jax.random.normal(jax.random.fold_in(key, 802), (6, D), jnp.float32)
    second_state = grad_scale * grad_scale * (0.001 / 0.999) * 2.0 * spread_factor(jax.random.fold_in(key, 803), (6, D))
    return jnp.stack([values, first_state, second_state])


def set_ends(array, key, low, largest):
    longest = array.shape.index(max(array.shape))
    spots = []
    for shift in (0, 1):
        where = [jax.random.randint(jax.random.fold_in(key, axis), (), 0, length) for axis, length in enumerate(array.shape)]
        where[longest] = (where[longest] + shift) % array.shape[longest]
        spots.append(tuple(where))
    return array.at[spots[0]].set(low).at[spots[1]].set(largest)


def steps_of(rng, dims, shards, least, high):
    def one(dim, blocks):
        heights = jax.random.uniform(jax.random.fold_in(jax.random.fold_in(rng, 6), dim), (blocks,), jnp.float32, least / len(shards), high / len(shards))
        return jnp.repeat(jnp.exp(heights), dims[dim] // blocks).reshape((-1,) + (1,) * (len(dims) - dim - 1))

    loudness = one(*shards[0])
    for cut in shards[1:]:
        loudness = loudness * one(*cut)
    return loudness


def split_up(count, total, most, slope):
    loads = [(1 << 20) // math.isqrt(rank ** slope) + 1 for rank in range(2, count + 1)]
    surplus, counts = total - most - (count - 1), [1] * (count - 1)
    while surplus > 0:
        movable = [i for i in range(count - 1) if counts[i] < most]
        pool, budget = sum([loads[i] for i in movable]), surplus
        for i in movable:
            extra = min(most - counts[i], max(1, budget * loads[i] // pool), surplus)
            counts[i] = counts[i] + extra
            surplus = surplus - extra
    return np.array([most] + counts)


def ragged(own_key, count, total, limit, slope):
    if count == 2:
        one = jax.random.randint(own_key, (), max(1, total - limit), min(limit, total - 1) + 1)
        return jnp.stack([one, total - one])
    tallies = jnp.asarray(split_up(count, total, limit, slope), jnp.int32)
    pairs = (count - 1) // 2
    donor, taker = tallies[1:1 + 2 * pairs:2], tallies[2:2 + 2 * pairs:2]
    room = jnp.minimum(donor - 1, limit - taker)
    shifted = jax.random.randint(jax.random.fold_in(own_key, 1), (pairs,), 0, 1 << 20) % (room + 1)
    tallies = tallies.at[1:1 + 2 * pairs:2].set(donor - shifted).at[2:2 + 2 * pairs:2].set(taker + shifted)
    return tallies[jax.random.permutation(jax.random.fold_in(own_key, 2), count)]


def centred(rng, shape, spread, most, pieces=(), kind=jnp.bfloat16):
    entries = jax.random.normal(rng, shape, jnp.float32) * spread
    if len(pieces) > 0:
        entries = steps_of(rng, shape, pieces, -0.22, 0.18) * entries
    return jnp.clip(entries, min=-most, max=most).astype(kind)


def setup_inputs(seed: int = 0) -> dict:
    keys = jax.random.split(jax.random.key(seed), 16)
    return {
        "layer_input": centred(keys[0], (TOKENS, D), 1.0, 6.0, ((0, 8),)),
        "output_cot": centred(keys[1], (TOKENS, D), 1.0, 6.0, ((0, 8),)),
        "score_cot": centred(keys[2], (NPAIR, NQ), 4.0, 24.0, (), jnp.float32),
        "query_lengths": jax.vmap(lambda own: ragged(own, NQ, ROW, QMAX, 1))(jax.random.split(keys[3], NPAIR)).reshape((NPAIR, NQ)).astype(jnp.int32),
        "passage_lengths": jax.vmap(lambda own: ragged(own, NP, ROW, PMAX, 2))(jax.random.split(keys[4], NPAIR)).reshape((NPAIR, NP)).astype(jnp.int32),
        "pairing": set_ends(jax.random.randint(keys[5], (NPAIR, NQ), 0, NP), jax.random.fold_in(keys[5], 1), 0, NP - 1).astype(jnp.int32),
        "match_offset": set_ends(jax.random.randint(keys[6], (NPAIR, ROW), 0, PMAX), jax.random.fold_in(keys[6], 1), 0, PMAX - 1).astype(jnp.int32),
        "block_order": draw_block_order(jax.random.fold_in(keys[15], 71), 0),
        "block_master": draw_block_master(jax.random.fold_in(keys[15], 71), 0),
        "block_first": draw_block_first(jax.random.fold_in(keys[15], 71), 0),
        "block_second": draw_block_second(jax.random.fold_in(keys[15], 71), 0),
        "basis_left": draw_basis_left(jax.random.fold_in(keys[15], 71), 0),
        "basis_right": draw_basis_right(jax.random.fold_in(keys[15], 71), 0),
        "bias_state": draw_bias_state(jax.random.fold_in(keys[15], 71), 0),
        "norm_state": draw_norm_state(jax.random.fold_in(keys[15], 71), 0),
    }


@jax.custom_vjp
def low(v):
    return lax.optimization_barrier(v.astype(jnp.bfloat16)).astype(jnp.float32)

@jax.custom_vjp
def low_back(v):
    return v

def low_keep(v):
    return (low(v), None)

def low_pass(kept, grad):
    return (grad,)

def back_keep(v):
    return (v, None)

def back_low(kept, grad):
    return (low(grad),)
low.defvjp(low_keep, low_pass)
low_back.defvjp(back_keep, back_low)
highest = lax.Precision.HIGHEST
beta_one = 0.9
beta_two = 0.999
adam_eps = 1e-08
norm_eps = 1e-05
block_rate = 0.05
small_rate = 0.1

def product(left, right):
    return jnp.dot(left.astype(jnp.float32), right.astype(jnp.float32), precision=highest, preferred_element_type=jnp.float32)

def both_low(values):
    return low_back(low(values))

def layer_norm(values, norm_gain, norm_shift):
    center = values - lax.optimization_barrier(jnp.mean(values, axis=-1, keepdims=True))
    inverse = lax.rsqrt(lax.optimization_barrier(jnp.mean(center * center, axis=-1, keepdims=True)) + norm_eps)
    return norm_gain * (center * inverse) + norm_shift

def segment_index(lengths, places):
    segment_ends = jnp.cumsum(lengths)
    return lax.optimization_barrier(jnp.sum((places[:, None] >= segment_ends[None, :]).astype(jnp.int32), axis=1))

def to_blocks(matrix):
    row_total, column_total = matrix.shape
    return matrix.reshape(row_total // BLK, BLK, column_total // BLK, BLK).transpose(0, 2, 1, 3).reshape(-1, BLK, BLK)

def join_blocks(blocks, row_total, column_total):
    return blocks.reshape(row_total // BLK, column_total // BLK, BLK, BLK).transpose(0, 2, 1, 3).reshape(row_total, column_total)

def encode(params, tokens, same_doc):
    w_query, w_key, w_value, w_out, w_up, w_down, b_query, b_value, b_up, b_attn, b_down, gain_one, shift_one, gain_two, shift_two = params
    query_rows = both_low(product(tokens, w_query) + b_query).reshape(ROW, H, HD)
    key_rows = both_low(product(tokens, w_key)).reshape(ROW, H, HD)
    value_rows = both_low(product(tokens, w_value) + b_value).reshape(ROW, H, HD)
    raw_scores = jnp.einsum('qhd,khd->hqk', query_rows, key_rows, precision=highest) * HD ** (-0.5)
    logits = jnp.where(same_doc[None], low_back(raw_scores), -jnp.inf)
    exponent = jnp.exp(logits - lax.optimization_barrier(jnp.max(logits, axis=-1, keepdims=True)))
    probs_low = low(exponent / lax.optimization_barrier(jnp.sum(exponent, axis=-1, keepdims=True)))
    context = both_low(jnp.einsum('hqk,khd->qhd', probs_low, value_rows, precision=highest).reshape(ROW, H * HD))
    attn_out = low_back(product(context, w_out))
    first_norm = layer_norm(tokens + attn_out + b_attn, gain_one, shift_one)
    pre_act = low_back(product(low(first_norm), w_up) + b_up)
    hidden = low(jax.nn.gelu(pre_act, approximate=False))
    ffn_out = low_back(product(hidden, w_down))
    return layer_norm(first_norm + ffn_out + b_down, gain_two, shift_two)

def adam_plain(grad_now, first_old, second_old, value_old, rate_now):
    first_new = beta_one * first_old + (1.0 - beta_one) * grad_now
    second_new = beta_two * second_old + (1.0 - beta_two) * grad_now * grad_now
    step_dir = first_new / (1.0 - beta_one ** STEP) / (jnp.sqrt(second_new / (1.0 - beta_two ** STEP)) + adam_eps)
    return (first_new, second_new, value_old - rate_now * step_dir)

def reference(layer_input, output_cot, score_cot, query_lengths, passage_lengths, pairing, match_offset, block_order, block_master, block_first, block_second, basis_left, basis_right, bias_state, norm_state):
    owned_count = NB_MP // N_DP
    shapes_list = [(D, 3 * LW), (LW, D), (D, FFL), (FFL, D)]

    def global_to_slots(blocks):
        return jnp.swapaxes(blocks.reshape(N_DP, N_MP, owned_count, BLK, BLK), 0, 1).reshape(N_MP, NB_MP, BLK, BLK)

    def slots_to_global(blocks):
        return jnp.swapaxes(blocks.reshape(N_MP, N_DP, owned_count, BLK, BLK), 0, 1).reshape(NBLK, BLK, BLK)
    slots = global_to_slots(block_master)
    block_range = jnp.arange(NB_MP, dtype=jnp.int32)
    shard_mats = [[], [], [], []]
    for shard_index in range(N_MP):
        slot_of = jnp.zeros((NB_MP,), jnp.int32).at[block_order[shard_index]].set(block_range)
        canonical = low(jnp.take(slots[shard_index], slot_of, axis=0))
        offset_now = 0
        for kind_index in range(4):
            row_total, column_total = shapes_list[kind_index]
            count_now = row_total // BLK * (column_total // BLK)
            shard_mats[kind_index].append(join_blocks(canonical[offset_now:offset_now + count_now], row_total, column_total))
            offset_now = offset_now + count_now
    w_query = jnp.concatenate([matrix[:, :LW] for matrix in shard_mats[0]], axis=1)
    w_key = jnp.concatenate([matrix[:, LW:2 * LW] for matrix in shard_mats[0]], axis=1)
    w_value = jnp.concatenate([matrix[:, 2 * LW:] for matrix in shard_mats[0]], axis=1)
    w_out = jnp.concatenate(shard_mats[1], axis=0)
    w_up = jnp.concatenate(shard_mats[2], axis=1)
    w_down = jnp.concatenate(shard_mats[3], axis=0)
    bias_shards = bias_state[0].reshape(N_MP, SB)
    b_query = bias_shards[:, :LW].reshape(-1)
    b_value = bias_shards[:, LW:2 * LW].reshape(-1)
    b_up = bias_shards[:, 2 * LW:].reshape(-1)
    norm_now = norm_state[0]
    params = (w_query, w_key, w_value, w_out, w_up, w_down, b_query, b_value, b_up, norm_now[0], norm_now[1], norm_now[2], norm_now[3], norm_now[4], norm_now[5])
    input_float = layer_input.astype(jnp.float32)
    cot_float = output_cot.astype(jnp.float32)
    places = jnp.arange(ROW, dtype=jnp.int32)
    pair_scale = D ** (-0.5)

    def pair_step(carry, pair_index):
        query_tokens = lax.dynamic_slice_in_dim(input_float, pair_index * ROW, ROW, 0)
        passage_tokens = lax.dynamic_slice_in_dim(input_float, (pair_index + NPAIR) * ROW, ROW, 0)
        query_cot = lax.dynamic_slice_in_dim(cot_float, pair_index * ROW, ROW, 0)
        passage_cot = lax.dynamic_slice_in_dim(cot_float, (pair_index + NPAIR) * ROW, ROW, 0)
        query_seg = segment_index(query_lengths[pair_index], places)
        passage_row = passage_lengths[pair_index]
        passage_seg = segment_index(passage_row, places)
        passage_start = jnp.cumsum(passage_row) - passage_row
        paired = pairing[pair_index][query_seg]
        target = passage_start[paired] + jnp.remainder(match_offset[pair_index], passage_row[paired])
        query_same = query_seg[:, None] == query_seg[None, :]
        passage_same = passage_seg[:, None] == passage_seg[None, :]

        def forward(params_in, query_in, passage_in):
            query_out = encode(params_in, query_in, query_same)
            passage_out = encode(params_in, passage_in, passage_same)
            passage_low = low(passage_out)
            token_score = lax.optimization_barrier(jnp.sum(low(query_out) * passage_low[target], axis=1))
            return (query_out, passage_out, jax.ops.segment_sum(token_score, query_seg, num_segments=NQ) * pair_scale)
        outputs, pullback = jax.vjp(forward, params, query_tokens, passage_tokens)
        param_grads, query_grad, passage_grad = pullback((query_cot, passage_cot, score_cot[pair_index]))
        carry = jax.tree.map(lambda running, addend: running + addend, carry, param_grads)
        return (carry, (outputs[0], outputs[1], outputs[2], query_grad, passage_grad))
    zero_grads = jax.tree.map(jnp.zeros_like, params)
    grads, stacked = lax.scan(pair_step, zero_grads, jnp.arange(NPAIR, dtype=jnp.int32))
    output_rows = jnp.concatenate([stacked[0].reshape(-1, D), stacked[1].reshape(-1, D)], axis=0).astype(jnp.bfloat16)
    scores = stacked[2]
    input_grad = jnp.concatenate([stacked[3].reshape(-1, D), stacked[4].reshape(-1, D)], axis=0).astype(jnp.bfloat16)
    grad_query, grad_key, grad_value, grad_out, grad_up, grad_down, grad_bquery, grad_bvalue, grad_bup, grad_battn, grad_bdown, grad_gone, grad_sone, grad_gtwo, grad_stwo = grads
    slot_grads = []
    bias_grads = []
    for shard_index in range(N_MP):
        head_cols = slice(shard_index * LW, (shard_index + 1) * LW)
        unit_cols = slice(shard_index * FFL, (shard_index + 1) * FFL)
        qkv_grad = jnp.concatenate([grad_query[:, head_cols], grad_key[:, head_cols], grad_value[:, head_cols]], axis=1)
        canonical_grad = jnp.concatenate([to_blocks(qkv_grad), to_blocks(grad_out[head_cols]), to_blocks(grad_up[:, unit_cols]), to_blocks(grad_down[unit_cols])], axis=0)
        slot_grads.append(jnp.take(canonical_grad, block_order[shard_index], axis=0))
        bias_grads.append(jnp.concatenate([grad_bquery[head_cols], grad_bvalue[head_cols], grad_bup[unit_cols]]))
    block_grad = slots_to_global(jnp.stack(slot_grads))
    bias_grad = jnp.concatenate(bias_grads)
    norm_grad = jnp.stack([grad_battn, grad_bdown, grad_gone, grad_sone, grad_gtwo, grad_stwo])
    first_new = beta_one * block_first + (1.0 - beta_one) * block_grad
    rotated_grad = jnp.einsum('kac,kcd->kad', jnp.einsum('kba,kbc->kac', basis_left, block_grad, precision=highest), basis_right, precision=highest)
    rotated_first = jnp.einsum('kac,kcd->kad', jnp.einsum('kba,kbc->kac', basis_left, first_new, precision=highest), basis_right, precision=highest)
    second_new = beta_two * block_second + (1.0 - beta_two) * rotated_grad * rotated_grad
    rotated_step = rotated_first / (1.0 - beta_one ** STEP) / (jnp.sqrt(second_new / (1.0 - beta_two ** STEP)) + adam_eps)
    step_back = jnp.einsum('kac,kdc->kad', jnp.einsum('kab,kbc->kac', basis_left, rotated_step, precision=highest), basis_right, precision=highest)
    master_new = block_master - block_rate * step_back
    bias_first, bias_second, bias_value = adam_plain(bias_grad, bias_state[1], bias_state[2], bias_state[0], small_rate)
    norm_first, norm_second, norm_value = adam_plain(norm_grad, norm_state[1], norm_state[2], norm_state[0], small_rate)
    bias_out = jnp.stack([bias_grad, bias_first, bias_second])
    norm_out = jnp.stack([norm_grad, norm_first, norm_second])
    small_values = jnp.concatenate([bias_value.reshape(N_MP, SB), norm_value.reshape(N_MP, 6 * D // N_MP)], axis=1).reshape(-1)
    return (output_rows, scores, input_grad, block_grad, first_new, second_new, master_new, bias_out, norm_out, small_values)
```

```python
import functools

import jax
import jax.numpy as jnp
from jax import lax
from jax.experimental import pallas as pl
from jax.experimental.pallas import tpu as pltpu
from jax.sharding import PartitionSpec as P

D = 1024
H = 16
HD = 64
FF = 4096
ROW = 1024
STEP = 10
TILE = 256

low = jnp.bfloat16
wide = jnp.float32
beta_one = 0.9
beta_two = 0.999
adam_eps = 1e-08
norm_eps = 1e-05
block_rate = 0.05
small_rate = 0.1
vmem_bytes = 48 * 1024 * 1024

NN = (((1,), (0,)), ((), ()))
NT = (((1,), (1,)), ((), ()))
TN = (((0,), (0,)), ((), ()))


def mul(left, right, dims=NN):
    return lax.dot_general(left, right, dims, preferred_element_type=wide)


def layer_norm(values, norm_gain, norm_shift):
    center = values - jnp.mean(values, axis=1, keepdims=True)
    inverse = lax.rsqrt(jnp.mean(center * center, axis=1, keepdims=True) + norm_eps)
    normed = center * inverse
    return (norm_gain * normed + norm_shift, normed, inverse)


def norm_back(grad_rows, norm_gain, normed, inverse):
    scaled = grad_rows * norm_gain
    first_mean = jnp.mean(scaled, axis=1, keepdims=True)
    second_mean = jnp.mean(scaled * normed, axis=1, keepdims=True)
    return inverse * (scaled - first_mean - normed * second_mean)


def gelu_parts(values):
    normal_cdf = 0.5 * (1.0 + lax.erf(values * 0.7071067811865476))
    slope = normal_cdf + values * jnp.exp(-0.5 * values * values) * 0.3989422804014327
    return ((values * normal_cdf).astype(low), slope)


def adam_plain(grad_now, first_old, second_old, value_old, rate_now):
    first_new = beta_one * first_old + (1.0 - beta_one) * grad_now
    second_new = beta_two * second_old + (1.0 - beta_two) * grad_now * grad_now
    step_dir = (
        first_new
        / (1.0 - beta_one**STEP)
        / (jnp.sqrt(second_new / (1.0 - beta_two**STEP)) + adam_eps)
    )
    return (first_new, second_new, value_old - rate_now * step_dir)


def ring_order(count):
    return [k for k in range(count) if k % 2 == 0] + [k for k in range(count) if k % 2][::-1]


def piece_bounds(owned):
    pieces = min(4, owned)
    return [owned * k // pieces for k in range(pieces + 1)]


def block_spans(shapes_list, side):
    spans = []
    start = 0
    for rows, columns in shapes_list:
        size = rows * columns // (side * side)
        spans.append((start, start + size))
        start += size
    return spans


def each_block(ids_ref, base, count, matrices, spans, side, move):
    def step(w, carry):
        block_id = ids_ref[base + w]
        for matrix, (first, last) in zip(matrices, spans):
            columns = matrix.shape[1] // side

            @pl.when((block_id >= first) & (block_id < last))
            def _():
                place = block_id - first
                row = pl.multiple_of(place // columns * side, side)
                column = pl.multiple_of(place % columns * side, side)
                move(w, matrix.at[pl.ds(row, side), pl.ds(column, side)])

        return carry

    lax.fori_loop(0, count, step, 0)


def assemble(pieces, ids, shapes_list, side):
    spans = block_spans(shapes_list, side)

    def kernel(ids_ref, *refs):
        parts, outs = refs[: len(pieces)], refs[len(pieces) :]
        base = 0
        for part in parts:

            def move(w, view, part=part):
                view[...] = part[w]

            each_block(ids_ref, base, part.shape[0], outs, spans, side, move)
            base += part.shape[0]

    vmem = pl.BlockSpec(memory_space=pltpu.VMEM)
    return pl.pallas_call(
        kernel,
        in_specs=[pl.BlockSpec(memory_space=pltpu.SMEM)] + [vmem] * len(pieces),
        out_specs=[vmem] * len(shapes_list),
        out_shape=[jax.ShapeDtypeStruct(shape, low) for shape in shapes_list],
        compiler_params=pltpu.CompilerParams(vmem_limit_bytes=vmem_bytes),
        cost_estimate=pl.CostEstimate(flops=0, bytes_accessed=12 * 2**20, transcendentals=0),
        name="assemble",
    )(ids, *pieces)


def spread(matrices, ids, sizes, side):
    spans = block_spans([m.shape for m in matrices], side)

    def kernel(ids_ref, *refs):
        sources, outs = refs[: len(matrices)], refs[len(matrices) :]
        base = 0
        for out in outs:

            def move(w, view, out=out):
                out[w] = view[...]

            each_block(ids_ref, base, out.shape[0], sources, spans, side, move)
            base += out.shape[0]

    vmem = pl.BlockSpec(memory_space=pltpu.VMEM)
    return pl.pallas_call(
        kernel,
        in_specs=[pl.BlockSpec(memory_space=pltpu.SMEM)] + [vmem] * len(matrices),
        out_specs=[vmem] * len(sizes),
        out_shape=[jax.ShapeDtypeStruct((size, side, side), low) for size in sizes],
        compiler_params=pltpu.CompilerParams(vmem_limit_bytes=vmem_bytes),
        cost_estimate=pl.CostEstimate(flops=0, bytes_accessed=12 * 2**20, transcendentals=0),
        name="spread",
    )(ids, *matrices)


def pair_tables(place, query_lengths, passage_lengths, pairing, score_cot, match_offset):
    queries, passages = query_lengths.shape[1], passage_lengths.shape[1]
    half = ROW // 2
    pair_scale = D ** (-0.5)

    def kernel(place_ref, ql_ref, pl_ref, pair_ref, cot_ref, offset_ref, link_ref, col_ref, row_ref):
        is_query = place_ref[0] == 1
        row = place_ref[1]
        first_core = place_ref[2] == 0
        token = lax.broadcasted_iota(jnp.int32, (1, ROW), 1)
        zero = jnp.zeros((1, ROW), jnp.int32)
        segment, start_at, length_at = zero, zero, zero
        cot = jnp.zeros((1, ROW), wide)
        start = jnp.int32(0)
        for e in range(queries):
            end = start + ql_ref[row, e]
            inside = (token >= start) & (token < end)
            chosen = pair_ref[row, e]
            before = jnp.int32(0)
            length = jnp.int32(1)
            for m in range(passages):
                span = pl_ref[row, m]
                before = before + jnp.where(m < chosen, span, 0)
                length = jnp.where(m == chosen, span, length)
            segment = jnp.where(inside, e, segment)
            start_at = jnp.where(inside, before, start_at)
            length_at = jnp.where(inside, length, length_at)
            cot = jnp.where(inside, cot_ref[row, e] * pair_scale, cot)
            start = end
        passage = zero
        start = jnp.int32(0)
        for m in range(passages):
            start = start + pl_ref[row, m]
            passage = passage + (token >= start).astype(jnp.int32)
        length_at = jnp.maximum(length_at, 1)
        target = start_at + lax.rem(offset_ref[pl.ds(row, 1), :], length_at)
        own = jnp.where(is_query, segment, passage)

        def turn(value):
            swapped = jnp.concatenate([value[:, half:], value[:, :half]], axis=1)
            return jnp.where(first_core, value, swapped)

        token = turn(token)
        target, cot, segment, own = turn(target), turn(cot), turn(segment), turn(own)
        stacked = jnp.concatenate(
            [target.astype(wide), cot, segment.astype(wide), own.astype(wide)]
            + [token.astype(wide)]
            + [jnp.zeros((3, ROW), wide)],
            axis=0,
        )
        columns = stacked.T
        col_ref[...] = columns
        row_ref[...] = own.astype(wide)
        left = jnp.where(is_query, columns[:half, 0:1], columns[:half, 4:5])
        right = jnp.where(is_query, token, target).astype(wide)
        value = jnp.where(is_query, jnp.ones_like(cot), cot)
        link_ref[...] = jnp.where(left == right, value, 0.0).astype(low)

    smem = pl.BlockSpec(memory_space=pltpu.SMEM)
    vmem = pl.BlockSpec(memory_space=pltpu.VMEM)
    return pl.pallas_call(
        kernel,
        in_specs=[smem] * 5 + [vmem],
        out_specs=[vmem] * 3,
        out_shape=[
            jax.ShapeDtypeStruct((half, ROW), low),
            jax.ShapeDtypeStruct((ROW, 8), wide),
            jax.ShapeDtypeStruct((1, ROW), wide),
        ],
        compiler_params=pltpu.CompilerParams(vmem_limit_bytes=vmem_bytes),
        name="pair_tables",
    )(place, query_lengths, passage_lengths, pairing, score_cot, match_offset)


def halves(value):
    top = value.astype(low)
    return (top, (value - top.astype(wide)).astype(low))


def mul_split(left, right, dims=NN):
    left_top, left_rest = left
    right_top, right_rest = right
    return (
        mul(left_top, right_rest, dims) + mul(left_rest, right_top, dims)
    ) + mul(left_top, right_top, dims)


def rotate_first(blocks, left_basis, right_basis):
    count, side = blocks.shape[0], blocks.shape[1]
    group = 6 if count % 6 == 0 else 3 if count % 3 == 0 else 1

    def kernel(m_ref, l_ref, r_ref, out_ref):
        for b in range(group):
            inner = mul_split(halves(l_ref[b].T), halves(m_ref[b]))
            out_ref[b] = mul_split(halves(inner), halves(r_ref[b]))

    spec = pl.BlockSpec((group, side, side), lambda t: (t, 0, 0))
    return pl.pallas_call(
        kernel,
        grid=(count // group,),
        in_specs=[spec] * 3,
        out_specs=spec,
        out_shape=jax.ShapeDtypeStruct(blocks.shape, wide),
        compiler_params=pltpu.CompilerParams(vmem_limit_bytes=vmem_bytes),
        cost_estimate=pl.CostEstimate(
            flops=count * 12 * side**3, bytes_accessed=16 * count * side**2, transcendentals=0
        ),
        name="rotate_first",
    )(blocks, left_basis, right_basis)


def optimize(grad, rotated_old, master, first, second, left_basis, right_basis):
    count, side = grad.shape[0], grad.shape[1]
    group = 6 if count % 6 == 0 else 3 if count % 3 == 0 else 1

    def kernel(g_ref, c_ref, w_ref, m_ref, v_ref, l_ref, r_ref, m_out, v_out, w_out):
        for b in range(group):
            grad_now = g_ref[b]
            m_out[b] = beta_one * m_ref[b] + (1.0 - beta_one) * grad_now
            left, right = l_ref[b], r_ref[b]
            right_parts = halves(right)
            inner = mul_split(halves(left.T), halves(grad_now))
            turned = mul_split(halves(inner), right_parts)
            second_new = beta_two * v_ref[b] + (1.0 - beta_two) * turned * turned
            v_out[b] = second_new
            first_turned = beta_one * c_ref[b] + (1.0 - beta_one) * turned
            step = (first_turned / (1.0 - beta_one**STEP)) / (
                jnp.sqrt(second_new / (1.0 - beta_two**STEP)) + adam_eps
            )
            inner = mul_split(halves(left), halves(step))
            w_out[b] = w_ref[b] - block_rate * mul_split(halves(inner), right_parts, NT)

    spec = pl.BlockSpec((group, side, side), lambda t: (t, 0, 0))
    return pl.pallas_call(
        kernel,
        grid=(count // group,),
        in_specs=[spec] * 7,
        out_specs=[spec] * 3,
        out_shape=[jax.ShapeDtypeStruct(grad.shape, wide)] * 3,
        compiler_params=pltpu.CompilerParams(vmem_limit_bytes=vmem_bytes),
        cost_estimate=pl.CostEstimate(
            flops=count * 24 * side**3, bytes_accessed=40 * count * side**2, transcendentals=0
        ),
        name="optimize",
    )(grad, rotated_old, master, first, second, left_basis, right_basis)


def head_mask(head):
    lane = lax.broadcasted_iota(jnp.int32, (1, 2 * HD), 1)
    return ((lane // HD) == head).astype(low)


def attention_forward(qkv, seg_column, seg_row):
    width = qkv.shape[1] // 3
    pairs = width // (2 * HD)

    def kernel(q_ref, k_ref, v_ref, sk_ref, sq_ref, ctx_ref, lse_ref):
        same = sk_ref[:, 3:4] == sq_ref[...]
        for pair in range(pairs):
            lanes = slice(pair * 2 * HD, (pair + 1) * 2 * HD)
            q = q_ref[:, lanes] * jnp.asarray(HD**-0.5, low)
            k = k_ref[:, lanes]
            v_t = v_ref[:, lanes].T
            parts = []
            for head in range(2):
                s = jnp.where(same, mul(k, q * head_mask(head), NT), -1e30)
                peak = jnp.max(s, axis=0, keepdims=True)
                e = jnp.exp(s - peak)
                total = jnp.sum(e, axis=0, keepdims=True)
                part = mul(v_t[head * HD : (head + 1) * HD], e.astype(low))
                parts.append(part * (1.0 / total))
                lse_ref[pair * 2 + head : pair * 2 + head + 1, :] = peak + jnp.log(total)
            ctx_ref[:, lanes] = jnp.concatenate(parts, axis=0).T.astype(low)

    rows = qkv.shape[0]
    return pl.pallas_call(
        kernel,
        grid=(rows // TILE,),
        in_specs=[
            pl.BlockSpec((TILE, width), lambda t: (t, 0)),
            pl.BlockSpec((rows, width), lambda t: (0, 1)),
            pl.BlockSpec((rows, width), lambda t: (0, 2)),
            pl.BlockSpec((rows, 8), lambda t: (0, 0)),
            pl.BlockSpec((1, TILE), lambda t: (0, t)),
        ],
        out_specs=[
            pl.BlockSpec((TILE, width), lambda t: (t, 0)),
            pl.BlockSpec((2 * pairs, TILE), lambda t: (0, t)),
        ],
        out_shape=[
            jax.ShapeDtypeStruct((rows, width), low),
            jax.ShapeDtypeStruct((2 * pairs, rows), wide),
        ],
        compiler_params=pltpu.CompilerParams(vmem_limit_bytes=vmem_bytes),
        cost_estimate=pl.CostEstimate(
            flops=4 * rows * rows * 256 * 4, bytes_accessed=4 * 2**20, transcendentals=4 * rows * rows
        ),
        name="attention_forward",
    )(qkv, qkv, qkv, seg_column, seg_row)


def attention_backward(qkv, ctx, ctx_grad, lse, seg_column, seg_row):
    width = qkv.shape[1] // 3
    pairs = width // (2 * HD)
    rows = qkv.shape[0]
    tiles = rows // TILE

    def kernel(
        q_ref, k_ref, v_ref, ctx_ref, g_ref, lse_ref, sk_ref, sq_ref, out_ref, bias_ref, gk, gv
    ):
        tile = pl.program_id(0)

        @pl.when(tile == 0)
        def _():
            gk[...] = jnp.zeros_like(gk)
            gv[...] = jnp.zeros_like(gv)
            bias_ref[...] = jnp.zeros_like(bias_ref)

        same = sk_ref[:, 3:4] == sq_ref[...]
        place = pl.multiple_of(tile * TILE, TILE)
        for pair in range(pairs):
            lanes = slice(pair * 2 * HD, (pair + 1) * 2 * HD)
            q = q_ref[:, lanes] * jnp.asarray(HD**-0.5, low)
            k = k_ref[:, lanes]
            v = v_ref[:, lanes]
            k_t = k.T
            grad = g_ref[:, lanes]
            dots = (grad.astype(wide) * ctx_ref[:, lanes].astype(wide)).T
            parts = []
            for head in range(2):
                mask = head_mask(head)
                row = pair * 2 + head
                q_head = q * mask
                grad_head = grad * mask
                features = slice(head * HD, (head + 1) * HD)
                delta = jnp.sum(dots[features], axis=0, keepdims=True)
                s = jnp.where(same, mul(k, q_head, NT), -1e30)
                p = jnp.exp(s - lse_ref[row : row + 1, :])
                gs = (p * (mul(v, grad_head, NT) - delta)).astype(low)
                gv[:, lanes] += mul(p.astype(low), grad_head)
                gk[:, lanes] += mul(gs, q_head)
                parts.append(mul(k_t[features], gs))
            gq = (jnp.concatenate(parts, axis=0).T * HD**-0.5).astype(low)
            out_ref[pl.ds(place, TILE), lanes] = gq
            bias_ref[0:1, lanes] += jnp.sum(gq.astype(wide), axis=0, keepdims=True)

        @pl.when(tile == tiles - 1)
        def _():
            out_ref[:, width : 2 * width] = gk[...].astype(low)
            gv_low = gv[...].astype(low)
            out_ref[:, 2 * width :] = gv_low
            bias_ref[1:2, :] = jnp.sum(gv_low.astype(wide), axis=0, keepdims=True)

    return pl.pallas_call(
        kernel,
        grid=(tiles,),
        in_specs=[
            pl.BlockSpec((TILE, width), lambda t: (t, 0)),
            pl.BlockSpec((rows, width), lambda t: (0, 1)),
            pl.BlockSpec((rows, width), lambda t: (0, 2)),
            pl.BlockSpec((TILE, width), lambda t: (t, 0)),
            pl.BlockSpec((TILE, width), lambda t: (t, 0)),
            pl.BlockSpec((2 * pairs, TILE), lambda t: (0, t)),
            pl.BlockSpec((rows, 8), lambda t: (0, 0)),
            pl.BlockSpec((1, TILE), lambda t: (0, t)),
        ],
        out_specs=[
            pl.BlockSpec((rows, 3 * width), lambda t: (0, 0)),
            pl.BlockSpec((2, width), lambda t: (0, 0)),
        ],
        out_shape=[
            jax.ShapeDtypeStruct((rows, 3 * width), low),
            jax.ShapeDtypeStruct((2, width), wide),
        ],
        scratch_shapes=[pltpu.VMEM((rows, width), wide)] * 2,
        compiler_params=pltpu.CompilerParams(vmem_limit_bytes=vmem_bytes),
        cost_estimate=pl.CostEstimate(
            flops=10 * rows * rows * 256 * 4,
            bytes_accessed=6 * 2**20,
            transcendentals=4 * rows * rows,
        ),
        name="attention_backward",
    )(qkv, qkv, qkv, ctx, ctx_grad, lse, seg_column, seg_row)


def body(
    layer_input,
    output_cot,
    score_cot,
    query_lengths,
    passage_lengths,
    pairing,
    match_offset,
    block_order,
    block_master,
    block_first,
    block_second,
    basis_left,
    basis_right,
    bias_state,
    norm_state,
):
    mp_count = lax.axis_size("mp")
    dp_count = lax.axis_size("dp")
    dp_index = lax.axis_index("dp")
    mp_index = lax.axis_index("mp")
    core, chip = mp_index % 2, mp_index // 2
    half_dp = dp_count // 2
    is_query = dp_index < half_dp
    table_row = dp_index % half_dp
    side = block_master.shape[1]
    owned = block_master.shape[0]
    local_width = H // mp_count * HD
    hidden_local = FF // mp_count
    shapes_list = [(D, 3 * local_width), (local_width, D), (D, hidden_local), (hidden_local, D)]
    half, quarter, eighth = ROW // 2, ROW // 4, ROW // 8

    core_pairs = [(s, s ^ 1) for s in range(mp_count)]
    chip_pairs = [(s, s ^ 2) for s in range(mp_count)]

    def core_swap(value):
        return lax.ppermute(value, "mp", core_pairs)

    def chip_swap(value):
        return lax.ppermute(value, "mp", chip_pairs)

    ring = ring_order(dp_count)
    ring_place = [0] * dp_count
    for place, member in enumerate(ring):
        ring_place[member] = place
    ring_table = jnp.asarray(ring, jnp.int32)
    my_place = jnp.asarray(ring_place, jnp.int32)[dp_index]
    ahead = [(ring[k], ring[(k + 1) % dp_count]) for k in range(dp_count)]
    routes = [ahead, [(b, a) for a, b in ahead]]
    bounds = piece_bounds(owned)
    piece_count = len(bounds) - 1
    order_list = block_order[0]
    order_grid = order_list.reshape(dp_count, owned)
    steps = jnp.arange(dp_count, dtype=jnp.int32)

    place = jnp.stack([is_query.astype(jnp.int32), table_row, core])
    link, seg_column, seg_row = pair_tables(
        place, query_lengths, passage_lengths, pairing, score_cot, match_offset
    )

    master_low = block_master.astype(low)
    arrived = [[master_low[bounds[k] : bounds[k + 1]]] for k in range(piece_count)]
    for step in range(dp_count - 1):
        for k in range(piece_count):
            arrived[k].append(lax.ppermute(arrived[k][-1], "dp", routes[k % 2]))
        if step == 1:
            arrived[0][-1], link, seg_column, seg_row = lax.optimization_barrier(
                (arrived[0][-1], link, seg_column, seg_row)
            )
    id_parts = []
    for k in range(piece_count):
        sign = 1 if k % 2 == 0 else -1
        owners = ring_table[(my_place - sign * steps) % dp_count]
        id_parts.append(order_grid[owners][:, bounds[k] : bounds[k + 1]].reshape(-1))
    w_qkv, w_out, w_up, w_down = assemble(
        [piece for k in range(piece_count) for piece in arrived[k]],
        jnp.concatenate(id_parts),
        shapes_list,
        side,
    )

    bias_now = bias_state[0]
    bias_query = bias_now[:local_width]
    bias_value = bias_now[local_width : 2 * local_width]
    bias_up = bias_now[2 * local_width :]
    qkv_bias = jnp.concatenate([bias_query, jnp.zeros_like(bias_query), bias_value])
    bias_attn, bias_down, gain_one, shift_one, gain_two, shift_two = [
        norm_state[0, k] for k in range(6)
    ]

    def turn(rows):
        first = lax.dynamic_slice_in_dim(rows, core * half, half, 0)
        second = lax.dynamic_slice_in_dim(rows, (1 - core) * half, half, 0)
        return (first, second)

    x_mine, x_other = turn(layer_input)
    x_rows = jnp.concatenate([x_mine, x_other], axis=0)

    qkv = (mul(x_rows, w_qkv) + qkv_bias).astype(low)
    context, lse = attention_forward(qkv, seg_column, seg_row)

    def chip_sum(mine_part, other_part):
        mixed = (mine_part + core_swap(other_part.astype(low)).astype(wide)).astype(low)
        return mixed.astype(wide) + chip_swap(mixed).astype(wide)

    def cut(value, k):
        return value[k * quarter : (k + 1) * quarter]

    attn_part = []
    for k in range(2):
        other_part = mul(cut(context, 2 + k), w_out)
        attn_part.append((mul(cut(context, k), w_out), other_part))
    first_norm, normed_one, inverse_one, first_mine, first_other = [], [], [], [], []
    hid_mine, hid_other, slope_mine, slope_other = [], [], [], []
    for k in range(2):
        attn_total = chip_sum(*attn_part[k])
        norm_k, normed_k, inverse_k = layer_norm(
            cut(x_mine, k).astype(wide) + attn_total + bias_attn, gain_one, shift_one
        )
        first_norm.append(norm_k)
        normed_one.append(normed_k)
        inverse_one.append(inverse_k)
        first_mine.append(norm_k.astype(low))
        first_other.append(core_swap(first_mine[k]))
    ffn_part = []
    for k in range(2):
        hid, slope = gelu_parts(mul(first_other[k], w_up) + bias_up)
        hid_other.append(hid)
        slope_other.append(slope)
        other_part = mul(hid, w_down)
        hid, slope = gelu_parts(mul(first_mine[k], w_up) + bias_up)
        hid_mine.append(hid)
        slope_mine.append(slope)
        ffn_part.append((mul(hid, w_down), other_part))
    normed_two, inverse_two, out_mine, out_other, partner = [], [], [], [], []
    exchange = [(s, s ^ half_dp) for s in range(dp_count)]
    for k in range(2):
        ffn_total = chip_sum(*ffn_part[k])
        final_k, normed_k, inverse_k = layer_norm(
            first_norm[k] + ffn_total + bias_down, gain_two, shift_two
        )
        normed_two.append(normed_k)
        inverse_two.append(inverse_k)
        out_k = final_k.astype(low)
        out_mine.append(out_k)
        out_other.append(core_swap(out_k))
        mine = lax.ppermute(
            lax.dynamic_slice_in_dim(out_k, chip * eighth, eighth, 0), "dp", exchange
        )
        theirs = chip_swap(mine)
        partner.append(
            jnp.where(
                chip == 0,
                jnp.concatenate([mine, theirs], axis=0),
                jnp.concatenate([theirs, mine], axis=0),
            )
        )

    def in_order(mine, other):
        mine = jnp.concatenate(mine, axis=0)
        other = jnp.concatenate(other, axis=0)
        return jnp.where(
            core == 0,
            jnp.concatenate([mine, other], axis=0),
            jnp.concatenate([other, mine], axis=0),
        )

    output_part = in_order(out_mine, out_other)
    partner = partner + [core_swap(value) for value in partner]
    linked = mul(link, jnp.concatenate(partner, axis=0))
    extra_grad = jnp.where(is_query, seg_column[:half, 1:2], 1.0) * linked
    token_score = jnp.sum(jnp.concatenate(out_mine, axis=0).astype(wide) * linked, axis=1)
    counted = is_query.astype(wide) * D ** (-0.5)
    seg_hot = (
        seg_column[:half, 2:3] == jnp.arange(score_cot.shape[1], dtype=jnp.int32).astype(wide)
    ).astype(wide)
    score_part = jnp.sum(seg_hot * (token_score * counted)[:, None], axis=0)
    row_hot = (jnp.arange(score_cot.shape[0], dtype=jnp.int32) == table_row).astype(wide)
    score_table = row_hot[:, None] * score_part[None, :]

    cot_mine_rows = lax.dynamic_slice_in_dim(output_cot, core * half, half, 0).astype(wide)
    second_grad, second_mine, second_other = [], [], []
    sums_two = []
    for k in range(2):
        output_grad = cut(cot_mine_rows, k) + cut(extra_grad, k)
        grad_k = norm_back(output_grad, gain_two, normed_two[k], inverse_two[k])
        second_grad.append(grad_k)
        second_mine.append(grad_k.astype(low))
        second_other.append(core_swap(second_mine[k]))
        sums_two.append(
            (
                jnp.sum(grad_k, axis=0),
                jnp.sum(output_grad * normed_two[k], axis=0),
                jnp.sum(output_grad, axis=0),
            )
        )
    pre_mine, pre_other, branch_part = [], [], []
    for k in range(2):
        pre_mine.append((mul(second_mine[k], w_down, NT) * slope_mine[k]).astype(low))
        pre_other.append((mul(second_other[k], w_down, NT) * slope_other[k]).astype(low))
        other_part = mul(pre_other[k], w_up, NT)
        branch_part.append((mul(pre_mine[k], w_up, NT), other_part))
    hidden = jnp.concatenate(hid_mine + hid_other, axis=0)
    second_rows = jnp.concatenate(second_mine + second_other, axis=0)
    first_rows = jnp.concatenate(first_mine + first_other, axis=0)
    pre_rows = jnp.concatenate(pre_mine + pre_other, axis=0)
    grad_down = mul(hidden, second_rows, TN).astype(low)
    grad_up = mul(first_rows, pre_rows, TN).astype(low)
    grad_bias_up = jnp.sum(pre_rows.astype(wide), axis=0)

    first_grad, attn_mine, attn_other, sums_one = [], [], [], []
    for k in range(2):
        first_total = second_grad[k] + chip_sum(*branch_part[k])
        grad_k = norm_back(first_total, gain_one, normed_one[k], inverse_one[k])
        first_grad.append(grad_k)
        attn_mine.append(grad_k.astype(low))
        attn_other.append(core_swap(attn_mine[k]))
        sums_one.append(
            (
                jnp.sum(grad_k, axis=0),
                jnp.sum(first_total * normed_one[k], axis=0),
                jnp.sum(first_total, axis=0),
            )
        )
    attn_rows = jnp.concatenate(attn_mine + attn_other, axis=0)
    context_grad = mul(attn_rows, w_out, NT).astype(low)
    grad_out = mul(context, attn_rows, TN).astype(low)
    qkv_grad, bias_pair = attention_backward(
        qkv, context, context_grad, lse, seg_column, seg_row
    )
    grad_qkv = mul(x_rows, qkv_grad, TN).astype(low)
    input_mine, input_other = [], []
    for k in range(2):
        other_part = mul(cut(qkv_grad, 2 + k), w_qkv, NT)
        branch_zero = chip_sum(mul(cut(qkv_grad, k), w_qkv, NT), other_part)
        input_mine.append((first_grad[k] + branch_zero).astype(low))
        input_other.append(core_swap(input_mine[k]))
    input_grad = in_order(input_mine, input_other)

    norm_local = jnp.stack(
        [
            sums_one[0][0] + sums_one[1][0],
            sums_two[0][0] + sums_two[1][0],
            sums_one[0][1] + sums_one[1][1],
            sums_one[0][2] + sums_one[1][2],
            sums_two[0][1] + sums_two[1][1],
            sums_two[0][2] + sums_two[1][2],
        ]
    )
    bias_local = jnp.concatenate([bias_pair[0], bias_pair[1], grad_bias_up])
    shared = jnp.concatenate([score_table.reshape(-1), norm_local.reshape(-1)])
    small = jnp.concatenate([shared + core_swap(shared), bias_local]).reshape(-1, 64)
    stride = 1
    while stride < dp_count:
        small = small + lax.ppermute(small, "dp", [(s, s ^ stride) for s in range(dp_count)])
        stride *= 2
    small = small.reshape(-1)
    scores = small[: score_table.size].reshape(score_table.shape)
    norm_grad = small[score_table.size : shared.size].reshape(norm_local.shape)
    bias_grad = small[shared.size :]

    id_parts, sizes = [], []
    for k in range(piece_count):
        sign = 1 if k % 2 == 0 else -1
        owners = ring_table[(my_place - sign * (1 + steps)) % dp_count]
        id_parts.append(order_grid[owners][:, bounds[k] : bounds[k + 1]].reshape(-1))
        sizes += [bounds[k + 1] - bounds[k]] * dp_count
    staged = spread(
        [grad_qkv, grad_out, grad_up, grad_down], jnp.concatenate(id_parts), sizes, side
    )
    travelling = [staged[k * dp_count] for k in range(piece_count)]
    for step in range(dp_count - 1):
        for k in range(piece_count):
            came = lax.ppermute(travelling[k], "dp", routes[k % 2])
            summed = came.astype(wide) + staged[k * dp_count + step + 1].astype(wide)
            travelling[k] = summed.astype(low) if step < dp_count - 2 else summed
    owned_grad = jnp.concatenate(travelling, axis=0)

    rotated_old = rotate_first(block_first, basis_left, basis_right)
    first_new, second_new, master_new = optimize(
        owned_grad, rotated_old, block_master, block_first, block_second, basis_left, basis_right
    )
    bias_first, bias_second, bias_value_new = adam_plain(
        bias_grad, bias_state[1], bias_state[2], bias_state[0], small_rate
    )
    norm_first, norm_second, norm_value_new = adam_plain(
        norm_grad, norm_state[1], norm_state[2], norm_state[0], small_rate
    )
    bias_out = jnp.stack([bias_grad, bias_first, bias_second])
    norm_out = jnp.stack([norm_grad, norm_first, norm_second])
    piece_length = norm_value_new.shape[0] * norm_value_new.shape[1] // mp_count
    norm_piece = lax.dynamic_slice_in_dim(
        norm_value_new.reshape(-1), mp_index * piece_length, piece_length, 0
    )
    small_values = jnp.concatenate([bias_value_new, norm_piece])
    return (
        output_part,
        scores,
        input_grad,
        owned_grad,
        first_new,
        second_new,
        master_new,
        bias_out,
        norm_out,
        small_values,
    )


def solution(mesh):
    blocks = P(("dp", "mp"), None, None)
    rows = P("dp", None)
    return jax.shard_map(
        body,
        mesh=mesh,
        in_specs=(rows, rows, P(), P(), P(), P(), P(), P("mp", None))
        + (blocks,) * 5
        + (P(None, "mp"), P()),
        out_specs=(rows, P(), rows) + (blocks,) * 4 + (P(None, "mp"), P(), P("mp")),
        check_vma=False,
    )
```

```python
import math

import jax
import jax.numpy as jnp
from jax import lax
from jax.experimental import pallas as pl
from jax.experimental.pallas import tpu as pltpu
from jax.sharding import PartitionSpec as P

D = 1024
H = 16
HD = 64
FF = 4096
ROW = 1024
STEP = 10
TILE = 256

low = jnp.bfloat16
wide = jnp.float32
beta_one = 0.9
beta_two = 0.999
adam_eps = 1e-08
norm_eps = 1e-05
block_rate = 0.05
small_rate = 0.1
mib = 2**20

NN = (((1,), (0,)), ((), ()))
NT = (((1,), (1,)), ((), ()))
TN = (((0,), (0,)), ((), ()))


def mul(left, right, dims=NN):
    return lax.dot_general(left, right, dims, preferred_element_type=wide)


def gelu_parts(values):
    normal_cdf = 0.5 * (1.0 + lax.erf(values * 0.7071067811865476))
    slope = normal_cdf + values * jnp.exp(-0.5 * values * values) * 0.3989422804014327
    return ((values * normal_cdf).astype(low), slope)


def adam_plain(grad_now, first_old, second_old, value_old, rate_now):
    first_new = beta_one * first_old + (1.0 - beta_one) * grad_now
    second_new = beta_two * second_old + (1.0 - beta_two) * grad_now * grad_now
    step_dir = (
        first_new
        / (1.0 - beta_one**STEP)
        / (jnp.sqrt(second_new / (1.0 - beta_two**STEP)) + adam_eps)
    )
    return (first_new, second_new, value_old - rate_now * step_dir)


def ring_order(count):
    return [k for k in range(count) if k % 2 == 0] + [k for k in range(count) if k % 2][::-1]


def piece_bounds(owned):
    pieces = 4 if owned >= 8 else min(2, owned)
    return [owned * k // pieces for k in range(pieces + 1)]


def vmem_call(kernel, name, outs, *args, smem=0, scratch=(), flops=0, room=4):
    vmem = pl.BlockSpec(memory_space=pltpu.VMEM)
    specs = [pl.BlockSpec(memory_space=pltpu.SMEM)] * smem + [vmem] * (len(args) - smem)
    taken = sum(v.size * v.dtype.itemsize for v in args)
    given = sum(v.size * jnp.dtype(v.dtype).itemsize for v in outs)
    held = sum(
        math.prod(v.shape) * jnp.dtype(v.dtype).itemsize for v in scratch if hasattr(v, "shape")
    )
    moved = taken + given
    return pl.pallas_call(
        kernel,
        in_specs=specs,
        out_specs=[vmem] * len(outs),
        out_shape=outs,
        scratch_shapes=list(scratch),
        compiler_params=pltpu.CompilerParams(vmem_limit_bytes=given + held + room * mib),
        cost_estimate=pl.CostEstimate(flops=flops, bytes_accessed=moved, transcendentals=0),
        name=name,
    )(*args)


def shaped(dtype, *shape):
    return jax.ShapeDtypeStruct(shape, dtype)


def matrix_views(refs, side):
    for ref in refs:
        for row in range(0, ref.shape[0], side):
            for column in range(0, ref.shape[1], side):
                yield ref.at[row : row + side, column : column + side]


def ring_member(place, count):
    place = lax.rem(place + 2 * count, count)
    return jnp.where(place < count // 2, 2 * place, 2 * count - 1 - 2 * place)


def each_travelling(place_ref, count, owned, bounds, first, visit):
    for k in range(len(bounds) - 1):
        sign = 1 if k % 2 == 0 else -1
        for step in range(count):
            owner = ring_member(place_ref[5] - sign * (first + step), count)
            start = owner * owned + bounds[k]
            for w in range(bounds[k + 1] - bounds[k]):
                visit(k * count + step, w, start + w)


def assemble(place, order, pieces, shapes_list, side, count, owned, bounds):
    def kernel(place_ref, order_ref, *refs):
        parts, outs, blocks = refs[: len(pieces)], refs[len(pieces) : -1], refs[-1]

        def visit(at, w, slot):
            blocks[order_ref[slot]] = parts[at][w]

        each_travelling(place_ref, count, owned, bounds, 0, visit)
        for k, view in enumerate(matrix_views(outs, side)):
            view[...] = blocks[k]

    return vmem_call(
        kernel,
        "assemble",
        [shaped(low, *shape) for shape in shapes_list],
        place,
        order,
        *pieces,
        smem=2,
        scratch=[pltpu.VMEM((count * owned, side, side), low)],
    )


def spread(place, order, matrices, side, count, owned, bounds):
    def kernel(place_ref, order_ref, *refs):
        sources, outs, blocks = refs[: len(matrices)], refs[len(matrices) : -1], refs[-1]
        for k, view in enumerate(matrix_views(sources, side)):
            blocks[k] = view[...]

        def visit(at, w, slot):
            outs[at][w] = blocks[order_ref[slot]]

        each_travelling(place_ref, count, owned, bounds, 1, visit)

    return vmem_call(
        kernel,
        "spread",
        [
            shaped(low, bounds[k + 1] - bounds[k], side, side)
            for k in range(len(bounds) - 1)
            for _ in range(count)
        ],
        place,
        order,
        *matrices,
        smem=2,
        scratch=[pltpu.VMEM((count * owned, side, side), low)],
    )


def in_order(place, mine, other):
    rows = mine[0].shape[0]
    count = len(mine)

    def kernel(place_ref, *refs):
        out = refs[-1]
        core = place_ref[2]
        for k in range(count):
            for ref, turn in ((refs[k], core), (refs[count + k], 1 - core)):
                start = pl.multiple_of((turn * count + k) * rows, rows)
                out[pl.ds(start, rows), :] = ref[...]

    return vmem_call(
        kernel, "in_order", [shaped(low, 2 * count * rows, D)], place, *mine, *other, smem=1
    )[0]


def feed_grads(hidden, second_rows, first_rows, pre_rows):
    count, rows = len(hidden), hidden[0].shape[0]
    inner = hidden[0].shape[1]

    def kernel(*refs):
        down_ref, up_ref, bias_ref, left, right = refs[4 * count :]

        def fill(target, sources):
            for k, ref in enumerate(sources):
                target[k * rows : (k + 1) * rows, :] = ref[...]

        fill(left, refs[:count])
        fill(right, refs[count : 2 * count])
        down_ref[...] = mul(left[...], right[...], TN).astype(low)
        fill(left, refs[2 * count : 3 * count])
        fill(right, refs[3 * count : 4 * count])
        up_ref[...] = mul(left[...], right[...], TN).astype(low)
        bias_ref[...] = jnp.sum(right[...].astype(wide), axis=0, keepdims=True)

    return vmem_call(
        kernel,
        "feed_grads",
        [shaped(low, inner, D), shaped(low, D, inner), shaped(wide, 1, inner)],
        *hidden,
        *second_rows,
        *first_rows,
        *pre_rows,
        scratch=[pltpu.VMEM((count * rows, D), low), pltpu.VMEM((count * rows, D), low)],
        flops=4 * count * rows * D * inner,
        room=12,
    )


def pair_tables(place, query_lengths, passage_lengths, pairing, score_cot, match_offset):
    queries, passages = query_lengths.shape[1], passage_lengths.shape[1]
    half = ROW // 2
    pair_scale = D ** (-0.5)

    def kernel(place_ref, ql_ref, pl_ref, pair_ref, cot_ref, offset_ref, link_ref, col_ref, row_ref):
        is_query = place_ref[0] == 1
        row = place_ref[1]
        first_core = place_ref[2] == 0
        token = lax.broadcasted_iota(jnp.int32, (1, ROW), 1)
        zero = jnp.zeros((1, ROW), jnp.int32)
        segment, start_at, length_at = zero, zero, zero
        cot = jnp.zeros((1, ROW), wide)
        start = jnp.int32(0)
        for e in range(queries):
            end = start + ql_ref[row, e]
            inside = (token >= start) & (token < end)
            chosen = pair_ref[row, e]
            before = jnp.int32(0)
            length = jnp.int32(1)
            for m in range(passages):
                span = pl_ref[row, m]
                before = before + jnp.where(m < chosen, span, 0)
                length = jnp.where(m == chosen, span, length)
            segment = jnp.where(inside, e, segment)
            start_at = jnp.where(inside, before, start_at)
            length_at = jnp.where(inside, length, length_at)
            cot = jnp.where(inside, cot_ref[row, e] * pair_scale, cot)
            start = end
        passage = zero
        start = jnp.int32(0)
        for m in range(passages):
            start = start + pl_ref[row, m]
            passage = passage + (token >= start).astype(jnp.int32)
        length_at = jnp.maximum(length_at, 1)
        target = start_at + lax.rem(offset_ref[pl.ds(row, 1), :], length_at)
        own = jnp.where(is_query, segment, passage)

        def turn(value):
            swapped = jnp.concatenate([value[:, half:], value[:, :half]], axis=1)
            return jnp.where(first_core, value, swapped)

        token = turn(token)
        target, cot, segment, own = turn(target), turn(cot), turn(segment), turn(own)
        stacked = jnp.concatenate(
            [target.astype(wide), cot, segment.astype(wide), own.astype(wide)]
            + [token.astype(wide)]
            + [jnp.zeros((3, ROW), wide)],
            axis=0,
        )
        columns = stacked.T
        col_ref[...] = columns
        row_ref[...] = own.astype(wide)
        left = jnp.where(is_query, columns[:half, 0:1], columns[:half, 4:5])
        right = jnp.where(is_query, token, target).astype(wide)
        value = jnp.where(is_query, jnp.ones_like(cot), cot)
        link_ref[...] = jnp.where(left == right, value, 0.0).astype(low)

    smem = pl.BlockSpec(memory_space=pltpu.SMEM)
    vmem = pl.BlockSpec(memory_space=pltpu.VMEM)
    return pl.pallas_call(
        kernel,
        in_specs=[smem] * 5 + [vmem],
        out_specs=[vmem] * 3,
        out_shape=[
            jax.ShapeDtypeStruct((half, ROW), low),
            jax.ShapeDtypeStruct((ROW, 8), wide),
            jax.ShapeDtypeStruct((1, ROW), wide),
        ],
        compiler_params=pltpu.CompilerParams(vmem_limit_bytes=16 * mib),
        name="pair_tables",
    )(place, query_lengths, passage_lengths, pairing, score_cot, match_offset)


def halves(value):
    top = value.astype(low)
    return (top, (value - top.astype(wide)).astype(low))


def left_parts(value):
    top, rest = halves(value)
    return jnp.concatenate([top, rest, top], axis=1)


def right_parts(value, axis=0):
    top, rest = halves(value)
    return jnp.concatenate([top, top, rest], axis=axis)


def rotate_first(blocks, left_basis, right_basis):
    count, side = blocks.shape[0], blocks.shape[1]
    group = 6 if count % 6 == 0 else 3 if count % 3 == 0 else 1

    def kernel(m_ref, l_ref, r_ref, out_ref):
        for b in range(group):
            inner = mul(left_parts(l_ref[b].T), right_parts(m_ref[b]))
            out_ref[b] = mul(left_parts(inner), right_parts(r_ref[b]))

    spec = pl.BlockSpec((group, side, side), lambda t: (t, 0, 0))
    return pl.pallas_call(
        kernel,
        grid=(count // group,),
        in_specs=[spec] * 3,
        out_specs=spec,
        out_shape=jax.ShapeDtypeStruct(blocks.shape, wide),
        compiler_params=pltpu.CompilerParams(vmem_limit_bytes=16 * mib),
        cost_estimate=pl.CostEstimate(
            flops=count * 12 * side**3, bytes_accessed=16 * count * side**2, transcendentals=0
        ),
        name="rotate_first",
    )(blocks, left_basis, right_basis)


def optimize(grad, rotated_old, master, first, second, left_basis, right_basis):
    count, side = grad.shape[0], grad.shape[1]
    group = 6 if count % 6 == 0 else 3 if count % 3 == 0 else 1

    def kernel(g_ref, c_ref, w_ref, m_ref, v_ref, l_ref, r_ref, m_out, v_out, w_out):
        for b in range(group):
            grad_now = g_ref[b]
            m_out[b] = beta_one * m_ref[b] + (1.0 - beta_one) * grad_now
            left, right = l_ref[b], r_ref[b]
            inner = mul(left_parts(left.T), right_parts(grad_now))
            turned = mul(left_parts(inner), right_parts(right))
            second_new = beta_two * v_ref[b] + (1.0 - beta_two) * turned * turned
            v_out[b] = second_new
            first_turned = beta_one * c_ref[b] + (1.0 - beta_one) * turned
            step = (first_turned / (1.0 - beta_one**STEP)) / (
                jnp.sqrt(second_new / (1.0 - beta_two**STEP)) + adam_eps
            )
            inner = mul(left_parts(left), right_parts(step))
            w_out[b] = w_ref[b] - block_rate * mul(left_parts(inner), right_parts(right, 1), NT)

    spec = pl.BlockSpec((group, side, side), lambda t: (t, 0, 0))
    return pl.pallas_call(
        kernel,
        grid=(count // group,),
        in_specs=[spec] * 7,
        out_specs=[spec] * 3,
        out_shape=[jax.ShapeDtypeStruct(grad.shape, wide)] * 3,
        compiler_params=pltpu.CompilerParams(vmem_limit_bytes=16 * mib),
        cost_estimate=pl.CostEstimate(
            flops=count * 24 * side**3, bytes_accessed=40 * count * side**2, transcendentals=0
        ),
        name="optimize",
    )(grad, rotated_old, master, first, second, left_basis, right_basis)


def head_mask(head):
    lane = lax.broadcasted_iota(jnp.int32, (1, 2 * HD), 1)
    return ((lane // HD) == head).astype(low)


def attention_tile(qkv, w_out, table, seg_row, tile, came=None):
    width = qkv.shape[1] // 3
    pairs = width // (2 * HD)
    rows = qkv.shape[0]
    span = slice(tile * TILE, (tile + 1) * TILE)

    def kernel(qkv_ref, w_ref, sk_ref, sq_ref, *refs):
        ctx_ref, lse_ref, part_ref = refs[-3:]
        same = sk_ref[:, 3:4] == sq_ref[:, span]
        for pair in range(pairs):
            place = pair * 2 * HD
            lanes = slice(place, place + 2 * HD)
            q = qkv_ref[span, lanes] * jnp.asarray(HD**-0.5, low)
            k = qkv_ref[:, width + place : width + place + 2 * HD]
            v_t = qkv_ref[:, 2 * width + place : 2 * width + place + 2 * HD].T
            parts = []
            for head in range(2):
                s = jnp.where(same, mul(k, q * head_mask(head), NT), -1e30)
                peak = jnp.max(s, axis=0, keepdims=True)
                e = jnp.exp(s - peak)
                total = jnp.sum(e, axis=0, keepdims=True)
                part = mul(v_t[head * HD : (head + 1) * HD], e.astype(low))
                parts.append(part * (1.0 / total))
                lse_ref[pair * 2 + head : pair * 2 + head + 1, :] = peak + jnp.log(total)
            ctx_ref[:, lanes] = jnp.concatenate(parts, axis=0).T.astype(low)
        part = mul(ctx_ref[...], w_ref[...])
        if came is not None:
            part = part + refs[0][...].astype(wide)
        part_ref[...] = part.astype(low)

    operands = [qkv, w_out, table, seg_row] + ([] if came is None else [came])
    return vmem_call(
        kernel,
        "attention_tile",
        [shaped(low, TILE, width), shaped(wide, 2 * pairs, TILE), shaped(low, TILE, D)],
        *operands,
        flops=16 * TILE * rows * width,
        room=8,
    )


def norm_rows(place, mixed, came, residual, vectors, which, keep):
    bias_row, gain_row, shift_row = which
    rows = mixed.shape[0]

    def kernel(place_ref, a_ref, b_ref, x_ref, v_ref, low_ref, normed_ref, inverse_ref, last_ref):
        total = a_ref[...].astype(wide) + b_ref[...].astype(wide)
        z = x_ref[...].astype(wide) + total + v_ref[bias_row : bias_row + 1, :]
        center = z - jnp.mean(z, axis=1, keepdims=True)
        inverse = lax.rsqrt(jnp.mean(center * center, axis=1, keepdims=True) + norm_eps)
        normed = center * inverse
        out = v_ref[gain_row : gain_row + 1, :] * normed + v_ref[shift_row : shift_row + 1, :]
        low_ref[...] = out.astype(low)
        normed_ref[...] = normed
        inverse_ref[...] = inverse
        if keep:
            last_ref[...] = out
        else:
            first_chip = place_ref[3] == 0
            last_ref[...] = jnp.where(first_chip, out[: rows // 2], out[rows // 2 :]).astype(low)

    outs = [shaped(low, rows, D), shaped(wide, rows, D), shaped(wide, rows, 1)]
    outs += [shaped(wide, rows, D) if keep else shaped(low, rows // 2, D)]
    return vmem_call(
        kernel,
        "norm_rows",
        outs,
        place,
        mixed,
        came,
        residual,
        vectors,
        smem=1,
        flops=20 * rows * D,
    )


def norm_back(grad_rows, norm_gain, normed, inverse):
    scaled = grad_rows * norm_gain
    first_mean = jnp.mean(scaled, axis=1, keepdims=True)
    second_mean = jnp.mean(scaled * normed, axis=1, keepdims=True)
    return inverse * (scaled - first_mean - normed * second_mean)


def column_sums(grad_z, grad_rows, normed):
    return jnp.concatenate(
        [
            jnp.sum(grad_z, axis=0, keepdims=True),
            jnp.sum(grad_rows * normed, axis=0, keepdims=True),
            jnp.sum(grad_rows, axis=0, keepdims=True),
        ],
        axis=0,
    )


def feed_forward(rows_low, w_up, bias_up, w_down):
    rows, hidden = rows_low.shape[0], w_up.shape[1]

    def kernel(h_ref, up_ref, b_ref, down_ref, part_ref, hid_ref, slope_ref):
        u = mul(h_ref[...], up_ref[...]) + b_ref[...]
        hid, slope = gelu_parts(u)
        hid_ref[...] = hid
        slope_ref[...] = slope
        part_ref[...] = mul(hid, down_ref[...]).astype(part_ref.dtype)

    return vmem_call(
        kernel,
        "feed_forward",
        [shaped(low, rows, D), shaped(low, rows, hidden), shaped(wide, rows, hidden)],
        rows_low,
        w_up,
        bias_up,
        w_down,
        flops=4 * rows * D * hidden,
    )


def feed_back(grad_low, slope, w_up, w_down):
    rows, hidden = grad_low.shape[0], w_up.shape[1]

    def kernel(g_ref, slope_ref, up_ref, down_ref, part_ref, pre_ref):
        pre = (mul(g_ref[...], down_ref[...], NT) * slope_ref[...]).astype(low)
        pre_ref[...] = pre
        part_ref[...] = mul(pre, up_ref[...], NT).astype(part_ref.dtype)

    return vmem_call(
        kernel,
        "feed_back",
        [shaped(low, rows, D), shaped(low, rows, hidden)],
        grad_low,
        slope,
        w_up,
        w_down,
        flops=4 * rows * D * hidden,
    )


def link_back(place, link, table, cot_rows, out_rows, normed, inverse, vectors, pieces, queries):
    rows = out_rows[0].shape[0]
    count = len(out_rows)
    piece_rows = pieces[0].shape[0]

    def kernel(place_ref, link_ref, table_ref, cot_ref, *refs):
        outs, refs = refs[:count], refs[count:]
        norms, refs = refs[:count], refs[count:]
        scales, refs = refs[:count], refs[count:]
        v_ref, refs = refs[0], refs[1:]
        parts, refs = refs[: len(pieces)], refs[len(pieces) :]
        grads, refs = refs[:count], refs[count:]
        lows, refs = refs[:count], refs[count:]
        sums_ref, score_ref, partner = refs
        is_query = place_ref[0] == 1
        chip = place_ref[3]
        for k, part in enumerate(parts):
            turn = chip if k % 2 == 0 else 1 - chip
            start = (k // 2 * 2 + turn) * piece_rows
            partner[pl.ds(pl.multiple_of(start, piece_rows), piece_rows), :] = part[...]
        gain = v_ref[4:5, :]
        sums = jnp.zeros((3, D), wide)
        score = jnp.zeros((1, queries), wide)
        for k in range(count):
            span = slice(k * rows, (k + 1) * rows)
            linked = mul(link_ref[span, :], partner[...])
            token = jnp.sum(outs[k][...].astype(wide) * linked, axis=1, keepdims=True)
            kinds = lax.broadcasted_iota(jnp.int32, (1, queries), 1).astype(wide)
            hot = table_ref[span, 2:3] == kinds
            score = score + jnp.sum(jnp.where(hot, token, 0.0), axis=0, keepdims=True)
            scale = jnp.where(is_query, table_ref[span, 1:2], 1.0)
            start = pl.multiple_of(place_ref[2] * count * rows + k * rows, rows)
            grad_rows = cot_ref[pl.ds(start, rows), :].astype(wide) + scale * linked
            normed_k = norms[k][...]
            grad_z = norm_back(grad_rows, gain, normed_k, scales[k][...])
            grads[k][...] = grad_z
            lows[k][...] = grad_z.astype(low)
            sums = sums + column_sums(grad_z, grad_rows, normed_k)
        sums_ref[...] = sums
        score_ref[...] = jnp.where(is_query, score * D ** (-0.5), 0.0)

    return vmem_call(
        kernel,
        "link_back",
        [shaped(wide, rows, D)] * count
        + [shaped(low, rows, D)] * count
        + [shaped(wide, 3, D), shaped(wide, 1, queries)],
        place,
        link,
        table,
        cot_rows,
        *out_rows,
        *normed,
        *inverse,
        vectors,
        *pieces,
        smem=1,
        scratch=[pltpu.VMEM((ROW, D), low)],
        flops=2 * count * rows * ROW * D,
    )


def first_back(mixed, came, second_grad, normed, inverse, vectors):
    rows = mixed.shape[0]

    def kernel(a_ref, b_ref, g_ref, n_ref, i_ref, v_ref, grad_ref, low_ref, sums_ref):
        total = a_ref[...].astype(wide) + b_ref[...].astype(wide)
        grad_rows = g_ref[...] + total
        normed_k = n_ref[...]
        grad_z = norm_back(grad_rows, v_ref[2:3, :], normed_k, i_ref[...])
        grad_ref[...] = grad_z
        low_ref[...] = grad_z.astype(low)
        sums_ref[...] = column_sums(grad_z, grad_rows, normed_k)

    return vmem_call(
        kernel,
        "first_back",
        [shaped(wide, rows, D), shaped(low, rows, D), shaped(wide, 3, D)],
        mixed,
        came,
        second_grad,
        normed,
        inverse,
        vectors,
        flops=20 * rows * D,
    )


def attention_backward(qkv, w_out, table, seg_row, contexts, rows_grads, lses):
    width = qkv.shape[1] // 3
    pairs = width // (2 * HD)
    rows = qkv.shape[0]
    tiles = rows // TILE

    def kernel(qkv_ref, w_ref, sk_ref, sq_ref, *refs):
        ctx_refs, refs = refs[:tiles], refs[tiles:]
        g_refs, refs = refs[:tiles], refs[tiles:]
        lse_refs, refs = refs[:tiles], refs[tiles:]
        out_ref, wgrad_ref, bias_ref, ctx, grad_rows, ctx_grad, lse, gk, gv = refs
        for t in range(tiles):
            span = slice(t * TILE, (t + 1) * TILE)
            ctx[span, :] = ctx_refs[t][...]
            grad_rows[span, :] = g_refs[t][...]
            lse[:, span] = lse_refs[t][...]
        ctx_grad[...] = mul(grad_rows[...], w_ref[...], NT).astype(low)
        wgrad_ref[...] = mul(ctx[...], grad_rows[...], TN).astype(low)
        gk[...] = jnp.zeros_like(gk)
        gv[...] = jnp.zeros_like(gv)
        bias_ref[...] = jnp.zeros_like(bias_ref)

        def step(tile, carry):
            span = pl.ds(pl.multiple_of(tile * TILE, TILE), TILE)
            same = sk_ref[:, 3:4] == sq_ref[:, span]
            for pair in range(pairs):
                place = pair * 2 * HD
                lanes = slice(place, place + 2 * HD)
                q = qkv_ref[span, lanes] * jnp.asarray(HD**-0.5, low)
                k = qkv_ref[:, width + place : width + place + 2 * HD]
                v = qkv_ref[:, 2 * width + place : 2 * width + place + 2 * HD]
                k_t = k.T
                grad = ctx_grad[span, lanes]
                dots = (grad.astype(wide) * ctx[span, lanes].astype(wide)).T
                parts = []
                for head in range(2):
                    mask = head_mask(head)
                    row = pair * 2 + head
                    q_head = q * mask
                    grad_head = grad * mask
                    features = slice(head * HD, (head + 1) * HD)
                    delta = jnp.sum(dots[features], axis=0, keepdims=True)
                    s = jnp.where(same, mul(k, q_head, NT), -1e30)
                    p = jnp.exp(s - lse[row : row + 1, span])
                    gs = (p * (mul(v, grad_head, NT) - delta)).astype(low)
                    gv[:, lanes] += mul(p.astype(low), grad_head)
                    gk[:, lanes] += mul(gs, q_head)
                    parts.append(mul(k_t[features], gs))
                gq = (jnp.concatenate(parts, axis=0).T * HD**-0.5).astype(low)
                out_ref[span, lanes] = gq
                bias_ref[:, lanes] += jnp.sum(gq.astype(wide), axis=0, keepdims=True)
            return carry

        lax.fori_loop(0, tiles, step, 0)
        out_ref[:, width : 2 * width] = gk[...].astype(low)
        gv_low = gv[...].astype(low)
        out_ref[:, 2 * width :] = gv_low
        bias_ref[:, width:] = jnp.sum(gv_low.astype(wide), axis=0, keepdims=True)

    return vmem_call(
        kernel,
        "attention_backward",
        [shaped(low, rows, 3 * width), shaped(low, width, D), shaped(wide, 1, 2 * width)],
        qkv,
        w_out,
        table,
        seg_row,
        *contexts,
        *rows_grads,
        *lses,
        scratch=[
            pltpu.VMEM((rows, width), low),
            pltpu.VMEM((rows, D), low),
            pltpu.VMEM((rows, width), low),
            pltpu.VMEM((2 * pairs, rows), wide),
            pltpu.VMEM((rows, width), wide),
            pltpu.VMEM((rows, width), wide),
        ],
        flops=40 * rows * rows * width,
        room=10,
    )


def pack_sums(place, sums_one, sums_two, score_part):
    queries = score_part.shape[1]

    def kernel(place_ref, one_a, one_b, two_ref, score_ref, out_ref):
        one = one_a[...] + one_b[...]
        two = two_ref[...]
        out_ref[0:1, :] = one[0:1]
        out_ref[1:2, :] = two[0:1]
        out_ref[2:4, :] = one[1:3]
        out_ref[4:6, :] = two[1:3]
        lane = lax.broadcasted_iota(jnp.int32, (1, D), 1)
        first = place_ref[1] * queries
        row = jnp.zeros((1, D), wide)
        score = score_ref[...]
        for e in range(queries):
            row = jnp.where(lane == first + e, score[:, e : e + 1], row)
        out_ref[6:7, :] = row
        out_ref[7:8, :] = jnp.zeros((1, D), wide)

    return vmem_call(
        kernel, "pack_sums", [shaped(wide, 8, D)], place, *sums_one, sums_two, score_part, smem=1
    )[0]


def add_biases(shared, came, pair_bias, up_grad):
    def kernel(a_ref, b_ref, pair_ref, up_ref, out_ref):
        out_ref[0:8, :] = a_ref[...] + b_ref[...]
        zero = jnp.zeros((1, D - pair_ref.shape[1]), wide)
        out_ref[8:9, :] = jnp.concatenate([pair_ref[...], zero], axis=1)
        out_ref[9:10, :] = up_ref[...]
        out_ref[10:16, :] = jnp.zeros((6, D), wide)

    return vmem_call(
        kernel, "add_biases", [shaped(wide, 16, D)], shared, came, pair_bias, up_grad
    )[0]


def small_update(place, total, bias_state, norm_state, local_width, packs, queries):
    bias_count = bias_state.shape[1]
    hidden = bias_count - 2 * local_width
    unit = D // 2
    pieces = norm_state.shape[1] * 2 // 4

    def kernel(place_ref, g_ref, bias_ref, norm_ref, bias_out, norm_out, score_out, value_out, new):
        bias_grad = jnp.concatenate([g_ref[8:9, : 2 * local_width], g_ref[9:10, :hidden]], axis=1)
        first, second, value = adam_plain(
            bias_grad, bias_ref[1:2], bias_ref[2:3], bias_ref[0:1], small_rate
        )
        bias_out[0:1, :] = bias_grad
        bias_out[1:2, :] = first
        bias_out[2:3, :] = second
        for k in range(bias_count // unit):
            value_out[k : k + 1, :] = value[:, k * unit : (k + 1) * unit]
        norm_grad = g_ref[0:6, :]
        first, second, value = adam_plain(
            norm_grad, norm_ref[1], norm_ref[2], norm_ref[0], small_rate
        )
        norm_out[0] = norm_grad
        norm_out[1] = first
        norm_out[2] = second
        for row in range(6):
            for side in range(2):
                new[2 * row + side] = value[row : row + 1, side * unit : (side + 1) * unit]
        start = place_ref[4] * pieces
        for k in range(pieces):
            at = bias_count // unit + k
            value_out[at : at + 1, :] = new[start + k]
        for pack in range(packs):
            score_out[pack : pack + 1, :] = g_ref[6:7, pack * queries : (pack + 1) * queries]

    bias_out, norm_out, scores, values = vmem_call(
        kernel,
        "small_update",
        [
            shaped(wide, 3, bias_count),
            shaped(wide, *norm_state.shape),
            shaped(wide, packs, queries),
            shaped(wide, bias_count // unit + pieces, unit),
        ],
        place,
        total,
        bias_state,
        norm_state,
        smem=1,
        scratch=[pltpu.VMEM((12, 1, unit), wide)],
    )
    return bias_out, norm_out, scores, values


def body(
    layer_input,
    output_cot,
    score_cot,
    query_lengths,
    passage_lengths,
    pairing,
    match_offset,
    block_order,
    block_master,
    block_first,
    block_second,
    basis_left,
    basis_right,
    bias_state,
    norm_state,
):
    mp_count = lax.axis_size("mp")
    dp_count = lax.axis_size("dp")
    dp_index = lax.axis_index("dp")
    mp_index = lax.axis_index("mp")
    core, chip = mp_index % 2, mp_index // 2
    half_dp = dp_count // 2
    is_query = dp_index < half_dp
    table_row = dp_index % half_dp
    side = block_master.shape[1]
    owned = block_master.shape[0]
    local_width = H // mp_count * HD
    hidden_local = FF // mp_count
    shapes_list = [(D, 3 * local_width), (local_width, D), (D, hidden_local), (hidden_local, D)]
    half, quarter = ROW // 2, ROW // 4

    core_pairs = [(s, s ^ 1) for s in range(mp_count)]
    chip_pairs = [(s, s ^ 2) for s in range(mp_count)]

    def core_swap(value):
        return lax.ppermute(value, "mp", core_pairs)

    def chip_swap(value):
        return lax.ppermute(value, "mp", chip_pairs)

    ring = ring_order(dp_count)
    ahead = [(ring[k], ring[(k + 1) % dp_count]) for k in range(dp_count)]
    routes = [ahead, [(b, a) for a, b in ahead]]
    bounds = piece_bounds(owned)
    piece_count = len(bounds) - 1
    order_list = block_order[0]
    ring_place = jnp.where(dp_index % 2 == 0, dp_index // 2, dp_count - 1 - dp_index // 2)
    place = jnp.stack(
        [is_query.astype(jnp.int32), table_row, core, chip, mp_index, ring_place]
    )
    link, seg_column, seg_row = pair_tables(
        place, query_lengths, passage_lengths, pairing, score_cot, match_offset
    )

    bias_now = bias_state[0]
    bias_query = bias_now[:local_width]
    bias_value = bias_now[local_width : 2 * local_width]
    bias_up = bias_now[2 * local_width :]
    qkv_bias = jnp.concatenate([bias_query, jnp.zeros_like(bias_query), bias_value])
    vectors = norm_state[0]

    x_rows = in_order(
        place, [layer_input[:half]], [layer_input[half:]]
    )

    master_low = block_master.astype(low)
    arrived = [[master_low[bounds[k] : bounds[k + 1]]] for k in range(piece_count)]
    for step in range(dp_count - 1):
        for k in range(piece_count):
            arrived[k].append(lax.ppermute(arrived[k][-1], "dp", routes[k % 2]))
        if step == 1:
            held = (arrived[0][-1], link, seg_column, seg_row, x_rows, qkv_bias)
            arrived[0][-1], link, seg_column, seg_row, x_rows, qkv_bias = (
                lax.optimization_barrier(held)
            )
    w_qkv, w_out, w_up, w_down = assemble(
        place,
        order_list,
        [piece for k in range(piece_count) for piece in arrived[k]],
        shapes_list,
        side,
        dp_count,
        owned,
        bounds,
    )

    x_mine = x_rows[:half]
    qkv = (mul(x_rows, w_qkv) + qkv_bias).astype(low)
    tiles = ROW // TILE
    half_tiles = tiles // 2

    def cut(value, k):
        return value[k * quarter : (k + 1) * quarter]

    context, lse, mixed = [None] * tiles, [None] * tiles, [None] * half_tiles
    sent = []
    for k in range(half_tiles):
        t = half_tiles + k
        context[t], lse[t], part = attention_tile(qkv, w_out, seg_column, seg_row, t)
        sent.append(core_swap(part))
    for k in range(half_tiles):
        context[k], lse[k], mixed[k] = attention_tile(
            qkv, w_out, seg_column, seg_row, k, sent[k]
        )
    came = [chip_swap(value) for value in mixed]
    normed_one, inverse_one, first_mine, first_other, first_norm = [], [], [], [], []
    for k in range(2):
        rows_low, normed_k, inverse_k, rows_wide = norm_rows(
            place, mixed[k], came[k], cut(x_mine, k), vectors, (0, 2, 3), True
        )
        first_mine.append(rows_low)
        normed_one.append(normed_k)
        inverse_one.append(inverse_k)
        first_norm.append(rows_wide)
        first_other.append(core_swap(rows_low))

    def mix(mine_part, other_part):
        return (mine_part.astype(wide) + core_swap(other_part).astype(wide)).astype(low)

    hid_mine, hid_other, slope_mine, slope_other, mixed = [], [], [], [], []
    up_row = bias_up[None, :]
    for k in range(2):
        mine_part, hid, slope = feed_forward(first_mine[k], w_up, up_row, w_down)
        hid_mine.append(hid)
        slope_mine.append(slope)
        other_part, hid, slope = feed_forward(first_other[k], w_up, up_row, w_down)
        hid_other.append(hid)
        slope_other.append(slope)
        mixed.append(mix(mine_part, other_part))
    came = [chip_swap(value) for value in mixed]
    normed_two, inverse_two, out_mine, out_other, pieces = [], [], [], [], []
    exchange = [(s, s ^ half_dp) for s in range(dp_count)]
    for k in range(2):
        out_k, normed_k, inverse_k, out_piece = norm_rows(
            place, mixed[k], came[k], first_norm[k], vectors, (1, 4, 5), False
        )
        normed_two.append(normed_k)
        inverse_two.append(inverse_k)
        out_mine.append(out_k)
        out_other.append(core_swap(out_k))
        mine = lax.ppermute(out_piece, "dp", exchange)
        pieces += [mine, chip_swap(mine)]

    output_part = in_order(place, out_mine, out_other)
    pieces = pieces + [core_swap(value) for value in pieces]
    linked = link_back(
        place,
        link,
        seg_column,
        output_cot,
        out_mine,
        normed_two,
        inverse_two,
        vectors,
        pieces,
        score_cot.shape[1],
    )
    second_grad, second_mine = list(linked[:2]), list(linked[2:4])
    sums_two, score_part = linked[4], linked[5]
    second_other = [core_swap(value) for value in second_mine]
    pre_mine, pre_other, mixed = [], [], []
    for k in range(2):
        mine_part, pre = feed_back(second_mine[k], slope_mine[k], w_up, w_down)
        pre_mine.append(pre)
        other_part, pre = feed_back(second_other[k], slope_other[k], w_up, w_down)
        pre_other.append(pre)
        mixed.append(mix(mine_part, other_part))
    came = [chip_swap(value) for value in mixed]
    grad_down, grad_up, up_grad = feed_grads(
        hid_mine + hid_other,
        second_mine + second_other,
        first_mine + first_other,
        pre_mine + pre_other,
    )

    rotated_old = rotate_first(block_first, basis_left, basis_right)
    ready = (vectors, grad_down, grad_up, up_grad, rotated_old, output_part)
    late_vectors, grad_down, grad_up, up_grad, rotated_old, output_part = (
        lax.optimization_barrier(ready)
    )

    first_grad, attn_mine, attn_other, sums_one = [], [], [], []
    for k in range(2):
        grad_k, low_k, sums_k = first_back(
            mixed[k], came[k], second_grad[k], normed_one[k], inverse_one[k], late_vectors
        )
        first_grad.append(grad_k)
        attn_mine.append(low_k)
        attn_other.append(core_swap(low_k))
        sums_one.append(sums_k)
    shared = pack_sums(place, sums_one, sums_two, score_part)
    shared_came = core_swap(shared)
    qkv_grad, grad_out, pair_bias = attention_backward(
        qkv, w_out, seg_column, seg_row, context, attn_mine + attn_other, lse
    )
    grad_qkv = mul(x_rows, qkv_grad, TN).astype(low)
    input_mine, input_other = [], []
    for k in range(2):
        other_part = mul(cut(qkv_grad, 2 + k), w_qkv, NT).astype(low)
        mixed_k = mix(mul(cut(qkv_grad, k), w_qkv, NT), other_part)
        branch_zero = mixed_k.astype(wide) + chip_swap(mixed_k).astype(wide)
        input_mine.append((first_grad[k] + branch_zero).astype(low))
        input_other.append(core_swap(input_mine[k]))
    input_grad = in_order(place, input_mine, input_other)

    small = add_biases(shared, shared_came, pair_bias, up_grad)
    stride = 1
    while stride < dp_count:
        small = small + lax.ppermute(small, "dp", [(s, s ^ stride) for s in range(dp_count)])
        stride *= 2
    bias_out, norm_out, scores, small_values = small_update(
        place, small, bias_state, norm_state, local_width, *score_cot.shape
    )

    staged = spread(
        place,
        order_list,
        [grad_qkv, grad_out, grad_up, grad_down],
        side,
        dp_count,
        owned,
        bounds,
    )
    travelling = [staged[k * dp_count] for k in range(piece_count)]
    for step in range(dp_count - 1):
        for k in range(piece_count):
            came = lax.ppermute(travelling[k], "dp", routes[k % 2])
            summed = came.astype(wide) + staged[k * dp_count + step + 1].astype(wide)
            travelling[k] = summed.astype(low) if step < dp_count - 2 else summed
    owned_grad = jnp.concatenate(travelling, axis=0)

    owned_grad, input_grad = lax.optimization_barrier((owned_grad, input_grad))
    first_new, second_new, master_new = optimize(
        owned_grad, rotated_old, block_master, block_first, block_second, basis_left, basis_right
    )
    small_values, master_new = lax.optimization_barrier((small_values, master_new))
    small_values = small_values.reshape(-1)
    return (
        output_part,
        scores,
        input_grad,
        owned_grad,
        first_new,
        second_new,
        master_new,
        bias_out,
        norm_out,
        small_values,
    )


def solution(mesh):
    blocks = P(("dp", "mp"), None, None)
    rows = P("dp", None)
    return jax.shard_map(
        body,
        mesh=mesh,
        in_specs=(rows, rows, P(), P(), P(), P(), P(), P("mp", None))
        + (blocks,) * 5
        + (P(None, "mp"), P()),
        out_specs=(rows, P(), rows) + (blocks,) * 4 + (P(None, "mp"), P(), P("mp")),
        check_vma=False,
    )
```

```python
import math

import jax
import jax.numpy as jnp
from jax import lax
from jax.experimental import pallas as pl
from jax.experimental.pallas import tpu as pltpu
from jax.sharding import PartitionSpec as P

D = 1024
H = 16
HD = 64
FF = 4096
ROW = 1024
STEP = 10
TILE = 256

low = jnp.bfloat16
wide = jnp.float32
beta_one = 0.9
beta_two = 0.999
adam_eps = 1e-08
norm_eps = 1e-05
block_rate = 0.05
small_rate = 0.1
mib = 2**20

NN = (((1,), (0,)), ((), ()))
NT = (((1,), (1,)), ((), ()))
TN = (((0,), (0,)), ((), ()))


def mul(left, right, dims=NN):
    return lax.dot_general(left, right, dims, preferred_element_type=wide)


def gelu_parts(values):
    normal_cdf = 0.5 * (1.0 + lax.erf(values * 0.7071067811865476))
    slope = normal_cdf + values * jnp.exp(-0.5 * values * values) * 0.3989422804014327
    return ((values * normal_cdf).astype(low), slope)


def adam_plain(grad_now, first_old, second_old, value_old, rate_now):
    first_new = beta_one * first_old + (1.0 - beta_one) * grad_now
    second_new = beta_two * second_old + (1.0 - beta_two) * grad_now * grad_now
    step_dir = (
        first_new
        / (1.0 - beta_one**STEP)
        / (jnp.sqrt(second_new / (1.0 - beta_two**STEP)) + adam_eps)
    )
    return (first_new, second_new, value_old - rate_now * step_dir)


def after(value, *others):
    return lax.optimization_barrier((value,) + others)[0]


def ring_order(count):
    return [k for k in range(count) if k % 2 == 0] + [k for k in range(count) if k % 2][::-1]


def piece_bounds(owned, pieces):
    pieces = pieces if owned % pieces == 0 else 1
    return [owned * k // pieces for k in range(pieces + 1)]


def vmem_call(kernel, name, outs, *args, smem=0, scratch=(), flops=0, room=4):
    vmem = pl.BlockSpec(memory_space=pltpu.VMEM)
    specs = [pl.BlockSpec(memory_space=pltpu.SMEM)] * smem + [vmem] * (len(args) - smem)
    taken = sum(v.size * v.dtype.itemsize for v in args)
    given = sum(v.size * jnp.dtype(v.dtype).itemsize for v in outs)
    held = sum(
        math.prod(v.shape) * jnp.dtype(v.dtype).itemsize for v in scratch if hasattr(v, "shape")
    )
    moved = taken + given
    return pl.pallas_call(
        kernel,
        in_specs=specs,
        out_specs=[vmem] * len(outs),
        out_shape=outs,
        scratch_shapes=list(scratch),
        compiler_params=pltpu.CompilerParams(vmem_limit_bytes=given + held + room * mib),
        cost_estimate=pl.CostEstimate(flops=0, bytes_accessed=1024, transcendentals=0),
        name=name,
    )(*args)


def shaped(dtype, *shape):
    return jax.ShapeDtypeStruct(shape, dtype)


def matrix_views(refs, side):
    for ref in refs:
        for row in range(0, ref.shape[0], side):
            for column in range(0, ref.shape[1], side):
                yield ref.at[row : row + side, column : column + side]


def ring_member(place, count):
    place = lax.rem(place + 2 * count, count)
    return jnp.where(place < count // 2, 2 * place, 2 * count - 1 - 2 * place)


def each_travelling(place_ref, count, owned, bounds, first, visit):
    for k in range(len(bounds) - 1):
        sign = 1 if k % 2 == 0 else -1
        for step in range(count):
            owner = ring_member(place_ref[5] - sign * (first + step), count)
            start = owner * owned + bounds[k]
            for w in range(bounds[k + 1] - bounds[k]):
                visit(k * count + step, w, start + w)


def assemble(place, order, pieces, shapes_list, side, count, owned, bounds):
    def kernel(place_ref, order_ref, *refs):
        parts, outs, blocks = refs[: len(pieces)], refs[len(pieces) : -1], refs[-1]

        def visit(at, w, slot):
            blocks[order_ref[slot]] = parts[at][w]

        each_travelling(place_ref, count, owned, bounds, 0, visit)
        for k, view in enumerate(matrix_views(outs, side)):
            view[...] = blocks[k]

    return vmem_call(
        kernel,
        "assemble",
        [shaped(low, *shape) for shape in shapes_list],
        place,
        order,
        *pieces,
        smem=2,
        scratch=[pltpu.VMEM((count * owned, side, side), low)],
    )


def spread(place, order, matrices, side, count, owned, bounds):
    def kernel(place_ref, order_ref, *refs):
        sources, outs, blocks = refs[: len(matrices)], refs[len(matrices) : -1], refs[-1]
        for k, view in enumerate(matrix_views(sources, side)):
            blocks[k] = view[...]

        def visit(at, w, slot):
            outs[at][w] = blocks[order_ref[slot]]

        each_travelling(place_ref, count, owned, bounds, 1, visit)

    return vmem_call(
        kernel,
        "spread",
        [
            shaped(low, bounds[k + 1] - bounds[k], side, side)
            for k in range(len(bounds) - 1)
            for _ in range(count)
        ],
        place,
        order,
        *matrices,
        smem=2,
        scratch=[pltpu.VMEM((count * owned, side, side), low)],
    )


def add_low(left, right):
    def kernel(a_ref, b_ref, out_ref):
        out_ref[...] = (a_ref[...].astype(wide) + b_ref[...].astype(wide)).astype(low)

    return vmem_call(kernel, "add_low", [shaped(low, *left.shape)], left, right)[0]


def in_order(place, mine, other):
    rows = mine[0].shape[0]
    count = len(mine)

    def kernel(place_ref, *refs):
        out = refs[-1]
        core = place_ref[2]
        for k in range(count):
            for ref, turn in ((refs[k], core), (refs[count + k], 1 - core)):
                start = pl.multiple_of((turn * count + k) * rows, rows)
                out[pl.ds(start, rows), :] = ref[...]

    return vmem_call(
        kernel, "in_order", [shaped(low, 2 * count * rows, D)], place, *mine, *other, smem=1
    )[0]


def feed_grads(hidden, second_rows, first_rows, pre_rows):
    count, rows = len(hidden), hidden[0].shape[0]
    inner = hidden[0].shape[1]

    def kernel(*refs):
        down_ref, up_ref, bias_ref, left, right = refs[4 * count :]

        def fill(target, sources):
            for k, ref in enumerate(sources):
                target[k * rows : (k + 1) * rows, :] = ref[...]

        fill(left, refs[:count])
        fill(right, refs[count : 2 * count])
        down_ref[...] = mul(left[...], right[...], TN).astype(low)
        fill(left, refs[2 * count : 3 * count])
        fill(right, refs[3 * count : 4 * count])
        up_ref[...] = mul(left[...], right[...], TN).astype(low)
        bias_ref[...] = jnp.sum(right[...].astype(wide), axis=0, keepdims=True)

    return vmem_call(
        kernel,
        "feed_grads",
        [shaped(low, inner, D), shaped(low, D, inner), shaped(wide, 1, inner)],
        *hidden,
        *second_rows,
        *first_rows,
        *pre_rows,
        scratch=[pltpu.VMEM((count * rows, D), low), pltpu.VMEM((count * rows, D), low)],
        flops=4 * count * rows * D * inner,
        room=12,
    )


def pair_tables(place, query_lengths, passage_lengths, pairing, score_cot, match_offset):
    queries, passages = query_lengths.shape[1], passage_lengths.shape[1]
    half = ROW // 2
    pair_scale = D ** (-0.5)

    def kernel(place_ref, ql_ref, pl_ref, pair_ref, cot_ref, offset_ref, link_ref, col_ref, row_ref):
        is_query = place_ref[0] == 1
        row = place_ref[1]
        first_core = place_ref[2] == 0
        token = lax.broadcasted_iota(jnp.int32, (1, ROW), 1)
        zero = jnp.zeros((1, ROW), jnp.int32)
        segment, start_at, length_at = zero, zero, zero
        cot = jnp.zeros((1, ROW), wide)
        start = jnp.int32(0)
        for e in range(queries):
            end = start + ql_ref[row, e]
            inside = (token >= start) & (token < end)
            chosen = pair_ref[row, e]
            before = jnp.int32(0)
            length = jnp.int32(1)
            for m in range(passages):
                span = pl_ref[row, m]
                before = before + jnp.where(m < chosen, span, 0)
                length = jnp.where(m == chosen, span, length)
            segment = jnp.where(inside, e, segment)
            start_at = jnp.where(inside, before, start_at)
            length_at = jnp.where(inside, length, length_at)
            cot = jnp.where(inside, cot_ref[row, e] * pair_scale, cot)
            start = end
        passage = zero
        start = jnp.int32(0)
        for m in range(passages):
            start = start + pl_ref[row, m]
            passage = passage + (token >= start).astype(jnp.int32)
        length_at = jnp.maximum(length_at, 1)
        target = start_at + lax.rem(offset_ref[pl.ds(row, 1), :], length_at)
        own = jnp.where(is_query, segment, passage)

        def turn(value):
            swapped = jnp.concatenate([value[:, half:], value[:, :half]], axis=1)
            return jnp.where(first_core, value, swapped)

        token = turn(token)
        target, cot, segment, own = turn(target), turn(cot), turn(segment), turn(own)
        stacked = jnp.concatenate(
            [target.astype(wide), cot, segment.astype(wide), own.astype(wide)]
            + [token.astype(wide)]
            + [jnp.zeros((3, ROW), wide)],
            axis=0,
        )
        columns = stacked.T
        col_ref[...] = columns
        row_ref[...] = own.astype(wide)
        left = jnp.where(is_query, columns[:half, 0:1], columns[:half, 4:5])
        right = jnp.where(is_query, token, target).astype(wide)
        value = jnp.where(is_query, jnp.ones_like(cot), cot)
        link_ref[...] = jnp.where(left == right, value, 0.0).astype(low)

    smem = pl.BlockSpec(memory_space=pltpu.SMEM)
    vmem = pl.BlockSpec(memory_space=pltpu.VMEM)
    return pl.pallas_call(
        kernel,
        in_specs=[smem] * 5 + [vmem],
        out_specs=[vmem] * 3,
        out_shape=[
            jax.ShapeDtypeStruct((half, ROW), low),
            jax.ShapeDtypeStruct((ROW, 8), wide),
            jax.ShapeDtypeStruct((1, ROW), wide),
        ],
        compiler_params=pltpu.CompilerParams(vmem_limit_bytes=16 * mib),
        name="pair_tables",
    )(place, query_lengths, passage_lengths, pairing, score_cot, match_offset)


def halves(value):
    top = value.astype(low)
    return (top, (value - top.astype(wide)).astype(low))


def left_parts(value):
    top, rest = halves(value)
    return jnp.concatenate([top, rest, top], axis=1)


def right_parts(value, axis=0):
    top, rest = halves(value)
    return jnp.concatenate([top, top, rest], axis=axis)


def rotate_first(blocks, left_basis, right_basis):
    count, side = blocks.shape[0], blocks.shape[1]
    group = count // (4 if count % 4 == 0 else 1)

    def kernel(m_ref, l_ref, r_ref, out_ref):
        every = range(group)
        inner = [mul(left_parts(l_ref[b].T), right_parts(m_ref[b])) for b in every]
        for b in every:
            out_ref[b] = mul(left_parts(inner[b]), right_parts(r_ref[b]))

    spec = pl.BlockSpec((group, side, side), lambda t: (t, 0, 0))
    return pl.pallas_call(
        kernel,
        grid=(count // group,),
        in_specs=[spec] * 3,
        out_specs=spec,
        out_shape=jax.ShapeDtypeStruct(blocks.shape, wide),
        compiler_params=pltpu.CompilerParams(vmem_limit_bytes=16 * mib),
        cost_estimate=pl.CostEstimate(
            flops=0, bytes_accessed=1024, transcendentals=0
        ),
        name="rotate_first",
    )(blocks, left_basis, right_basis)


def optimize(came, local, rotated_old, master, first, second, left_basis, right_basis):
    count, side = master.shape[0], master.shape[1]
    pieces = len(came)
    group = count // pieces

    def kernel(*refs):
        came_refs, refs = refs[:pieces], refs[pieces:]
        local_refs, refs = refs[:pieces], refs[pieces:]
        c_ref, w_ref, m_ref, v_ref, l_ref, r_ref, g_out, m_out, v_out, w_out = refs
        for k in range(pieces):

            @pl.when(pl.program_id(0) == k)
            def _():
                g_out[...] = came_refs[k][...].astype(wide) + local_refs[k][...].astype(wide)

        every = range(group)
        for b in every:
            m_out[b] = beta_one * m_ref[b] + (1.0 - beta_one) * g_out[b]
        inner = [mul(left_parts(l_ref[b].T), right_parts(g_out[b])) for b in every]
        turned = [mul(left_parts(inner[b]), right_parts(r_ref[b])) for b in every]
        steps = []
        for b in every:
            second_new = beta_two * v_ref[b] + (1.0 - beta_two) * turned[b] * turned[b]
            v_out[b] = second_new
            first_turned = beta_one * c_ref[b] + (1.0 - beta_one) * turned[b]
            steps.append(
                (first_turned / (1.0 - beta_one**STEP))
                / (jnp.sqrt(second_new / (1.0 - beta_two**STEP)) + adam_eps)
            )
        inner = [mul(left_parts(l_ref[b]), right_parts(steps[b])) for b in every]
        for b in every:
            back = mul(left_parts(inner[b]), right_parts(r_ref[b], 1), NT)
            w_out[b] = w_ref[b] - block_rate * back

    spec = pl.BlockSpec((group, side, side), lambda t: (t, 0, 0))
    vmem = pl.BlockSpec(memory_space=pltpu.VMEM)
    return pl.pallas_call(
        kernel,
        grid=(pieces,),
        in_specs=[vmem] * (2 * pieces) + [spec] * 6,
        out_specs=[spec] * 4,
        out_shape=[jax.ShapeDtypeStruct(master.shape, wide)] * 4,
        compiler_params=pltpu.CompilerParams(vmem_limit_bytes=20 * mib),
        cost_estimate=pl.CostEstimate(
            flops=0, bytes_accessed=1024, transcendentals=0
        ),
        name="optimize",
    )(*came, *local, rotated_old, master, first, second, left_basis, right_basis)


def head_mask(head):
    lane = lax.broadcasted_iota(jnp.int32, (1, 2 * HD), 1)
    return ((lane // HD) == head).astype(low)


def attention_tile(qkv, w_out, table, seg_row, tile, kind):
    width = qkv.shape[1] // 3
    pairs = width // (2 * HD)
    rows = qkv.shape[0]
    span = slice(tile * TILE, (tile + 1) * TILE)

    def kernel(qkv_ref, w_ref, sk_ref, sq_ref, *refs):
        ctx_ref, lse_ref, part_ref = refs[-3:]
        same = sk_ref[:, 3:4] == sq_ref[:, span]
        for pair in range(pairs):
            place = pair * 2 * HD
            lanes = slice(place, place + 2 * HD)
            q = qkv_ref[span, lanes] * jnp.asarray(HD**-0.5, low)
            k = qkv_ref[:, width + place : width + place + 2 * HD]
            v_t = qkv_ref[:, 2 * width + place : 2 * width + place + 2 * HD].T
            parts = []
            for head in range(2):
                s = jnp.where(same, mul(k, q * head_mask(head), NT), -1e30)
                peak = jnp.max(s, axis=0, keepdims=True)
                e = jnp.exp(s - peak)
                total = jnp.sum(e, axis=0, keepdims=True)
                part = mul(v_t[head * HD : (head + 1) * HD], e.astype(low))
                parts.append(part * (1.0 / total))
                lse_ref[pair * 2 + head : pair * 2 + head + 1, :] = peak + jnp.log(total)
            ctx_ref[:, lanes] = jnp.concatenate(parts, axis=0).T.astype(low)
        part_ref[...] = mul(ctx_ref[...], w_ref[...]).astype(kind)

    return vmem_call(
        kernel,
        "attention_tile",
        [shaped(low, TILE, width), shaped(wide, 2 * pairs, TILE), shaped(kind, TILE, D)],
        qkv,
        w_out,
        table,
        seg_row,
        flops=16 * TILE * rows * width,
        room=8,
    )


def norm_rows(place, mixed, came, residual, vectors, which, keep):
    bias_row, gain_row, shift_row = which
    rows = mixed.shape[0]

    def kernel(place_ref, a_ref, b_ref, x_ref, v_ref, low_ref, normed_ref, inverse_ref, last_ref):
        total = a_ref[...].astype(wide) + b_ref[...].astype(wide)
        z = x_ref[...].astype(wide) + total + v_ref[bias_row : bias_row + 1, :]
        center = z - jnp.mean(z, axis=1, keepdims=True)
        inverse = lax.rsqrt(jnp.mean(center * center, axis=1, keepdims=True) + norm_eps)
        normed = center * inverse
        out = v_ref[gain_row : gain_row + 1, :] * normed + v_ref[shift_row : shift_row + 1, :]
        low_ref[...] = out.astype(low)
        normed_ref[...] = normed
        inverse_ref[...] = inverse
        if keep:
            last_ref[...] = out
        else:
            first_chip = place_ref[3] == 0
            last_ref[...] = jnp.where(first_chip, out[: rows // 2], out[rows // 2 :]).astype(low)

    outs = [shaped(low, rows, D), shaped(wide, rows, D), shaped(wide, rows, 1)]
    outs += [shaped(wide, rows, D) if keep else shaped(low, rows // 2, D)]
    return vmem_call(
        kernel,
        "norm_rows",
        outs,
        place,
        mixed,
        came,
        residual,
        vectors,
        smem=1,
        flops=20 * rows * D,
    )


def norm_back(grad_rows, norm_gain, normed, inverse):
    scaled = grad_rows * norm_gain
    first_mean = jnp.mean(scaled, axis=1, keepdims=True)
    second_mean = jnp.mean(scaled * normed, axis=1, keepdims=True)
    return inverse * (scaled - first_mean - normed * second_mean)


def column_sums(grad_z, grad_rows, normed):
    return jnp.concatenate(
        [
            jnp.sum(grad_z, axis=0, keepdims=True),
            jnp.sum(grad_rows * normed, axis=0, keepdims=True),
            jnp.sum(grad_rows, axis=0, keepdims=True),
        ],
        axis=0,
    )


def feed_forward(rows_low, w_up, bias_up, w_down):
    rows, hidden = rows_low.shape[0], w_up.shape[1]

    def kernel(h_ref, up_ref, b_ref, down_ref, part_ref, hid_ref, slope_ref):
        u = mul(h_ref[...], up_ref[...]) + b_ref[...]
        hid, slope = gelu_parts(u)
        hid_ref[...] = hid
        slope_ref[...] = slope
        part_ref[...] = mul(hid, down_ref[...]).astype(part_ref.dtype)

    return vmem_call(
        kernel,
        "feed_forward",
        [shaped(low, rows, D), shaped(low, rows, hidden), shaped(wide, rows, hidden)],
        rows_low,
        w_up,
        bias_up,
        w_down,
        flops=4 * rows * D * hidden,
    )


def feed_back(grad_low, slope, w_up, w_down):
    rows, hidden = grad_low.shape[0], w_up.shape[1]

    def kernel(g_ref, slope_ref, up_ref, down_ref, part_ref, pre_ref):
        pre = (mul(g_ref[...], down_ref[...], NT) * slope_ref[...]).astype(low)
        pre_ref[...] = pre
        part_ref[...] = mul(pre, up_ref[...], NT).astype(part_ref.dtype)

    return vmem_call(
        kernel,
        "feed_back",
        [shaped(low, rows, D), shaped(low, rows, hidden)],
        grad_low,
        slope,
        w_up,
        w_down,
        flops=4 * rows * D * hidden,
    )


def link_back(place, link, table, cot_rows, out_rows, normed, inverse, vectors, pieces, queries):
    rows = out_rows[0].shape[0]
    count = len(out_rows)
    piece_rows = pieces[0].shape[0]

    def kernel(place_ref, link_ref, table_ref, cot_ref, *refs):
        outs, refs = refs[:count], refs[count:]
        norms, refs = refs[:count], refs[count:]
        scales, refs = refs[:count], refs[count:]
        v_ref, refs = refs[0], refs[1:]
        parts, refs = refs[: len(pieces)], refs[len(pieces) :]
        grads, refs = refs[:count], refs[count:]
        lows, refs = refs[:count], refs[count:]
        sums_ref, score_ref, partner = refs
        is_query = place_ref[0] == 1
        chip = place_ref[3]
        for k, part in enumerate(parts):
            turn = chip if k % 2 == 0 else 1 - chip
            start = (k // 2 * 2 + turn) * piece_rows
            partner[pl.ds(pl.multiple_of(start, piece_rows), piece_rows), :] = part[...]
        gain = v_ref[4:5, :]
        sums = jnp.zeros((3, D), wide)
        score = jnp.zeros((1, queries), wide)
        for k in range(count):
            span = slice(k * rows, (k + 1) * rows)
            linked = mul(link_ref[span, :], partner[...])
            token = jnp.sum(outs[k][...].astype(wide) * linked, axis=1, keepdims=True)
            kinds = lax.broadcasted_iota(jnp.int32, (1, queries), 1).astype(wide)
            hot = table_ref[span, 2:3] == kinds
            score = score + jnp.sum(jnp.where(hot, token, 0.0), axis=0, keepdims=True)
            scale = jnp.where(is_query, table_ref[span, 1:2], 1.0)
            start = pl.multiple_of(place_ref[2] * count * rows + k * rows, rows)
            grad_rows = cot_ref[pl.ds(start, rows), :].astype(wide) + scale * linked
            normed_k = norms[k][...]
            grad_z = norm_back(grad_rows, gain, normed_k, scales[k][...])
            grads[k][...] = grad_z
            lows[k][...] = grad_z.astype(low)
            sums = sums + column_sums(grad_z, grad_rows, normed_k)
        sums_ref[...] = sums
        score_ref[...] = jnp.where(is_query, score * D ** (-0.5), 0.0)

    return vmem_call(
        kernel,
        "link_back",
        [shaped(wide, rows, D)] * count
        + [shaped(low, rows, D)] * count
        + [shaped(wide, 3, D), shaped(wide, 1, queries)],
        place,
        link,
        table,
        cot_rows,
        *out_rows,
        *normed,
        *inverse,
        vectors,
        *pieces,
        smem=1,
        scratch=[pltpu.VMEM((ROW, D), low)],
        flops=2 * count * rows * ROW * D,
    )


def first_back(mixed, came, second_grad, normed, inverse, vectors):
    rows = mixed.shape[0]

    def kernel(a_ref, b_ref, g_ref, n_ref, i_ref, v_ref, grad_ref, low_ref, sums_ref):
        total = a_ref[...].astype(wide) + b_ref[...].astype(wide)
        grad_rows = g_ref[...] + total
        normed_k = n_ref[...]
        grad_z = norm_back(grad_rows, v_ref[2:3, :], normed_k, i_ref[...])
        grad_ref[...] = grad_z
        low_ref[...] = grad_z.astype(low)
        sums_ref[...] = column_sums(grad_z, grad_rows, normed_k)

    return vmem_call(
        kernel,
        "first_back",
        [shaped(wide, rows, D), shaped(low, rows, D), shaped(wide, 3, D)],
        mixed,
        came,
        second_grad,
        normed,
        inverse,
        vectors,
        flops=20 * rows * D,
    )


def attention_backward(qkv, w_out, table, seg_row, tiles, contexts, rows_grads, lses, carried):
    width = qkv.shape[1] // 3
    pairs = width // (2 * HD)
    rows = qkv.shape[0]
    count = len(tiles)
    last = carried is not None
    before = [t for t in range(rows // TILE) if t not in tiles]

    def kernel(qkv_ref, w_ref, sk_ref, sq_ref, *refs):
        ctx_refs, refs = refs[:count], refs[count:]
        g_refs, refs = refs[:count], refs[count:]
        lse_refs, refs = refs[:count], refs[count:]
        if last:
            (old_q, old_k, old_v, old_w, old_b), refs = refs[:5], refs[5:]
            out_ref, wgrad_ref, bias_ref, ctx, grad_rows, ctx_grad, lse, gk, gv, sums = refs
        else:
            out_ref, gk, gv, wgrad_ref, sums, ctx, grad_rows, ctx_grad, lse = refs
        for t in range(count):
            span = slice(t * TILE, (t + 1) * TILE)
            ctx[span, :] = ctx_refs[t][...]
            grad_rows[span, :] = g_refs[t][...]
            lse[:, span] = lse_refs[t][...]
        ctx_grad[...] = mul(grad_rows[...], w_ref[...], NT).astype(low)
        wgrad = mul(ctx[...], grad_rows[...], TN)
        if last:
            wgrad_ref[...] = (wgrad + old_w[...]).astype(low)
            gk[...] = old_k[...]
            gv[...] = old_v[...]
            sums[...] = old_b[...]
        else:
            wgrad_ref[...] = wgrad
            gk[...] = jnp.zeros_like(gk)
            gv[...] = jnp.zeros_like(gv)
            sums[...] = jnp.zeros_like(sums)

        def step(index, carry):
            tile = tiles[0] + index
            span = pl.ds(pl.multiple_of(tile * TILE, TILE), TILE)
            here = pl.ds(pl.multiple_of(index * TILE, TILE), TILE)
            same = sk_ref[:, 3:4] == sq_ref[:, span]
            for pair in range(pairs):
                place = pair * 2 * HD
                lanes = slice(place, place + 2 * HD)
                q = qkv_ref[span, lanes] * jnp.asarray(HD**-0.5, low)
                k = qkv_ref[:, width + place : width + place + 2 * HD]
                v = qkv_ref[:, 2 * width + place : 2 * width + place + 2 * HD]
                k_t = k.T
                grad = ctx_grad[here, lanes]
                dots = (grad.astype(wide) * ctx[here, lanes].astype(wide)).T
                parts = []
                for head in range(2):
                    mask = head_mask(head)
                    row = pair * 2 + head
                    q_head = q * mask
                    grad_head = grad * mask
                    features = slice(head * HD, (head + 1) * HD)
                    delta = jnp.sum(dots[features], axis=0, keepdims=True)
                    s = jnp.where(same, mul(k, q_head, NT), -1e30)
                    p = jnp.exp(s - lse[row : row + 1, here])
                    gs = (p * (mul(v, grad_head, NT) - delta)).astype(low)
                    gv[:, lanes] += mul(p.astype(low), grad_head)
                    gk[:, lanes] += mul(gs, q_head)
                    parts.append(mul(k_t[features], gs))
                gq = (jnp.concatenate(parts, axis=0).T * HD**-0.5).astype(low)
                out_ref[span if last else here, lanes] = gq
                sums[:, lanes] += jnp.sum(gq.astype(wide), axis=0, keepdims=True)
            return carry

        lax.fori_loop(0, count, step, 0)
        if last:
            for k, t in enumerate(before):
                out_ref[t * TILE : (t + 1) * TILE, :width] = old_q[k * TILE : (k + 1) * TILE, :]
            out_ref[:, width : 2 * width] = gk[...].astype(low)
            gv_low = gv[...].astype(low)
            out_ref[:, 2 * width :] = gv_low
            bias_ref[:, :width] = sums[...]
            bias_ref[:, width:] = jnp.sum(gv_low.astype(wide), axis=0, keepdims=True)

    scratch = [
        pltpu.VMEM((count * TILE, width), low),
        pltpu.VMEM((count * TILE, D), low),
        pltpu.VMEM((count * TILE, width), low),
        pltpu.VMEM((2 * pairs, count * TILE), wide),
    ]
    if last:
        outs = [shaped(low, rows, 3 * width), shaped(low, width, D), shaped(wide, 1, 2 * width)]
        scratch += [pltpu.VMEM((rows, width), wide)] * 2 + [pltpu.VMEM((1, width), wide)]
    else:
        outs = [shaped(low, count * TILE, width)] + [shaped(wide, rows, width)] * 2
        outs += [shaped(wide, width, D), shaped(wide, 1, width)]
    return vmem_call(
        kernel,
        "attention_backward",
        outs,
        qkv,
        w_out,
        table,
        seg_row,
        *contexts,
        *rows_grads,
        *lses,
        *(carried or []),
        scratch=scratch,
        flops=40 * rows * count * TILE * width,
        room=10,
    )


def pack_sums(place, sums_one, sums_two, score_part):
    queries = score_part.shape[1]

    def kernel(place_ref, one_a, one_b, two_ref, score_ref, out_ref):
        one = one_a[...] + one_b[...]
        two = two_ref[...]
        out_ref[0:1, :] = one[0:1]
        out_ref[1:2, :] = two[0:1]
        out_ref[2:4, :] = one[1:3]
        out_ref[4:6, :] = two[1:3]
        lane = lax.broadcasted_iota(jnp.int32, (1, D), 1)
        first = place_ref[1] * queries
        row = jnp.zeros((1, D), wide)
        score = score_ref[...]
        for e in range(queries):
            row = jnp.where(lane == first + e, score[:, e : e + 1], row)
        out_ref[6:7, :] = row
        out_ref[7:8, :] = jnp.zeros((1, D), wide)

    return vmem_call(
        kernel, "pack_sums", [shaped(wide, 8, D)], place, *sums_one, sums_two, score_part, smem=1
    )[0]


def add_biases(shared, came, pair_bias, up_grad):
    def kernel(a_ref, b_ref, pair_ref, up_ref, out_ref):
        out_ref[0:8, :] = a_ref[...] + b_ref[...]
        zero = jnp.zeros((1, D - pair_ref.shape[1]), wide)
        out_ref[8:9, :] = jnp.concatenate([pair_ref[...], zero], axis=1)
        out_ref[9:10, :] = up_ref[...]
        out_ref[10:16, :] = jnp.zeros((6, D), wide)

    return vmem_call(
        kernel, "add_biases", [shaped(wide, 16, D)], shared, came, pair_bias, up_grad
    )[0]


def small_update(place, total, bias_state, norm_state, local_width, packs, queries):
    bias_count = bias_state.shape[1]
    hidden = bias_count - 2 * local_width
    unit = D // 2
    pieces = norm_state.shape[1] * 2 // 4

    def kernel(place_ref, g_ref, bias_ref, norm_ref, bias_out, norm_out, score_out, value_out, new):
        bias_grad = jnp.concatenate([g_ref[8:9, : 2 * local_width], g_ref[9:10, :hidden]], axis=1)
        first, second, value = adam_plain(
            bias_grad, bias_ref[1:2], bias_ref[2:3], bias_ref[0:1], small_rate
        )
        bias_out[0:1, :] = bias_grad
        bias_out[1:2, :] = first
        bias_out[2:3, :] = second
        for k in range(bias_count // unit):
            value_out[k : k + 1, :] = value[:, k * unit : (k + 1) * unit]
        norm_grad = g_ref[0:6, :]
        first, second, value = adam_plain(
            norm_grad, norm_ref[1], norm_ref[2], norm_ref[0], small_rate
        )
        norm_out[0] = norm_grad
        norm_out[1] = first
        norm_out[2] = second
        for row in range(6):
            for side in range(2):
                new[2 * row + side] = value[row : row + 1, side * unit : (side + 1) * unit]
        start = place_ref[4] * pieces
        for k in range(pieces):
            at = bias_count // unit + k
            value_out[at : at + 1, :] = new[start + k]
        for pack in range(packs):
            score_out[pack : pack + 1, :] = g_ref[6:7, pack * queries : (pack + 1) * queries]

    bias_out, norm_out, scores, values = vmem_call(
        kernel,
        "small_update",
        [
            shaped(wide, 3, bias_count),
            shaped(wide, *norm_state.shape),
            shaped(wide, packs, queries),
            shaped(wide, bias_count // unit + pieces, unit),
        ],
        place,
        total,
        bias_state,
        norm_state,
        smem=1,
        scratch=[pltpu.VMEM((12, 1, unit), wide)],
    )
    return bias_out, norm_out, scores, values


def body(
    layer_input,
    output_cot,
    score_cot,
    query_lengths,
    passage_lengths,
    pairing,
    match_offset,
    block_order,
    block_master,
    block_first,
    block_second,
    basis_left,
    basis_right,
    bias_state,
    norm_state,
):
    mp_count = lax.axis_size("mp")
    dp_count = lax.axis_size("dp")
    dp_index = lax.axis_index("dp")
    mp_index = lax.axis_index("mp")
    core, chip = mp_index % 2, mp_index // 2
    half_dp = dp_count // 2
    is_query = dp_index < half_dp
    table_row = dp_index % half_dp
    side = block_master.shape[1]
    owned = block_master.shape[0]
    local_width = H // mp_count * HD
    hidden_local = FF // mp_count
    shapes_list = [(D, 3 * local_width), (local_width, D), (D, hidden_local), (hidden_local, D)]
    half, quarter = ROW // 2, ROW // 4

    core_pairs = [(s, s ^ 1) for s in range(mp_count)]
    chip_pairs = [(s, s ^ 2) for s in range(mp_count)]

    def core_swap(value):
        return lax.ppermute(value, "mp", core_pairs)

    def chip_swap(value):
        return lax.ppermute(value, "mp", chip_pairs)

    ring = ring_order(dp_count)
    ahead = [(ring[k], ring[(k + 1) % dp_count]) for k in range(dp_count)]
    routes = [ahead, [(b, a) for a, b in ahead]]
    bounds = piece_bounds(owned, 4)
    piece_count = len(bounds) - 1
    order_list = block_order[0]
    ring_place = jnp.where(dp_index % 2 == 0, dp_index // 2, dp_count - 1 - dp_index // 2)
    place = jnp.stack(
        [is_query.astype(jnp.int32), table_row, core, chip, mp_index, ring_place]
    )
    link, seg_column, seg_row = pair_tables(
        place, query_lengths, passage_lengths, pairing, score_cot, match_offset
    )

    bias_now = bias_state[0]
    bias_query = bias_now[:local_width]
    bias_value = bias_now[local_width : 2 * local_width]
    bias_up = bias_now[2 * local_width :]
    qkv_bias = jnp.concatenate([bias_query, jnp.zeros_like(bias_query), bias_value])
    vectors = norm_state[0]

    x_rows = in_order(
        place, [layer_input[:half]], [layer_input[half:]]
    )

    master_low = block_master.astype(low)
    arrived = [[master_low[bounds[k] : bounds[k + 1]]] for k in range(piece_count)]
    for step in range(dp_count - 1):
        for k in range(piece_count):
            arrived[k].append(lax.ppermute(arrived[k][-1], "dp", routes[k % 2]))
        if step == 1:
            held = (arrived[0][-1], link, seg_column, seg_row, x_rows, qkv_bias)
            arrived[0][-1], link, seg_column, seg_row, x_rows, qkv_bias = (
                lax.optimization_barrier(held)
            )
    w_qkv, w_out, w_up, w_down = assemble(
        place,
        order_list,
        [piece for k in range(piece_count) for piece in arrived[k]],
        shapes_list,
        side,
        dp_count,
        owned,
        bounds,
    )

    x_mine = x_rows[:half]
    qkv = (mul(x_rows, w_qkv) + qkv_bias).astype(low)
    tiles = ROW // TILE
    half_tiles = tiles // 2

    def cut(value, k):
        return value[k * quarter : (k + 1) * quarter]

    context, lse, mixed = [None] * tiles, [None] * tiles, [None] * half_tiles
    row = seg_row
    for k in range(half_tiles):
        for t in (half_tiles + k, k):
            context[t], lse[t], part = attention_tile(
                qkv, w_out, seg_column, row, t, wide if t < half_tiles else low
            )
            if t >= half_tiles:
                sent = core_swap(part)
                row = after(seg_row, part)
        mixed[k] = add_low(part, sent)
        row = after(seg_row, mixed[k])
    came = [chip_swap(value) for value in mixed]
    def mix(mine_part, other_part):
        return add_low(mine_part, core_swap(other_part))

    normed_one, inverse_one, first_mine, first_other, first_norm = [], [], [], [], []
    hid_mine, hid_other, slope_mine, slope_other = [], [], [], []
    mine_parts, ffn_mixed = [], []
    up_row = bias_up[None, :]
    ready = mixed[1]
    for k in range(2):
        rows_low, normed_k, inverse_k, rows_wide = norm_rows(
            place, mixed[k], came[k], cut(x_mine, k), after(vectors, ready), (0, 2, 3), True
        )
        first_mine.append(rows_low)
        normed_one.append(normed_k)
        inverse_one.append(inverse_k)
        first_norm.append(rows_wide)
        first_other.append(core_swap(rows_low))
        ready, hid, slope = feed_forward(rows_low, w_up, up_row, w_down)
        mine_parts.append(ready)
        hid_mine.append(hid)
        slope_mine.append(slope)
    for k in range(2):
        other_part, hid, slope = feed_forward(first_other[k], w_up, up_row, w_down)
        hid_other.append(hid)
        slope_other.append(slope)
        ffn_mixed.append(mix(mine_parts[k], other_part))
    mixed = ffn_mixed
    came = [chip_swap(value) for value in mixed]
    normed_two, inverse_two, out_mine, out_other, pieces = [], [], [], [], []
    exchange = [(s, s ^ half_dp) for s in range(dp_count)]
    for k in range(2):
        out_k, normed_k, inverse_k, out_piece = norm_rows(
            place, mixed[k], came[k], first_norm[k], vectors, (1, 4, 5), False
        )
        normed_two.append(normed_k)
        inverse_two.append(inverse_k)
        out_mine.append(out_k)
        out_other.append(core_swap(out_k))
        mine = lax.ppermute(out_piece, "dp", exchange)
        pieces += [mine, chip_swap(mine)]

    output_part = in_order(place, out_mine, out_other)
    pieces = pieces + [core_swap(value) for value in pieces]
    linked = link_back(
        place,
        link,
        seg_column,
        output_cot,
        out_mine,
        normed_two,
        inverse_two,
        vectors,
        pieces,
        score_cot.shape[1],
    )
    second_grad, second_mine = list(linked[:2]), list(linked[2:4])
    sums_two, score_part = linked[4], linked[5]
    second_other = [core_swap(value) for value in second_mine]
    pre_mine, pre_other, mixed = [], [], []
    for k in range(2):
        mine_low = after(second_mine[k], other_part) if k else second_mine[k]
        mine_part, pre = feed_back(mine_low, slope_mine[k], w_up, w_down)
        pre_mine.append(pre)
        other_low = after(second_other[k], mine_part)
        other_part, pre = feed_back(other_low, slope_other[k], w_up, w_down)
        pre_other.append(pre)
        mixed.append(mix(mine_part, other_part))
    came = [chip_swap(value) for value in mixed]
    grad_down, grad_up, up_grad = feed_grads(
        hid_mine + hid_other,
        second_mine + second_other,
        first_mine + first_other,
        pre_mine + pre_other,
    )

    rotated_old = rotate_first(after(block_first, mixed[1]), basis_left, basis_right)
    ready = (vectors, grad_down, grad_up, up_grad, rotated_old, output_part)
    late_vectors, grad_down, grad_up, up_grad, rotated_old, output_part = (
        lax.optimization_barrier(ready)
    )

    first_grad, sums_one, attn_mine, attn_other, carried = [], [], [], [], None

    def attention_part(some):
        rows_grads = attn_mine + attn_other
        return attention_backward(
            qkv,
            w_out,
            seg_column,
            seg_row,
            some,
            [context[t] for t in some],
            [rows_grads[t] for t in some],
            [lse[t] for t in some],
            carried,
        )

    for k in range(2):
        grad_k, low_k, sums_k = first_back(
            mixed[k],
            came[k],
            second_grad[k],
            normed_one[k],
            inverse_one[k],
            late_vectors if carried is None else after(late_vectors, *carried),
        )
        first_grad.append(grad_k)
        sums_one.append(sums_k)
        attn_mine.append(low_k)
        attn_other.append(core_swap(low_k))
        if k == 0:
            carried = attention_part([0])
    shared = pack_sums(place, sums_one, sums_two, score_part)
    shared_came = core_swap(shared)
    seg_row = after(seg_row, shared)
    carried = attention_part(list(range(1, tiles)))
    qkv_grad, grad_out, pair_bias = carried
    grad_qkv = mul(x_rows, qkv_grad, TN).astype(low)
    bounds = piece_bounds(owned, 4)
    piece_count = len(bounds) - 1
    staged = spread(
        place,
        order_list,
        [grad_qkv, grad_out, grad_up, grad_down],
        side,
        dp_count,
        owned,
        bounds,
    )

    small = add_biases(shared, shared_came, pair_bias, up_grad)
    stride = 1
    input_stage = 0
    travelling = [staged[k * dp_count] for k in range(piece_count)]
    for step in range(dp_count - 1):
        for k in range(piece_count):
            came = lax.ppermute(travelling[k], "dp", routes[k % 2])
            if step < dp_count - 2:
                local = staged[k * dp_count + step + 1]
                if step or k:
                    local = after(local, travelling[k - 1])
                if k == 0 and step in (2, 4):
                    local = after(local, small_came)
                came = (came.astype(wide) + local.astype(wide)).astype(low)
            travelling[k] = came
        if step >= dp_count - 2:
            continue
        mark = travelling[piece_count - 1]
        if step % 2 == 0 and stride < dp_count:
            if stride > 1:
                small = after(small, mark) + small_came
            else:
                small = after(small, mark)
            pairs = [(s, s ^ stride) for s in range(dp_count)]
            small_came = lax.ppermute(small, "dp", pairs)
            stride *= 2
        if step == 0:
            late_grad = after(qkv_grad, mark)
            other_part = core_swap(mul(late_grad[half:], w_qkv, NT).astype(low))
            mine_part = mul(late_grad[:half], w_qkv, NT)
        if step == 1:
            mine_part = after(mine_part, mark)
            input_mixed = add_low(mine_part, other_part)
            input_came = chip_swap(input_mixed)
        if step == 4:
            branch_zero = after(input_mixed, mark).astype(wide) + input_came.astype(wide)
            input_mine = (jnp.concatenate(first_grad, axis=0) + branch_zero).astype(low)
            input_other = core_swap(input_mine)
        if step == 5:
            input_grad = in_order(after(place, mark), [input_mine], [input_other])
    small = small + small_came
    while stride < dp_count:
        small = small + lax.ppermute(small, "dp", [(s, s ^ stride) for s in range(dp_count)])
        stride *= 2
    bias_out, norm_out, scores, small_values = small_update(
        place, small, bias_state, norm_state, local_width, *score_cot.shape
    )
    local = [staged[(k + 1) * dp_count - 1] for k in range(piece_count)]

    travelling[0], input_grad = lax.optimization_barrier((travelling[0], input_grad))
    owned_grad, first_new, second_new, master_new = optimize(
        travelling,
        local,
        rotated_old,
        block_master,
        block_first,
        block_second,
        basis_left,
        basis_right,
    )
    small_values, master_new = lax.optimization_barrier((small_values, master_new))
    small_values = small_values.reshape(-1)
    return (
        output_part,
        scores,
        input_grad,
        owned_grad,
        first_new,
        second_new,
        master_new,
        bias_out,
        norm_out,
        small_values,
    )


def solution(mesh):
    blocks = P(("dp", "mp"), None, None)
    rows = P("dp", None)
    return jax.shard_map(
        body,
        mesh=mesh,
        in_specs=(rows, rows, P(), P(), P(), P(), P(), P("mp", None))
        + (blocks,) * 5
        + (P(None, "mp"), P()),
        out_specs=(rows, P(), rows) + (blocks,) * 4 + (P(None, "mp"), P(), P("mp")),
        check_vma=False,
    )
```

```python
import math

import jax
import jax.numpy as jnp
from jax import lax
from jax.experimental import pallas as pl
from jax.experimental.pallas import tpu as pltpu
from jax.sharding import PartitionSpec as P

D = 1024
H = 16
HD = 64
FF = 4096
ROW = 1024
STEP = 10
TILE = 256

low = jnp.bfloat16
wide = jnp.float32
beta_one = 0.9
beta_two = 0.999
adam_eps = 1e-08
norm_eps = 1e-05
block_rate = 0.05
small_rate = 0.1
mib = 2**20

NN = (((1,), (0,)), ((), ()))
NT = (((1,), (1,)), ((), ()))
TN = (((0,), (0,)), ((), ()))


def mul(left, right, dims=NN):
    return lax.dot_general(left, right, dims, preferred_element_type=wide)


def gelu_parts(values):
    normal_cdf = 0.5 * (1.0 + lax.erf(values * 0.7071067811865476))
    slope = normal_cdf + values * jnp.exp(-0.5 * values * values) * 0.3989422804014327
    return ((values * normal_cdf).astype(low), slope)


def adam_plain(grad_now, first_old, second_old, value_old, rate_now):
    first_new = beta_one * first_old + (1.0 - beta_one) * grad_now
    second_new = beta_two * second_old + (1.0 - beta_two) * grad_now * grad_now
    step_dir = (
        first_new
        / (1.0 - beta_one**STEP)
        / (jnp.sqrt(second_new / (1.0 - beta_two**STEP)) + adam_eps)
    )
    return (first_new, second_new, value_old - rate_now * step_dir)


def after(value, *others):
    return lax.optimization_barrier((value,) + others)[0]


def ring_order(count):
    return [k for k in range(count) if k % 2 == 0] + [k for k in range(count) if k % 2][::-1]


def piece_bounds(owned, pieces):
    pieces = pieces if owned % pieces == 0 else 1
    return [owned * k // pieces for k in range(pieces + 1)]


def vmem_call(kernel, name, outs, *args, smem=0, scratch=(), flops=0, room=4):
    vmem = pl.BlockSpec(memory_space=pltpu.VMEM)
    specs = [pl.BlockSpec(memory_space=pltpu.SMEM)] * smem + [vmem] * (len(args) - smem)
    taken = sum(v.size * v.dtype.itemsize for v in args)
    given = sum(v.size * jnp.dtype(v.dtype).itemsize for v in outs)
    held = sum(
        math.prod(v.shape) * jnp.dtype(v.dtype).itemsize for v in scratch if hasattr(v, "shape")
    )
    moved = taken + given
    return pl.pallas_call(
        kernel,
        in_specs=specs,
        out_specs=[vmem] * len(outs),
        out_shape=outs,
        scratch_shapes=list(scratch),
        compiler_params=pltpu.CompilerParams(vmem_limit_bytes=given + held + room * mib),
        cost_estimate=pl.CostEstimate(flops=0, bytes_accessed=1024, transcendentals=0),
        name=name,
    )(*args)


def shaped(dtype, *shape):
    return jax.ShapeDtypeStruct(shape, dtype)


def matrix_views(refs, side):
    for ref in refs:
        for row in range(0, ref.shape[0], side):
            for column in range(0, ref.shape[1], side):
                yield ref.at[row : row + side, column : column + side]


def ring_member(place, count):
    place = lax.rem(place + 2 * count, count)
    return jnp.where(place < count // 2, 2 * place, 2 * count - 1 - 2 * place)


def each_travelling(place_ref, count, owned, bounds, first, visit):
    for k in range(len(bounds) - 1):
        sign = 1 if k % 2 == 0 else -1
        for step in range(count):
            owner = ring_member(place_ref[5] - sign * (first + step), count)
            start = owner * owned + bounds[k]
            for w in range(bounds[k + 1] - bounds[k]):
                visit(k * count + step, w, start + w)


def assemble(place, order, pieces, shapes_list, side, count, owned, bounds):
    def kernel(place_ref, order_ref, *refs):
        parts, outs, blocks = refs[: len(pieces)], refs[len(pieces) : -1], refs[-1]

        def visit(at, w, slot):
            blocks[order_ref[slot]] = parts[at][w]

        each_travelling(place_ref, count, owned, bounds, 0, visit)
        for k, view in enumerate(matrix_views(outs, side)):
            view[...] = blocks[k]

    return vmem_call(
        kernel,
        "assemble",
        [shaped(low, *shape) for shape in shapes_list],
        place,
        order,
        *pieces,
        smem=2,
        scratch=[pltpu.VMEM((count * owned, side, side), low)],
    )


def spread(place, order, matrices, side, count, owned, bounds):
    def kernel(place_ref, order_ref, *refs):
        sources, outs, blocks = refs[: len(matrices)], refs[len(matrices) : -1], refs[-1]
        for k, view in enumerate(matrix_views(sources, side)):
            blocks[k] = view[...]

        def visit(at, w, slot):
            outs[at][w] = blocks[order_ref[slot]]

        each_travelling(place_ref, count, owned, bounds, 1, visit)

    return vmem_call(
        kernel,
        "spread",
        [
            shaped(low, bounds[k + 1] - bounds[k], side, side)
            for k in range(len(bounds) - 1)
            for _ in range(count)
        ],
        place,
        order,
        *matrices,
        smem=2,
        scratch=[pltpu.VMEM((count * owned, side, side), low)],
    )


def joined(refs):
    values = [ref[...] for ref in refs]
    return values[0] if len(values) == 1 else jnp.concatenate(values, axis=0)


def add_low(left, right):
    def kernel(a_ref, *refs):
        refs[-1][...] = (a_ref[...].astype(wide) + joined(refs[:-1]).astype(wide)).astype(low)

    return vmem_call(kernel, "add_low", [shaped(low, *left.shape)], left, *right)[0]


def in_order(place, mine, other):
    rows = mine[0].shape[0]
    count = len(mine)

    def kernel(place_ref, *refs):
        out = refs[-1]
        core = place_ref[2]
        for k in range(count):
            for ref, turn in ((refs[k], core), (refs[count + k], 1 - core)):
                start = pl.multiple_of((turn * count + k) * rows, rows)
                out[pl.ds(start, rows), :] = ref[...]

    return vmem_call(
        kernel, "in_order", [shaped(low, 2 * count * rows, D)], place, *mine, *other, smem=1
    )[0]


def feed_grads(hidden, second_rows, first_rows, pre_rows):
    count, rows = len(hidden), hidden[0].shape[0]
    inner = hidden[0].shape[1]
    pieces = 3 * count + len(first_rows)

    def kernel(*refs):
        down_ref, up_ref, bias_ref, left, right = refs[pieces:]

        def fill(target, sources):
            start = 0
            for ref in sources:
                target[start : start + ref.shape[0], :] = ref[...]
                start += ref.shape[0]

        fill(left, refs[:count])
        fill(right, refs[count : 2 * count])
        down_ref[...] = mul(left[...], right[...], TN).astype(low)
        fill(left, refs[2 * count : pieces - count])
        fill(right, refs[pieces - count : pieces])
        up_ref[...] = mul(left[...], right[...], TN).astype(low)
        bias_ref[...] = jnp.sum(right[...].astype(wide), axis=0, keepdims=True)

    return vmem_call(
        kernel,
        "feed_grads",
        [shaped(low, inner, D), shaped(low, D, inner), shaped(wide, 1, inner)],
        *hidden,
        *second_rows,
        *first_rows,
        *pre_rows,
        scratch=[pltpu.VMEM((count * rows, D), low), pltpu.VMEM((count * rows, D), low)],
        flops=4 * count * rows * D * inner,
        room=12,
    )


def pair_tables(place, query_lengths, passage_lengths, pairing, score_cot, match_offset):
    queries, passages = query_lengths.shape[1], passage_lengths.shape[1]
    half = ROW // 2
    pair_scale = D ** (-0.5)

    def kernel(place_ref, ql_ref, pl_ref, pair_ref, cot_ref, offset_ref, link_ref, col_ref, row_ref):
        is_query = place_ref[0] == 1
        row = place_ref[1]
        first_core = place_ref[2] == 0
        token = lax.broadcasted_iota(jnp.int32, (1, ROW), 1)
        zero = jnp.zeros((1, ROW), jnp.int32)
        segment, start_at, length_at = zero, zero, zero
        cot = jnp.zeros((1, ROW), wide)
        start = jnp.int32(0)
        for e in range(queries):
            end = start + ql_ref[row, e]
            inside = (token >= start) & (token < end)
            chosen = pair_ref[row, e]
            before = jnp.int32(0)
            length = jnp.int32(1)
            for m in range(passages):
                span = pl_ref[row, m]
                before = before + jnp.where(m < chosen, span, 0)
                length = jnp.where(m == chosen, span, length)
            segment = jnp.where(inside, e, segment)
            start_at = jnp.where(inside, before, start_at)
            length_at = jnp.where(inside, length, length_at)
            cot = jnp.where(inside, cot_ref[row, e] * pair_scale, cot)
            start = end
        passage = zero
        start = jnp.int32(0)
        for m in range(passages):
            start = start + pl_ref[row, m]
            passage = passage + (token >= start).astype(jnp.int32)
        length_at = jnp.maximum(length_at, 1)
        target = start_at + lax.rem(offset_ref[pl.ds(row, 1), :], length_at)
        own = jnp.where(is_query, segment, passage)

        def turn(value):
            swapped = jnp.concatenate([value[:, half:], value[:, :half]], axis=1)
            return jnp.where(first_core, value, swapped)

        token = turn(token)
        target, cot, segment, own = turn(target), turn(cot), turn(segment), turn(own)
        stacked = jnp.concatenate(
            [target.astype(wide), cot, segment.astype(wide), own.astype(wide)]
            + [token.astype(wide)]
            + [jnp.zeros((3, ROW), wide)],
            axis=0,
        )
        columns = stacked.T
        col_ref[...] = columns
        row_ref[...] = own.astype(wide)
        left = jnp.where(is_query, columns[:half, 0:1], columns[:half, 4:5])
        right = jnp.where(is_query, token, target).astype(wide)
        value = jnp.where(is_query, jnp.ones_like(cot), cot)
        link_ref[...] = jnp.where(left == right, value, 0.0).astype(low)

    smem = pl.BlockSpec(memory_space=pltpu.SMEM)
    vmem = pl.BlockSpec(memory_space=pltpu.VMEM)
    return pl.pallas_call(
        kernel,
        in_specs=[smem] * 5 + [vmem],
        out_specs=[vmem] * 3,
        out_shape=[
            jax.ShapeDtypeStruct((half, ROW), low),
            jax.ShapeDtypeStruct((ROW, 8), wide),
            jax.ShapeDtypeStruct((1, ROW), wide),
        ],
        compiler_params=pltpu.CompilerParams(vmem_limit_bytes=16 * mib),
        name="pair_tables",
    )(place, query_lengths, passage_lengths, pairing, score_cot, match_offset)


def halves(value):
    top = value.astype(low)
    return (top, (value - top.astype(wide)).astype(low))


def left_parts(value):
    top, rest = halves(value)
    return jnp.concatenate([top, rest, top], axis=1)


def right_parts(value, axis=0):
    top, rest = halves(value)
    return jnp.concatenate([top, top, rest], axis=axis)


def rotate_first(blocks, left_basis, right_basis):
    count, side = blocks.shape[0], blocks.shape[1]
    group = count // (4 if count % 4 == 0 else 1)

    def kernel(m_ref, l_ref, r_ref, out_ref):
        every = range(group)
        inner = [mul(left_parts(l_ref[b].T), right_parts(m_ref[b])) for b in every]
        for b in every:
            out_ref[b] = mul(left_parts(inner[b]), right_parts(r_ref[b]))

    spec = pl.BlockSpec((group, side, side), lambda t: (t, 0, 0))
    return pl.pallas_call(
        kernel,
        grid=(count // group,),
        in_specs=[spec] * 3,
        out_specs=spec,
        out_shape=jax.ShapeDtypeStruct(blocks.shape, wide),
        compiler_params=pltpu.CompilerParams(vmem_limit_bytes=16 * mib),
        cost_estimate=pl.CostEstimate(
            flops=0, bytes_accessed=1024, transcendentals=0
        ),
        name="rotate_first",
    )(blocks, left_basis, right_basis)


def optimize(came, local, rotated_old, master, first, second, left_basis, right_basis):
    count, side = master.shape[0], master.shape[1]
    pieces = len(came)
    group = count // pieces

    def kernel(*refs):
        came_refs, refs = refs[:pieces], refs[pieces:]
        local_refs, refs = refs[:pieces], refs[pieces:]
        c_ref, w_ref, m_ref, v_ref, l_ref, r_ref, g_out, m_out, v_out, w_out = refs
        for k in range(pieces):

            @pl.when(pl.program_id(0) == k)
            def _():
                g_out[...] = came_refs[k][...].astype(wide) + local_refs[k][...].astype(wide)

        every = range(group)
        for b in every:
            m_out[b] = beta_one * m_ref[b] + (1.0 - beta_one) * g_out[b]
        inner = [mul(left_parts(l_ref[b].T), right_parts(g_out[b])) for b in every]
        turned = [mul(left_parts(inner[b]), right_parts(r_ref[b])) for b in every]
        steps = []
        for b in every:
            second_new = beta_two * v_ref[b] + (1.0 - beta_two) * turned[b] * turned[b]
            v_out[b] = second_new
            first_turned = beta_one * c_ref[b] + (1.0 - beta_one) * turned[b]
            steps.append(
                (first_turned / (1.0 - beta_one**STEP))
                / (jnp.sqrt(second_new / (1.0 - beta_two**STEP)) + adam_eps)
            )
        inner = [mul(left_parts(l_ref[b]), right_parts(steps[b])) for b in every]
        for b in every:
            back = mul(left_parts(inner[b]), right_parts(r_ref[b], 1), NT)
            w_out[b] = w_ref[b] - block_rate * back

    spec = pl.BlockSpec((group, side, side), lambda t: (t, 0, 0))
    vmem = pl.BlockSpec(memory_space=pltpu.VMEM)
    return pl.pallas_call(
        kernel,
        grid=(pieces,),
        in_specs=[vmem] * (2 * pieces) + [spec] * 6,
        out_specs=[spec] * 4,
        out_shape=[jax.ShapeDtypeStruct(master.shape, wide)] * 4,
        compiler_params=pltpu.CompilerParams(vmem_limit_bytes=20 * mib),
        cost_estimate=pl.CostEstimate(
            flops=0, bytes_accessed=1024, transcendentals=0
        ),
        name="optimize",
    )(*came, *local, rotated_old, master, first, second, left_basis, right_basis)


def head_mask(head):
    lane = lax.broadcasted_iota(jnp.int32, (1, 2 * HD), 1)
    return ((lane // HD) == head).astype(low)


def attention_tile(qkv, w_out, table, seg_row, tile, kind, pieces):
    width = qkv.shape[1] // 3
    pairs = width // (2 * HD)
    rows = qkv.shape[0]
    span = slice(tile * TILE, (tile + 1) * TILE)

    def kernel(qkv_ref, w_ref, sk_ref, sq_ref, *refs):
        ctx_ref, lse_ref, *part_refs = refs
        same = sk_ref[:, 3:4] == sq_ref[:, span]
        for pair in range(pairs):
            place = pair * 2 * HD
            lanes = slice(place, place + 2 * HD)
            q = qkv_ref[span, lanes] * jnp.asarray(HD**-0.5, low)
            k = qkv_ref[:, width + place : width + place + 2 * HD]
            v_t = qkv_ref[:, 2 * width + place : 2 * width + place + 2 * HD].T
            parts = []
            for head in range(2):
                s = jnp.where(same, mul(k, q * head_mask(head), NT), -1e30)
                peak = jnp.max(s, axis=0, keepdims=True)
                e = jnp.exp(s - peak)
                total = jnp.sum(e, axis=0, keepdims=True)
                part = mul(v_t[head * HD : (head + 1) * HD], e.astype(low))
                parts.append(part * (1.0 / total))
                lse_ref[pair * 2 + head : pair * 2 + head + 1, :] = peak + jnp.log(total)
            ctx_ref[:, lanes] = jnp.concatenate(parts, axis=0).T.astype(low)
        part = mul(ctx_ref[...], w_ref[...]).astype(kind)
        size = TILE // len(part_refs)
        for k, part_ref in enumerate(part_refs):
            part_ref[...] = part[k * size : (k + 1) * size]

    return vmem_call(
        kernel,
        "attention_tile",
        [shaped(low, TILE, width), shaped(wide, 2 * pairs, TILE)]
        + [shaped(kind, TILE // pieces, D)] * pieces,
        qkv,
        w_out,
        table,
        seg_row,
        flops=16 * TILE * rows * width,
        room=8,
    )


def norm_rows(place, mixed, came, residual, vectors, which, keep):
    bias_row, gain_row, shift_row = which
    rows = mixed.shape[0]

    pieces = 2 if keep else 1

    def kernel(place_ref, a_ref, b_ref, x_ref, v_ref, normed_ref, inverse_ref, last_ref, *low_refs):
        total = a_ref[...].astype(wide) + b_ref[...].astype(wide)
        z = x_ref[...].astype(wide) + total + v_ref[bias_row : bias_row + 1, :]
        center = z - jnp.mean(z, axis=1, keepdims=True)
        inverse = lax.rsqrt(jnp.mean(center * center, axis=1, keepdims=True) + norm_eps)
        normed = center * inverse
        out = v_ref[gain_row : gain_row + 1, :] * normed + v_ref[shift_row : shift_row + 1, :]
        out_low = out.astype(low)
        for k, low_ref in enumerate(low_refs):
            low_ref[...] = out_low[k * rows // pieces : (k + 1) * rows // pieces]
        normed_ref[...] = normed
        inverse_ref[...] = inverse
        if keep:
            last_ref[...] = out
        else:
            first_chip = place_ref[3] == 0
            last_ref[...] = jnp.where(first_chip, out[: rows // 2], out[rows // 2 :]).astype(low)

    outs = [shaped(wide, rows, D), shaped(wide, rows, 1)]
    outs += [shaped(wide, rows, D) if keep else shaped(low, rows // 2, D)]
    outs += [shaped(low, rows // pieces, D)] * pieces
    return vmem_call(
        kernel,
        "norm_rows",
        outs,
        place,
        mixed,
        came,
        residual,
        vectors,
        smem=1,
        flops=20 * rows * D,
    )


def norm_back(grad_rows, norm_gain, normed, inverse):
    scaled = grad_rows * norm_gain
    first_mean = jnp.mean(scaled, axis=1, keepdims=True)
    second_mean = jnp.mean(scaled * normed, axis=1, keepdims=True)
    return inverse * (scaled - first_mean - normed * second_mean)


def column_sums(grad_z, grad_rows, normed):
    return jnp.concatenate(
        [
            jnp.sum(grad_z, axis=0, keepdims=True),
            jnp.sum(grad_rows * normed, axis=0, keepdims=True),
            jnp.sum(grad_rows, axis=0, keepdims=True),
        ],
        axis=0,
    )


def feed_forward(rows_low, w_up, bias_up, w_down):
    rows, hidden = sum(value.shape[0] for value in rows_low), w_up.shape[1]

    def kernel(up_ref, b_ref, down_ref, *refs):
        part_ref, hid_ref, slope_ref = refs[-3:]
        u = mul(joined(refs[:-3]), up_ref[...]) + b_ref[...]
        hid, slope = gelu_parts(u)
        hid_ref[...] = hid
        slope_ref[...] = slope
        part_ref[...] = mul(hid, down_ref[...]).astype(part_ref.dtype)

    return vmem_call(
        kernel,
        "feed_forward",
        [shaped(low, rows, D), shaped(low, rows, hidden), shaped(wide, rows, hidden)],
        w_up,
        bias_up,
        w_down,
        *rows_low,
        flops=4 * rows * D * hidden,
    )


def feed_back(grad_low, slope, w_up, w_down):
    rows, hidden = grad_low.shape[0], w_up.shape[1]

    def kernel(g_ref, slope_ref, up_ref, down_ref, part_ref, pre_ref):
        pre = (mul(g_ref[...], down_ref[...], NT) * slope_ref[...]).astype(low)
        pre_ref[...] = pre
        part_ref[...] = mul(pre, up_ref[...], NT).astype(part_ref.dtype)

    return vmem_call(
        kernel,
        "feed_back",
        [shaped(low, rows, D), shaped(low, rows, hidden)],
        grad_low,
        slope,
        w_up,
        w_down,
        flops=4 * rows * D * hidden,
    )


def link_back(place, link, table, cot_rows, out_rows, normed, inverse, vectors, pieces, queries):
    rows = out_rows[0].shape[0]
    count = len(out_rows)
    piece_rows = pieces[0].shape[0]

    def kernel(place_ref, link_ref, table_ref, cot_ref, *refs):
        outs, refs = refs[:count], refs[count:]
        norms, refs = refs[:count], refs[count:]
        scales, refs = refs[:count], refs[count:]
        v_ref, refs = refs[0], refs[1:]
        parts, refs = refs[: len(pieces)], refs[len(pieces) :]
        grads, refs = refs[:count], refs[count:]
        lows, refs = refs[:count], refs[count:]
        sums_ref, score_ref, partner = refs
        is_query = place_ref[0] == 1
        chip = place_ref[3]
        for k, part in enumerate(parts):
            turn = chip if k % 2 == 0 else 1 - chip
            start = (k // 2 * 2 + turn) * piece_rows
            partner[pl.ds(pl.multiple_of(start, piece_rows), piece_rows), :] = part[...]
        gain = v_ref[4:5, :]
        sums = jnp.zeros((3, D), wide)
        score = jnp.zeros((1, queries), wide)
        for k in range(count):
            span = slice(k * rows, (k + 1) * rows)
            linked = mul(link_ref[span, :], partner[...])
            token = jnp.sum(outs[k][...].astype(wide) * linked, axis=1, keepdims=True)
            kinds = lax.broadcasted_iota(jnp.int32, (1, queries), 1).astype(wide)
            hot = table_ref[span, 2:3] == kinds
            score = score + jnp.sum(jnp.where(hot, token, 0.0), axis=0, keepdims=True)
            scale = jnp.where(is_query, table_ref[span, 1:2], 1.0)
            start = pl.multiple_of(place_ref[2] * count * rows + k * rows, rows)
            grad_rows = cot_ref[pl.ds(start, rows), :].astype(wide) + scale * linked
            normed_k = norms[k][...]
            grad_z = norm_back(grad_rows, gain, normed_k, scales[k][...])
            grads[k][...] = grad_z
            lows[k][...] = grad_z.astype(low)
            sums = sums + column_sums(grad_z, grad_rows, normed_k)
        sums_ref[...] = sums
        score_ref[...] = jnp.where(is_query, score * D ** (-0.5), 0.0)

    return vmem_call(
        kernel,
        "link_back",
        [shaped(wide, rows, D)] * count
        + [shaped(low, rows, D)] * count
        + [shaped(wide, 3, D), shaped(wide, 1, queries)],
        place,
        link,
        table,
        cot_rows,
        *out_rows,
        *normed,
        *inverse,
        vectors,
        *pieces,
        smem=1,
        scratch=[pltpu.VMEM((ROW, D), low)],
        flops=2 * count * rows * ROW * D,
    )


def first_back(mixed, came, second_grad, normed, inverse, vectors):
    rows = mixed.shape[0]

    def kernel(a_ref, b_ref, g_ref, n_ref, i_ref, v_ref, grad_ref, sums_ref, *low_refs):
        total = a_ref[...].astype(wide) + b_ref[...].astype(wide)
        grad_rows = g_ref[...] + total
        normed_k = n_ref[...]
        grad_z = norm_back(grad_rows, v_ref[2:3, :], normed_k, i_ref[...])
        grad_ref[...] = grad_z
        grad_low = grad_z.astype(low)
        for k, low_ref in enumerate(low_refs):
            low_ref[...] = grad_low[k * rows // 2 : (k + 1) * rows // 2]
        sums_ref[...] = column_sums(grad_z, grad_rows, normed_k)

    return vmem_call(
        kernel,
        "first_back",
        [shaped(wide, rows, D), shaped(wide, 3, D)] + [shaped(low, rows // 2, D)] * 2,
        mixed,
        came,
        second_grad,
        normed,
        inverse,
        vectors,
        flops=20 * rows * D,
    )


def attention_backward(qkv, w_out, table, seg_row, tiles, contexts, rows_grads, lses, carried):
    width = qkv.shape[1] // 3
    pairs = width // (2 * HD)
    rows = qkv.shape[0]
    count = len(tiles)
    last = carried is not None
    before = [t for t in range(rows // TILE) if t not in tiles]

    def kernel(qkv_ref, w_ref, sk_ref, sq_ref, *refs):
        ctx_refs, refs = refs[:count], refs[count:]
        g_refs, refs = refs[: len(rows_grads)], refs[len(rows_grads) :]
        lse_refs, refs = refs[:count], refs[count:]
        if last:
            (old_q, old_k, old_v, old_w, old_b), refs = refs[:5], refs[5:]
            out_ref, wgrad_ref, bias_ref, ctx, grad_rows, ctx_grad, lse, gk, gv, sums = refs
        else:
            out_ref, gk, gv, wgrad_ref, sums, ctx, grad_rows, ctx_grad, lse = refs
        for t in range(count):
            span = slice(t * TILE, (t + 1) * TILE)
            ctx[span, :] = ctx_refs[t][...]
            lse[:, span] = lse_refs[t][...]
        for k, ref in enumerate(g_refs):
            grad_rows[k * ref.shape[0] : (k + 1) * ref.shape[0], :] = ref[...]
        ctx_grad[...] = mul(grad_rows[...], w_ref[...], NT).astype(low)
        wgrad = mul(ctx[...], grad_rows[...], TN)
        if last:
            wgrad_ref[...] = (wgrad + old_w[...]).astype(low)
            gk[...] = old_k[...]
            gv[...] = old_v[...]
            sums[...] = old_b[...]
        else:
            wgrad_ref[...] = wgrad
            gk[...] = jnp.zeros_like(gk)
            gv[...] = jnp.zeros_like(gv)
            sums[...] = jnp.zeros_like(sums)

        def step(index, carry):
            tile = tiles[0] + (tiles[1] - tiles[0]) * index
            span = pl.ds(pl.multiple_of(tile * TILE, TILE), TILE)
            here = pl.ds(pl.multiple_of(index * TILE, TILE), TILE)
            same = sk_ref[:, 3:4] == sq_ref[:, span]
            for pair in range(pairs):
                place = pair * 2 * HD
                lanes = slice(place, place + 2 * HD)
                q = qkv_ref[span, lanes] * jnp.asarray(HD**-0.5, low)
                k = qkv_ref[:, width + place : width + place + 2 * HD]
                v = qkv_ref[:, 2 * width + place : 2 * width + place + 2 * HD]
                k_t = k.T
                grad = ctx_grad[here, lanes]
                dots = (grad.astype(wide) * ctx[here, lanes].astype(wide)).T
                parts = []
                for head in range(2):
                    mask = head_mask(head)
                    row = pair * 2 + head
                    q_head = q * mask
                    grad_head = grad * mask
                    features = slice(head * HD, (head + 1) * HD)
                    delta = jnp.sum(dots[features], axis=0, keepdims=True)
                    s = jnp.where(same, mul(k, q_head, NT), -1e30)
                    p = jnp.exp(s - lse[row : row + 1, here])
                    gs = (p * (mul(v, grad_head, NT) - delta)).astype(low)
                    gv[:, lanes] += mul(p.astype(low), grad_head)
                    gk[:, lanes] += mul(gs, q_head)
                    parts.append(mul(k_t[features], gs))
                gq = (jnp.concatenate(parts, axis=0).T * HD**-0.5).astype(low)
                out_ref[span if last else here, lanes] = gq
                sums[:, lanes] += jnp.sum(gq.astype(wide), axis=0, keepdims=True)
            return carry

        lax.fori_loop(0, count, step, 0)
        if last:
            for k, t in enumerate(before):
                out_ref[t * TILE : (t + 1) * TILE, :width] = old_q[k * TILE : (k + 1) * TILE, :]
            out_ref[:, width : 2 * width] = gk[...].astype(low)
            gv_low = gv[...].astype(low)
            out_ref[:, 2 * width :] = gv_low
            bias_ref[:, :width] = sums[...]
            bias_ref[:, width:] = jnp.sum(gv_low.astype(wide), axis=0, keepdims=True)

    scratch = [
        pltpu.VMEM((count * TILE, width), low),
        pltpu.VMEM((count * TILE, D), low),
        pltpu.VMEM((count * TILE, width), low),
        pltpu.VMEM((2 * pairs, count * TILE), wide),
    ]
    if last:
        outs = [shaped(low, rows, 3 * width), shaped(low, width, D), shaped(wide, 1, 2 * width)]
        scratch += [pltpu.VMEM((rows, width), wide)] * 2 + [pltpu.VMEM((1, width), wide)]
    else:
        outs = [shaped(low, count * TILE, width)] + [shaped(wide, rows, width)] * 2
        outs += [shaped(wide, width, D), shaped(wide, 1, width)]
    return vmem_call(
        kernel,
        "attention_backward",
        outs,
        qkv,
        w_out,
        table,
        seg_row,
        *contexts,
        *rows_grads,
        *lses,
        *(carried or []),
        scratch=scratch,
        flops=40 * rows * count * TILE * width,
        room=10,
    )


def pack_sums(place, sums_one, sums_two, score_part):
    queries = score_part.shape[1]

    def kernel(place_ref, one_a, one_b, two_ref, score_ref, out_ref):
        one = one_a[...] + one_b[...]
        two = two_ref[...]
        out_ref[0:1, :] = one[0:1]
        out_ref[1:2, :] = two[0:1]
        out_ref[2:4, :] = one[1:3]
        out_ref[4:6, :] = two[1:3]
        lane = lax.broadcasted_iota(jnp.int32, (1, D), 1)
        first = place_ref[1] * queries
        row = jnp.zeros((1, D), wide)
        score = score_ref[...]
        for e in range(queries):
            row = jnp.where(lane == first + e, score[:, e : e + 1], row)
        out_ref[6:7, :] = row
        out_ref[7:8, :] = jnp.zeros((1, D), wide)

    return vmem_call(
        kernel, "pack_sums", [shaped(wide, 8, D)], place, *sums_one, sums_two, score_part, smem=1
    )[0]


def add_biases(shared, came, pair_bias, up_grad):
    def kernel(a_ref, b_ref, pair_ref, up_ref, out_ref):
        out_ref[0:8, :] = a_ref[...] + b_ref[...]
        zero = jnp.zeros((1, D - pair_ref.shape[1]), wide)
        out_ref[8:9, :] = jnp.concatenate([pair_ref[...], zero], axis=1)
        out_ref[9:10, :] = up_ref[...]
        out_ref[10:16, :] = jnp.zeros((6, D), wide)

    return vmem_call(
        kernel, "add_biases", [shaped(wide, 16, D)], shared, came, pair_bias, up_grad
    )[0]


def small_update(place, total, bias_state, norm_state, local_width, packs, queries):
    bias_count = bias_state.shape[1]
    hidden = bias_count - 2 * local_width
    unit = D // 2
    pieces = norm_state.shape[1] * 2 // 4

    def kernel(place_ref, g_ref, bias_ref, norm_ref, bias_out, norm_out, score_out, value_out, new):
        bias_grad = jnp.concatenate([g_ref[8:9, : 2 * local_width], g_ref[9:10, :hidden]], axis=1)
        first, second, value = adam_plain(
            bias_grad, bias_ref[1:2], bias_ref[2:3], bias_ref[0:1], small_rate
        )
        bias_out[0:1, :] = bias_grad
        bias_out[1:2, :] = first
        bias_out[2:3, :] = second
        for k in range(bias_count // unit):
            value_out[k : k + 1, :] = value[:, k * unit : (k + 1) * unit]
        norm_grad = g_ref[0:6, :]
        first, second, value = adam_plain(
            norm_grad, norm_ref[1], norm_ref[2], norm_ref[0], small_rate
        )
        norm_out[0] = norm_grad
        norm_out[1] = first
        norm_out[2] = second
        for row in range(6):
            for side in range(2):
                new[2 * row + side] = value[row : row + 1, side * unit : (side + 1) * unit]
        start = place_ref[4] * pieces
        for k in range(pieces):
            at = bias_count // unit + k
            value_out[at : at + 1, :] = new[start + k]
        for pack in range(packs):
            score_out[pack : pack + 1, :] = g_ref[6:7, pack * queries : (pack + 1) * queries]

    bias_out, norm_out, scores, values = vmem_call(
        kernel,
        "small_update",
        [
            shaped(wide, 3, bias_count),
            shaped(wide, *norm_state.shape),
            shaped(wide, packs, queries),
            shaped(wide, bias_count // unit + pieces, unit),
        ],
        place,
        total,
        bias_state,
        norm_state,
        smem=1,
        scratch=[pltpu.VMEM((12, 1, unit), wide)],
    )
    return bias_out, norm_out, scores, values


def body(
    layer_input,
    output_cot,
    score_cot,
    query_lengths,
    passage_lengths,
    pairing,
    match_offset,
    block_order,
    block_master,
    block_first,
    block_second,
    basis_left,
    basis_right,
    bias_state,
    norm_state,
):
    mp_count = lax.axis_size("mp")
    dp_count = lax.axis_size("dp")
    dp_index = lax.axis_index("dp")
    mp_index = lax.axis_index("mp")
    core, chip = mp_index % 2, mp_index // 2
    half_dp = dp_count // 2
    is_query = dp_index < half_dp
    table_row = dp_index % half_dp
    side = block_master.shape[1]
    owned = block_master.shape[0]
    local_width = H // mp_count * HD
    hidden_local = FF // mp_count
    shapes_list = [(D, 3 * local_width), (local_width, D), (D, hidden_local), (hidden_local, D)]
    half, quarter = ROW // 2, ROW // 4

    core_pairs = [(s, s ^ 1) for s in range(mp_count)]
    chip_pairs = [(s, s ^ 2) for s in range(mp_count)]

    def core_swap(value):
        return lax.ppermute(value, "mp", core_pairs)

    def chip_swap(value):
        return lax.ppermute(value, "mp", chip_pairs)

    ring = ring_order(dp_count)
    ahead = [(ring[k], ring[(k + 1) % dp_count]) for k in range(dp_count)]
    routes = [ahead, [(b, a) for a, b in ahead]]
    bounds = piece_bounds(owned, 4)
    piece_count = len(bounds) - 1
    order_list = block_order[0]
    ring_place = jnp.where(dp_index % 2 == 0, dp_index // 2, dp_count - 1 - dp_index // 2)
    place = jnp.stack(
        [is_query.astype(jnp.int32), table_row, core, chip, mp_index, ring_place]
    )
    link, seg_column, seg_row = pair_tables(
        place, query_lengths, passage_lengths, pairing, score_cot, match_offset
    )

    bias_now = bias_state[0]
    bias_query = bias_now[:local_width]
    bias_value = bias_now[local_width : 2 * local_width]
    bias_up = bias_now[2 * local_width :]
    qkv_bias = jnp.concatenate([bias_query, jnp.zeros_like(bias_query), bias_value])
    vectors = norm_state[0]

    x_rows = in_order(
        place, [layer_input[:half]], [layer_input[half:]]
    )

    master_low = block_master.astype(low)
    arrived = [[master_low[bounds[k] : bounds[k + 1]]] for k in range(piece_count)]
    for step in range(dp_count - 1):
        for k in range(piece_count):
            arrived[k].append(lax.ppermute(arrived[k][-1], "dp", routes[k % 2]))
        if step == 1:
            held = (arrived[0][-1], link, seg_column, seg_row, x_rows, qkv_bias)
            arrived[0][-1], link, seg_column, seg_row, x_rows, qkv_bias = (
                lax.optimization_barrier(held)
            )
    w_qkv, w_out, w_up, w_down = assemble(
        place,
        order_list,
        [piece for k in range(piece_count) for piece in arrived[k]],
        shapes_list,
        side,
        dp_count,
        owned,
        bounds,
    )

    x_mine = x_rows[:half]
    qkv = (mul(x_rows, w_qkv) + qkv_bias).astype(low)
    tiles = ROW // TILE
    half_tiles = tiles // 2

    def cut(value, k):
        return value[k * quarter : (k + 1) * quarter]

    context, lse, mixed = [None] * tiles, [None] * tiles, [None] * half_tiles
    row = seg_row
    for k in range(half_tiles):
        for t in (half_tiles + k, k):
            own = t < half_tiles
            context[t], lse[t], *part = attention_tile(
                qkv, w_out, seg_column, row, t, wide if own else low, 1 if own else 2
            )
            if not own:
                sent = [core_swap(value) for value in part]
                row = after(seg_row, *part)
        mixed[k] = add_low(part[0], sent)
        row = after(seg_row, mixed[k])
    came = [chip_swap(value) for value in mixed]
    def mix(mine_part, other_part):
        return add_low(mine_part, [core_swap(other_part)])

    normed_one, inverse_one, first_mine, first_other, first_norm = [], [], [], [], []
    hid_mine, hid_other, slope_mine, slope_other = [], [], [], []
    ffn_mixed = []
    up_row = bias_up[None, :]
    ready = mixed[1]
    for k in range(2):
        normed_k, inverse_k, rows_wide, *rows_low = norm_rows(
            place, mixed[k], came[k], cut(x_mine, k), after(vectors, ready), (0, 2, 3), True
        )
        normed_one.append(normed_k)
        inverse_one.append(inverse_k)
        first_norm.append(rows_wide)
        first_mine += rows_low
        rows_other = [core_swap(value) for value in rows_low]
        first_other += rows_other
        mine_part, hid, slope = feed_forward(rows_low, w_up, up_row, w_down)
        hid_mine.append(hid)
        slope_mine.append(slope)
        other_part, hid, slope = feed_forward(
            rows_other, w_up, after(up_row, mine_part), w_down
        )
        hid_other.append(hid)
        slope_other.append(slope)
        ready = other_part
        ffn_mixed.append(mix(mine_part, other_part))
    mixed = ffn_mixed
    came = [chip_swap(value) for value in mixed]
    normed_two, inverse_two, out_mine, out_other, pieces = [], [], [], [], []
    exchange = [(s, s ^ half_dp) for s in range(dp_count)]
    for k in range(2):
        normed_k, inverse_k, out_piece, out_k = norm_rows(
            place, mixed[k], came[k], first_norm[k], vectors, (1, 4, 5), False
        )
        normed_two.append(normed_k)
        inverse_two.append(inverse_k)
        out_mine.append(out_k)
        out_other.append(core_swap(out_k))
        mine = lax.ppermute(out_piece, "dp", exchange)
        pieces += [mine, chip_swap(mine)]

    output_part = in_order(place, out_mine, out_other)
    pieces = pieces + [core_swap(value) for value in pieces]
    linked = link_back(
        place,
        link,
        seg_column,
        output_cot,
        out_mine,
        normed_two,
        inverse_two,
        vectors,
        pieces,
        score_cot.shape[1],
    )
    second_grad, second_mine = list(linked[:2]), list(linked[2:4])
    sums_two, score_part = linked[4], linked[5]
    second_other = [core_swap(value) for value in second_mine]
    pre_mine, pre_other, mixed = [], [], []
    for k in range(2):
        mine_low = after(second_mine[k], other_part) if k else second_mine[k]
        mine_part, pre = feed_back(mine_low, slope_mine[k], w_up, w_down)
        pre_mine.append(pre)
        other_low = after(second_other[k], mine_part)
        other_part, pre = feed_back(other_low, slope_other[k], w_up, w_down)
        pre_other.append(pre)
        mixed.append(mix(mine_part, other_part))
    came = [chip_swap(value) for value in mixed]
    grad_down, grad_up, up_grad = feed_grads(
        hid_mine + hid_other,
        second_mine + second_other,
        first_mine + first_other,
        pre_mine + pre_other,
    )

    rotated_old = rotate_first(after(block_first, mixed[1]), basis_left, basis_right)
    ready = (vectors, grad_down, grad_up, up_grad, rotated_old, output_part)
    late_vectors, grad_down, grad_up, up_grad, rotated_old, output_part = (
        lax.optimization_barrier(ready)
    )

    first_grad, sums_one, attn_mine, attn_other, carried = [], [], [], [], None

    def attention_part(some):
        rows_grads = attn_mine + attn_other
        return attention_backward(
            qkv,
            w_out,
            seg_column,
            seg_row,
            some,
            [context[t] for t in some],
            sum([rows_grads[t] for t in some], []),
            [lse[t] for t in some],
            carried,
        )

    for k in range(2):
        grad_k, sums_k, *low_k = first_back(
            mixed[k],
            came[k],
            second_grad[k],
            normed_one[k],
            inverse_one[k],
            late_vectors if carried is None else after(late_vectors, *carried),
        )
        first_grad.append(grad_k)
        sums_one.append(sums_k)
        attn_mine.append(low_k)
        attn_other.append([core_swap(value) for value in low_k])
        if k == 0:
            attn_mine.append(None)
            carried = attention_part([0, half_tiles])
            attn_mine.pop()
    shared = pack_sums(place, sums_one, sums_two, score_part)
    shared_came = core_swap(shared)
    seg_row = after(seg_row, shared)
    carried = attention_part([1, half_tiles + 1])
    qkv_grad, grad_out, pair_bias = carried
    grad_qkv = mul(x_rows, qkv_grad, TN).astype(low)
    bounds = piece_bounds(owned, 4)
    piece_count = len(bounds) - 1
    staged = spread(
        place,
        order_list,
        [grad_qkv, grad_out, grad_up, grad_down],
        side,
        dp_count,
        owned,
        bounds,
    )

    small = add_biases(shared, shared_came, pair_bias, up_grad)
    stride = 1
    input_stage = 0
    travelling = [staged[k * dp_count] for k in range(piece_count)]
    for step in range(dp_count - 1):
        for k in range(piece_count):
            came = lax.ppermute(travelling[k], "dp", routes[k % 2])
            if step < dp_count - 2:
                local = staged[k * dp_count + step + 1]
                if step or k:
                    local = after(local, travelling[k - 1])
                if k == 0 and step in (2, 4):
                    local = after(local, small_came)
                if step in (2, 3, 4):
                    came = add_low(came, [local])
                else:
                    came = (came.astype(wide) + local.astype(wide)).astype(low)
            travelling[k] = came
        if step >= dp_count - 2:
            continue
        mark = travelling[piece_count - 1]
        if step % 2 == 0 and stride < dp_count:
            if stride > 1:
                small = after(small, mark) + small_came
            else:
                small = after(small, mark)
            pairs = [(s, s ^ stride) for s in range(dp_count)]
            small_came = lax.ppermute(small, "dp", pairs)
            stride *= 2
        if step == 0:
            late_grad = after(qkv_grad, mark)
            other_part = core_swap(mul(late_grad[half:], w_qkv, NT).astype(low))
            mine_part = mul(late_grad[:half], w_qkv, NT)
        if step == 1:
            mine_part = after(mine_part, mark)
            input_mixed = add_low(mine_part, [other_part])
            input_came = chip_swap(input_mixed)
        if step == 4:
            branch_zero = after(input_mixed, mark).astype(wide) + input_came.astype(wide)
            input_mine = (jnp.concatenate(first_grad, axis=0) + branch_zero).astype(low)
            input_other = core_swap(input_mine)
    small = small + small_came
    while stride < dp_count:
        small = small + lax.ppermute(small, "dp", [(s, s ^ stride) for s in range(dp_count)])
        stride *= 2
    bias_out, norm_out, scores, small_values = small_update(
        place, small, bias_state, norm_state, local_width, *score_cot.shape
    )
    local = [staged[(k + 1) * dp_count - 1] for k in range(piece_count)]

    owned_grad, first_new, second_new, master_new = optimize(
        travelling,
        local,
        rotated_old,
        block_master,
        block_first,
        block_second,
        basis_left,
        basis_right,
    )
    input_grad = in_order(place, [input_mine], [input_other])
    small_values, master_new = lax.optimization_barrier((small_values, master_new))
    small_values = small_values.reshape(-1)
    return (
        output_part,
        scores,
        input_grad,
        owned_grad,
        first_new,
        second_new,
        master_new,
        bias_out,
        norm_out,
        small_values,
    )


def solution(mesh):
    blocks = P(("dp", "mp"), None, None)
    rows = P("dp", None)
    return jax.shard_map(
        body,
        mesh=mesh,
        in_specs=(rows, rows, P(), P(), P(), P(), P(), P("mp", None))
        + (blocks,) * 5
        + (P(None, "mp"), P()),
        out_specs=(rows, P(), rows) + (blocks,) * 4 + (P(None, "mp"), P(), P("mp")),
        check_vma=False,
    )
```

```python
import math

import jax
import jax.numpy as jnp
from jax import lax
from jax.experimental import pallas as pl
from jax.experimental.pallas import tpu as pltpu
from jax.sharding import PartitionSpec as P

D = 1024
H = 16
HD = 64
FF = 4096
ROW = 1024
STEP = 10
TILE = 256

low = jnp.bfloat16
wide = jnp.float32
beta_one = 0.9
beta_two = 0.999
adam_eps = 1e-08
norm_eps = 1e-05
block_rate = 0.05
small_rate = 0.1
mib = 2**20

NN = (((1,), (0,)), ((), ()))
NT = (((1,), (1,)), ((), ()))
TN = (((0,), (0,)), ((), ()))


def mul(left, right, dims=NN):
    return lax.dot_general(left, right, dims, preferred_element_type=wide)


def gelu_parts(values):
    normal_cdf = 0.5 * (1.0 + lax.erf(values * 0.7071067811865476))
    slope = normal_cdf + values * jnp.exp(-0.5 * values * values) * 0.3989422804014327
    return ((values * normal_cdf).astype(low), slope)


def adam_plain(grad_now, first_old, second_old, value_old, rate_now):
    first_new = beta_one * first_old + (1.0 - beta_one) * grad_now
    second_new = beta_two * second_old + (1.0 - beta_two) * grad_now * grad_now
    step_dir = (
        first_new
        / (1.0 - beta_one**STEP)
        / (jnp.sqrt(second_new / (1.0 - beta_two**STEP)) + adam_eps)
    )
    return (first_new, second_new, value_old - rate_now * step_dir)


def after(value, *others):
    return lax.optimization_barrier((value,) + others)[0]


def ring_order(count):
    return [k for k in range(count) if k % 2 == 0] + [k for k in range(count) if k % 2][::-1]


def piece_bounds(owned, pieces):
    pieces = pieces if owned % pieces == 0 else 1
    return [owned * k // pieces for k in range(pieces + 1)]


def vmem_call(kernel, name, outs, *args, smem=0, scratch=(), flops=0, room=4):
    vmem = pl.BlockSpec(memory_space=pltpu.VMEM)
    specs = [pl.BlockSpec(memory_space=pltpu.SMEM)] * smem + [vmem] * (len(args) - smem)
    taken = sum(v.size * v.dtype.itemsize for v in args)
    given = sum(v.size * jnp.dtype(v.dtype).itemsize for v in outs)
    held = sum(
        math.prod(v.shape) * jnp.dtype(v.dtype).itemsize for v in scratch if hasattr(v, "shape")
    )
    moved = taken + given
    return pl.pallas_call(
        kernel,
        in_specs=specs,
        out_specs=[vmem] * len(outs),
        out_shape=outs,
        scratch_shapes=list(scratch),
        compiler_params=pltpu.CompilerParams(vmem_limit_bytes=given + held + room * mib),
        cost_estimate=pl.CostEstimate(flops=0, bytes_accessed=1024, transcendentals=0),
        name=name,
    )(*args)


def shaped(dtype, *shape):
    return jax.ShapeDtypeStruct(shape, dtype)


def matrix_views(refs, side):
    for ref in refs:
        for row in range(0, ref.shape[0], side):
            for column in range(0, ref.shape[1], side):
                yield ref.at[row : row + side, column : column + side]


def ring_member(place, count):
    place = lax.rem(place + 2 * count, count)
    return jnp.where(place < count // 2, 2 * place, 2 * count - 1 - 2 * place)


def each_travelling(place_ref, count, owned, bounds, first, visit):
    for k in range(len(bounds) - 1):
        sign = 1 if k % 2 == 0 else -1
        for step in range(count):
            owner = ring_member(place_ref[5] - sign * (first + step), count)
            start = owner * owned + bounds[k]
            for w in range(bounds[k + 1] - bounds[k]):
                visit(k * count + step, w, start + w)


def assemble(place, order, pieces, shapes_list, side, count, owned, bounds):
    def kernel(place_ref, order_ref, *refs):
        parts, outs, blocks = refs[: len(pieces)], refs[len(pieces) : -1], refs[-1]

        def visit(at, w, slot):
            blocks[order_ref[slot]] = parts[at][w]

        each_travelling(place_ref, count, owned, bounds, 0, visit)
        for k, view in enumerate(matrix_views(outs, side)):
            view[...] = blocks[k]

    return vmem_call(
        kernel,
        "assemble",
        [shaped(low, *shape) for shape in shapes_list],
        place,
        order,
        *pieces,
        smem=2,
        scratch=[pltpu.VMEM((count * owned, side, side), low)],
    )


def spread(place, order, matrices, side, count, owned, bounds):
    def kernel(place_ref, order_ref, *refs):
        sources, outs, blocks = refs[: len(matrices)], refs[len(matrices) : -1], refs[-1]
        for k, view in enumerate(matrix_views(sources, side)):
            blocks[k] = view[...]

        def visit(at, w, slot):
            outs[at][w] = blocks[order_ref[slot]]

        each_travelling(place_ref, count, owned, bounds, 1, visit)

    return vmem_call(
        kernel,
        "spread",
        [
            shaped(low, bounds[k + 1] - bounds[k], side, side)
            for k in range(len(bounds) - 1)
            for _ in range(count)
        ],
        place,
        order,
        *matrices,
        smem=2,
        scratch=[pltpu.VMEM((count * owned, side, side), low)],
    )


def joined(refs):
    values = [ref[...] for ref in refs]
    return values[0] if len(values) == 1 else jnp.concatenate(values, axis=0)


def add_low(left, right):
    def kernel(a_ref, *refs):
        refs[-1][...] = (a_ref[...].astype(wide) + joined(refs[:-1]).astype(wide)).astype(low)

    return vmem_call(kernel, "add_low", [shaped(low, *left.shape)], left, *right)[0]


def in_order(place, mine, other):
    rows = mine[0].shape[0]
    count = len(mine)

    def kernel(place_ref, *refs):
        out = refs[-1]
        core = place_ref[2]
        for k in range(count):
            for ref, turn in ((refs[k], core), (refs[count + k], 1 - core)):
                start = pl.multiple_of((turn * count + k) * rows, rows)
                out[pl.ds(start, rows), :] = ref[...]

    return vmem_call(
        kernel, "in_order", [shaped(low, 2 * count * rows, D)], place, *mine, *other, smem=1
    )[0]


def feed_grads(hidden, second_rows, first_rows, pre_rows):
    count, rows = len(hidden), hidden[0].shape[0]
    inner = hidden[0].shape[1]
    pieces = 3 * count + len(first_rows)

    def kernel(*refs):
        down_ref, up_ref, bias_ref, left, right = refs[pieces:]

        def fill(target, sources):
            start = 0
            for ref in sources:
                target[start : start + ref.shape[0], :] = ref[...]
                start += ref.shape[0]

        fill(left, refs[:count])
        fill(right, refs[count : 2 * count])
        down_ref[...] = mul(left[...], right[...], TN).astype(low)
        fill(left, refs[2 * count : pieces - count])
        fill(right, refs[pieces - count : pieces])
        up_ref[...] = mul(left[...], right[...], TN).astype(low)
        bias_ref[...] = jnp.sum(right[...].astype(wide), axis=0, keepdims=True)

    return vmem_call(
        kernel,
        "feed_grads",
        [shaped(low, inner, D), shaped(low, D, inner), shaped(wide, 1, inner)],
        *hidden,
        *second_rows,
        *first_rows,
        *pre_rows,
        scratch=[pltpu.VMEM((count * rows, D), low), pltpu.VMEM((count * rows, D), low)],
        flops=4 * count * rows * D * inner,
        room=12,
    )


def pair_tables(place, query_lengths, passage_lengths, pairing, score_cot, match_offset):
    queries, passages = query_lengths.shape[1], passage_lengths.shape[1]
    half = ROW // 2
    pair_scale = D ** (-0.5)

    def kernel(place_ref, ql_ref, pl_ref, pair_ref, cot_ref, offset_ref, link_ref, col_ref, row_ref):
        is_query = place_ref[0] == 1
        row = place_ref[1]
        first_core = place_ref[2] == 0
        token = lax.broadcasted_iota(jnp.int32, (1, ROW), 1)
        zero = jnp.zeros((1, ROW), jnp.int32)
        segment, start_at, length_at = zero, zero, zero
        cot = jnp.zeros((1, ROW), wide)
        start = jnp.int32(0)
        for e in range(queries):
            end = start + ql_ref[row, e]
            inside = (token >= start) & (token < end)
            chosen = pair_ref[row, e]
            before = jnp.int32(0)
            length = jnp.int32(1)
            for m in range(passages):
                span = pl_ref[row, m]
                before = before + jnp.where(m < chosen, span, 0)
                length = jnp.where(m == chosen, span, length)
            segment = jnp.where(inside, e, segment)
            start_at = jnp.where(inside, before, start_at)
            length_at = jnp.where(inside, length, length_at)
            cot = jnp.where(inside, cot_ref[row, e] * pair_scale, cot)
            start = end
        passage = zero
        start = jnp.int32(0)
        for m in range(passages):
            start = start + pl_ref[row, m]
            passage = passage + (token >= start).astype(jnp.int32)
        length_at = jnp.maximum(length_at, 1)
        target = start_at + lax.rem(offset_ref[pl.ds(row, 1), :], length_at)
        own = jnp.where(is_query, segment, passage)

        def turn(value):
            swapped = jnp.concatenate([value[:, half:], value[:, :half]], axis=1)
            return jnp.where(first_core, value, swapped)

        token = turn(token)
        target, cot, segment, own = turn(target), turn(cot), turn(segment), turn(own)
        stacked = jnp.concatenate(
            [target.astype(wide), cot, segment.astype(wide), own.astype(wide)]
            + [token.astype(wide)]
            + [jnp.zeros((3, ROW), wide)],
            axis=0,
        )
        columns = stacked.T
        col_ref[...] = columns
        row_ref[...] = own.astype(wide)
        left = jnp.where(is_query, columns[:half, 0:1], columns[:half, 4:5])
        right = jnp.where(is_query, token, target).astype(wide)
        value = jnp.where(is_query, jnp.ones_like(cot), cot)
        link_ref[...] = jnp.where(left == right, value, 0.0).astype(low)

    smem = pl.BlockSpec(memory_space=pltpu.SMEM)
    vmem = pl.BlockSpec(memory_space=pltpu.VMEM)
    return pl.pallas_call(
        kernel,
        in_specs=[smem] * 5 + [vmem],
        out_specs=[vmem] * 3,
        out_shape=[
            jax.ShapeDtypeStruct((half, ROW), low),
            jax.ShapeDtypeStruct((ROW, 8), wide),
            jax.ShapeDtypeStruct((1, ROW), wide),
        ],
        compiler_params=pltpu.CompilerParams(vmem_limit_bytes=16 * mib),
        name="pair_tables",
    )(place, query_lengths, passage_lengths, pairing, score_cot, match_offset)


def halves(value):
    top = value.astype(low)
    return (top, (value - top.astype(wide)).astype(low))


def left_parts(value):
    top, rest = halves(value)
    return jnp.concatenate([top, rest, top], axis=1)


def right_parts(value, axis=0):
    top, rest = halves(value)
    return jnp.concatenate([top, top, rest], axis=axis)


def rotate_first(blocks, left_basis, right_basis):
    count, side = blocks.shape[0], blocks.shape[1]
    group = count // (4 if count % 4 == 0 else 1)

    def kernel(m_ref, l_ref, r_ref, out_ref):
        every = range(group)
        inner = [mul(left_parts(l_ref[b].T), right_parts(m_ref[b])) for b in every]
        for b in every:
            out_ref[b] = mul(left_parts(inner[b]), right_parts(r_ref[b]))

    spec = pl.BlockSpec((group, side, side), lambda t: (t, 0, 0))
    return pl.pallas_call(
        kernel,
        grid=(count // group,),
        in_specs=[spec] * 3,
        out_specs=spec,
        out_shape=jax.ShapeDtypeStruct(blocks.shape, wide),
        compiler_params=pltpu.CompilerParams(vmem_limit_bytes=16 * mib),
        cost_estimate=pl.CostEstimate(
            flops=0, bytes_accessed=1024, transcendentals=0
        ),
        name="rotate_first",
    )(blocks, left_basis, right_basis)


def optimize(came, local, rotated_old, master, first, second, left_basis, right_basis):
    count, side = master.shape[0], master.shape[1]
    pieces = len(came)
    group = count // pieces

    def kernel(*refs):
        came_refs, refs = refs[:pieces], refs[pieces:]
        local_refs, refs = refs[:pieces], refs[pieces:]
        c_ref, w_ref, m_ref, v_ref, l_ref, r_ref, g_out, m_out, v_out, w_out = refs
        for k in range(pieces):

            @pl.when(pl.program_id(0) == k)
            def _():
                g_out[...] = came_refs[k][...].astype(wide) + local_refs[k][...].astype(wide)

        every = range(group)
        for b in every:
            m_out[b] = beta_one * m_ref[b] + (1.0 - beta_one) * g_out[b]
        inner = [mul(left_parts(l_ref[b].T), right_parts(g_out[b])) for b in every]
        turned = [mul(left_parts(inner[b]), right_parts(r_ref[b])) for b in every]
        steps = []
        for b in every:
            second_new = beta_two * v_ref[b] + (1.0 - beta_two) * turned[b] * turned[b]
            v_out[b] = second_new
            first_turned = beta_one * c_ref[b] + (1.0 - beta_one) * turned[b]
            steps.append(
                (first_turned / (1.0 - beta_one**STEP))
                / (jnp.sqrt(second_new / (1.0 - beta_two**STEP)) + adam_eps)
            )
        inner = [mul(left_parts(l_ref[b]), right_parts(steps[b])) for b in every]
        for b in every:
            back = mul(left_parts(inner[b]), right_parts(r_ref[b], 1), NT)
            w_out[b] = w_ref[b] - block_rate * back

    spec = pl.BlockSpec((group, side, side), lambda t: (t, 0, 0))
    vmem = pl.BlockSpec(memory_space=pltpu.VMEM)
    return pl.pallas_call(
        kernel,
        grid=(pieces,),
        in_specs=[vmem] * (2 * pieces) + [spec] * 6,
        out_specs=[spec] * 4,
        out_shape=[jax.ShapeDtypeStruct(master.shape, wide)] * 4,
        compiler_params=pltpu.CompilerParams(vmem_limit_bytes=20 * mib),
        cost_estimate=pl.CostEstimate(
            flops=0, bytes_accessed=1024, transcendentals=0
        ),
        name="optimize",
    )(*came, *local, rotated_old, master, first, second, left_basis, right_basis)


def head_mask(head):
    lane = lax.broadcasted_iota(jnp.int32, (1, 2 * HD), 1)
    return ((lane // HD) == head).astype(low)


def attention_tile(qkv, w_out, table, seg_row, tile, kind, pieces):
    width = qkv.shape[1] // 3
    pairs = width // (2 * HD)
    rows = qkv.shape[0]
    span = slice(tile * TILE, (tile + 1) * TILE)

    def kernel(qkv_ref, w_ref, sk_ref, sq_ref, *refs):
        ctx_ref, lse_ref, *part_refs = refs
        same = sk_ref[:, 3:4] == sq_ref[:, span]
        for pair in range(pairs):
            place = pair * 2 * HD
            lanes = slice(place, place + 2 * HD)
            q = qkv_ref[span, lanes] * jnp.asarray(HD**-0.5, low)
            k = qkv_ref[:, width + place : width + place + 2 * HD]
            v_t = qkv_ref[:, 2 * width + place : 2 * width + place + 2 * HD].T
            parts = []
            for head in range(2):
                s = jnp.where(same, mul(k, q * head_mask(head), NT), -1e30)
                peak = jnp.max(s, axis=0, keepdims=True)
                e = jnp.exp(s - peak)
                total = jnp.sum(e, axis=0, keepdims=True)
                part = mul(v_t[head * HD : (head + 1) * HD], e.astype(low))
                parts.append(part * (1.0 / total))
                lse_ref[pair * 2 + head : pair * 2 + head + 1, :] = peak + jnp.log(total)
            ctx_ref[:, lanes] = jnp.concatenate(parts, axis=0).T.astype(low)
        part = mul(ctx_ref[...], w_ref[...]).astype(kind)
        size = TILE // len(part_refs)
        for k, part_ref in enumerate(part_refs):
            part_ref[...] = part[k * size : (k + 1) * size]

    return vmem_call(
        kernel,
        "attention_tile",
        [shaped(low, TILE, width), shaped(wide, 2 * pairs, TILE)]
        + [shaped(kind, TILE // pieces, D)] * pieces,
        qkv,
        w_out,
        table,
        seg_row,
        flops=16 * TILE * rows * width,
        room=8,
    )


def norm_rows(place, mixed, came, residual, vectors, which, keep):
    bias_row, gain_row, shift_row = which
    rows = mixed.shape[0]

    pieces = 2 if keep else 1

    def kernel(place_ref, a_ref, b_ref, x_ref, v_ref, normed_ref, inverse_ref, last_ref, *low_refs):
        total = a_ref[...].astype(wide) + b_ref[...].astype(wide)
        z = x_ref[...].astype(wide) + total + v_ref[bias_row : bias_row + 1, :]
        center = z - jnp.mean(z, axis=1, keepdims=True)
        inverse = lax.rsqrt(jnp.mean(center * center, axis=1, keepdims=True) + norm_eps)
        normed = center * inverse
        out = v_ref[gain_row : gain_row + 1, :] * normed + v_ref[shift_row : shift_row + 1, :]
        out_low = out.astype(low)
        for k, low_ref in enumerate(low_refs):
            low_ref[...] = out_low[k * rows // pieces : (k + 1) * rows // pieces]
        normed_ref[...] = normed
        inverse_ref[...] = inverse
        if keep:
            last_ref[...] = out
        else:
            first_chip = place_ref[3] == 0
            last_ref[...] = jnp.where(first_chip, out[: rows // 2], out[rows // 2 :]).astype(low)

    outs = [shaped(wide, rows, D), shaped(wide, rows, 1)]
    outs += [shaped(wide, rows, D) if keep else shaped(low, rows // 2, D)]
    outs += [shaped(low, rows // pieces, D)] * pieces
    return vmem_call(
        kernel,
        "norm_rows",
        outs,
        place,
        mixed,
        came,
        residual,
        vectors,
        smem=1,
        flops=20 * rows * D,
    )


def norm_back(grad_rows, norm_gain, normed, inverse):
    scaled = grad_rows * norm_gain
    first_mean = jnp.mean(scaled, axis=1, keepdims=True)
    second_mean = jnp.mean(scaled * normed, axis=1, keepdims=True)
    return inverse * (scaled - first_mean - normed * second_mean)


def column_sums(grad_z, grad_rows, normed):
    return jnp.concatenate(
        [
            jnp.sum(grad_z, axis=0, keepdims=True),
            jnp.sum(grad_rows * normed, axis=0, keepdims=True),
            jnp.sum(grad_rows, axis=0, keepdims=True),
        ],
        axis=0,
    )


def feed_forward(rows_low, w_up, bias_up, w_down):
    rows, hidden = sum(value.shape[0] for value in rows_low), w_up.shape[1]

    def kernel(up_ref, b_ref, down_ref, *refs):
        part_ref, hid_ref, slope_ref = refs[-3:]
        u = mul(joined(refs[:-3]), up_ref[...]) + b_ref[...]
        hid, slope = gelu_parts(u)
        hid_ref[...] = hid
        slope_ref[...] = slope
        part_ref[...] = mul(hid, down_ref[...]).astype(part_ref.dtype)

    return vmem_call(
        kernel,
        "feed_forward",
        [shaped(low, rows, D), shaped(low, rows, hidden), shaped(wide, rows, hidden)],
        w_up,
        bias_up,
        w_down,
        *rows_low,
        flops=4 * rows * D * hidden,
    )


def feed_back(grad_low, slope, w_up, w_down):
    rows, hidden = grad_low.shape[0], w_up.shape[1]

    def kernel(g_ref, slope_ref, up_ref, down_ref, part_ref, pre_ref):
        pre = (mul(g_ref[...], down_ref[...], NT) * slope_ref[...]).astype(low)
        pre_ref[...] = pre
        part_ref[...] = mul(pre, up_ref[...], NT).astype(part_ref.dtype)

    return vmem_call(
        kernel,
        "feed_back",
        [shaped(low, rows, D), shaped(low, rows, hidden)],
        grad_low,
        slope,
        w_up,
        w_down,
        flops=4 * rows * D * hidden,
    )


def link_back(place, link, table, cot_rows, out_rows, normed, inverse, vectors, pieces, queries):
    rows = out_rows[0].shape[0]
    count = len(out_rows)
    piece_rows = pieces[0].shape[0]

    def kernel(place_ref, link_ref, table_ref, cot_ref, *refs):
        outs, refs = refs[:count], refs[count:]
        norms, refs = refs[:count], refs[count:]
        scales, refs = refs[:count], refs[count:]
        v_ref, refs = refs[0], refs[1:]
        parts, refs = refs[: len(pieces)], refs[len(pieces) :]
        grads, refs = refs[:count], refs[count:]
        lows, refs = refs[:count], refs[count:]
        sums_ref, score_ref, partner = refs
        is_query = place_ref[0] == 1
        chip = place_ref[3]
        for k, part in enumerate(parts):
            turn = chip if k % 2 == 0 else 1 - chip
            start = (k // 2 * 2 + turn) * piece_rows
            partner[pl.ds(pl.multiple_of(start, piece_rows), piece_rows), :] = part[...]
        gain = v_ref[4:5, :]
        sums = jnp.zeros((3, D), wide)
        score = jnp.zeros((1, queries), wide)
        for k in range(count):
            span = slice(k * rows, (k + 1) * rows)
            linked = mul(link_ref[span, :], partner[...])
            token = jnp.sum(outs[k][...].astype(wide) * linked, axis=1, keepdims=True)
            kinds = lax.broadcasted_iota(jnp.int32, (1, queries), 1).astype(wide)
            hot = table_ref[span, 2:3] == kinds
            score = score + jnp.sum(jnp.where(hot, token, 0.0), axis=0, keepdims=True)
            scale = jnp.where(is_query, table_ref[span, 1:2], 1.0)
            start = pl.multiple_of(place_ref[2] * count * rows + k * rows, rows)
            grad_rows = cot_ref[pl.ds(start, rows), :].astype(wide) + scale * linked
            normed_k = norms[k][...]
            grad_z = norm_back(grad_rows, gain, normed_k, scales[k][...])
            grads[k][...] = grad_z
            lows[k][...] = grad_z.astype(low)
            sums = sums + column_sums(grad_z, grad_rows, normed_k)
        sums_ref[...] = sums
        score_ref[...] = jnp.where(is_query, score * D ** (-0.5), 0.0)

    return vmem_call(
        kernel,
        "link_back",
        [shaped(wide, rows, D)] * count
        + [shaped(low, rows, D)] * count
        + [shaped(wide, 3, D), shaped(wide, 1, queries)],
        place,
        link,
        table,
        cot_rows,
        *out_rows,
        *normed,
        *inverse,
        vectors,
        *pieces,
        smem=1,
        scratch=[pltpu.VMEM((ROW, D), low)],
        flops=2 * count * rows * ROW * D,
    )


def first_back(mixed, came, second_grad, normed, inverse, vectors):
    rows = mixed.shape[0]

    def kernel(a_ref, b_ref, g_ref, n_ref, i_ref, v_ref, grad_ref, sums_ref, *low_refs):
        total = a_ref[...].astype(wide) + b_ref[...].astype(wide)
        grad_rows = g_ref[...] + total
        normed_k = n_ref[...]
        grad_z = norm_back(grad_rows, v_ref[2:3, :], normed_k, i_ref[...])
        grad_ref[...] = grad_z
        grad_low = grad_z.astype(low)
        for k, low_ref in enumerate(low_refs):
            low_ref[...] = grad_low[k * rows // 2 : (k + 1) * rows // 2]
        sums_ref[...] = column_sums(grad_z, grad_rows, normed_k)

    return vmem_call(
        kernel,
        "first_back",
        [shaped(wide, rows, D), shaped(wide, 3, D)] + [shaped(low, rows // 2, D)] * 2,
        mixed,
        came,
        second_grad,
        normed,
        inverse,
        vectors,
        flops=20 * rows * D,
    )


def attention_backward(qkv, w_out, table, seg_row, tiles, contexts, rows_grads, lses, carried):
    width = qkv.shape[1] // 3
    pairs = width // (2 * HD)
    rows = qkv.shape[0]
    count = len(tiles)
    last = carried is not None
    before = [t for t in range(rows // TILE) if t not in tiles]

    def kernel(qkv_ref, w_ref, sk_ref, sq_ref, *refs):
        ctx_refs, refs = refs[:count], refs[count:]
        g_refs, refs = refs[: len(rows_grads)], refs[len(rows_grads) :]
        lse_refs, refs = refs[:count], refs[count:]
        if last:
            (old_q, old_k, old_v, old_w, old_b), refs = refs[:5], refs[5:]
            out_ref, wgrad_ref, bias_ref, ctx, grad_rows, ctx_grad, lse, gk, gv, sums = refs
        else:
            out_ref, gk, gv, wgrad_ref, sums, ctx, grad_rows, ctx_grad, lse = refs
        for t in range(count):
            span = slice(t * TILE, (t + 1) * TILE)
            ctx[span, :] = ctx_refs[t][...]
            lse[:, span] = lse_refs[t][...]
        for k, ref in enumerate(g_refs):
            grad_rows[k * ref.shape[0] : (k + 1) * ref.shape[0], :] = ref[...]
        ctx_grad[...] = mul(grad_rows[...], w_ref[...], NT).astype(low)
        wgrad = mul(ctx[...], grad_rows[...], TN)
        if last:
            wgrad_ref[...] = (wgrad + old_w[...]).astype(low)
            gk[...] = old_k[...]
            gv[...] = old_v[...]
            sums[...] = old_b[...]
        else:
            wgrad_ref[...] = wgrad
            gk[...] = jnp.zeros_like(gk)
            gv[...] = jnp.zeros_like(gv)
            sums[...] = jnp.zeros_like(sums)

        def step(index, carry):
            tile = tiles[0] + (tiles[1] - tiles[0]) * index
            span = pl.ds(pl.multiple_of(tile * TILE, TILE), TILE)
            here = pl.ds(pl.multiple_of(index * TILE, TILE), TILE)
            same = sk_ref[:, 3:4] == sq_ref[:, span]
            for pair in range(pairs):
                place = pair * 2 * HD
                lanes = slice(place, place + 2 * HD)
                q = qkv_ref[span, lanes] * jnp.asarray(HD**-0.5, low)
                k = qkv_ref[:, width + place : width + place + 2 * HD]
                v = qkv_ref[:, 2 * width + place : 2 * width + place + 2 * HD]
                k_t = k.T
                grad = ctx_grad[here, lanes]
                dots = (grad.astype(wide) * ctx[here, lanes].astype(wide)).T
                parts = []
                for head in range(2):
                    mask = head_mask(head)
                    row = pair * 2 + head
                    q_head = q * mask
                    grad_head = grad * mask
                    features = slice(head * HD, (head + 1) * HD)
                    delta = jnp.sum(dots[features], axis=0, keepdims=True)
                    s = jnp.where(same, mul(k, q_head, NT), -1e30)
                    p = jnp.exp(s - lse[row : row + 1, here])
                    gs = (p * (mul(v, grad_head, NT) - delta)).astype(low)
                    gv[:, lanes] += mul(p.astype(low), grad_head)
                    gk[:, lanes] += mul(gs, q_head)
                    parts.append(mul(k_t[features], gs))
                gq = (jnp.concatenate(parts, axis=0).T * HD**-0.5).astype(low)
                out_ref[span if last else here, lanes] = gq
                sums[:, lanes] += jnp.sum(gq.astype(wide), axis=0, keepdims=True)
            return carry

        lax.fori_loop(0, count, step, 0)
        if last:
            for k, t in enumerate(before):
                out_ref[t * TILE : (t + 1) * TILE, :width] = old_q[k * TILE : (k + 1) * TILE, :]
            out_ref[:, width : 2 * width] = gk[...].astype(low)
            gv_low = gv[...].astype(low)
            out_ref[:, 2 * width :] = gv_low
            bias_ref[:, :width] = sums[...]
            bias_ref[:, width:] = jnp.sum(gv_low.astype(wide), axis=0, keepdims=True)

    scratch = [
        pltpu.VMEM((count * TILE, width), low),
        pltpu.VMEM((count * TILE, D), low),
        pltpu.VMEM((count * TILE, width), low),
        pltpu.VMEM((2 * pairs, count * TILE), wide),
    ]
    if last:
        outs = [shaped(low, rows, 3 * width), shaped(low, width, D), shaped(wide, 1, 2 * width)]
        scratch += [pltpu.VMEM((rows, width), wide)] * 2 + [pltpu.VMEM((1, width), wide)]
    else:
        outs = [shaped(low, count * TILE, width)] + [shaped(wide, rows, width)] * 2
        outs += [shaped(wide, width, D), shaped(wide, 1, width)]
    return vmem_call(
        kernel,
        "attention_backward",
        outs,
        qkv,
        w_out,
        table,
        seg_row,
        *contexts,
        *rows_grads,
        *lses,
        *(carried or []),
        scratch=scratch,
        flops=40 * rows * count * TILE * width,
        room=10,
    )


def pack_sums(place, sums_one, sums_two, score_part):
    queries = score_part.shape[1]

    def kernel(place_ref, one_a, one_b, two_ref, score_ref, out_ref):
        one = one_a[...] + one_b[...]
        two = two_ref[...]
        out_ref[0:1, :] = one[0:1]
        out_ref[1:2, :] = two[0:1]
        out_ref[2:4, :] = one[1:3]
        out_ref[4:6, :] = two[1:3]
        lane = lax.broadcasted_iota(jnp.int32, (1, D), 1)
        first = place_ref[1] * queries
        row = jnp.zeros((1, D), wide)
        score = score_ref[...]
        for e in range(queries):
            row = jnp.where(lane == first + e, score[:, e : e + 1], row)
        out_ref[6:7, :] = row
        out_ref[7:8, :] = jnp.zeros((1, D), wide)

    return vmem_call(
        kernel, "pack_sums", [shaped(wide, 8, D)], place, *sums_one, sums_two, score_part, smem=1
    )[0]


def add_biases(shared, came, pair_bias, up_grad):
    def kernel(a_ref, b_ref, pair_ref, up_ref, out_ref):
        out_ref[0:8, :] = a_ref[...] + b_ref[...]
        zero = jnp.zeros((1, D - pair_ref.shape[1]), wide)
        out_ref[8:9, :] = jnp.concatenate([pair_ref[...], zero], axis=1)
        out_ref[9:10, :] = up_ref[...]
        out_ref[10:16, :] = jnp.zeros((6, D), wide)

    return vmem_call(
        kernel, "add_biases", [shaped(wide, 16, D)], shared, came, pair_bias, up_grad
    )[0]


def small_update(place, total, bias_state, norm_state, local_width, packs, queries):
    bias_count = bias_state.shape[1]
    hidden = bias_count - 2 * local_width
    unit = D // 2
    pieces = norm_state.shape[1] * 2 // 4

    def kernel(place_ref, g_ref, bias_ref, norm_ref, bias_out, norm_out, score_out, value_out, new):
        bias_grad = jnp.concatenate([g_ref[8:9, : 2 * local_width], g_ref[9:10, :hidden]], axis=1)
        first, second, value = adam_plain(
            bias_grad, bias_ref[1:2], bias_ref[2:3], bias_ref[0:1], small_rate
        )
        bias_out[0:1, :] = bias_grad
        bias_out[1:2, :] = first
        bias_out[2:3, :] = second
        for k in range(bias_count // unit):
            value_out[k : k + 1, :] = value[:, k * unit : (k + 1) * unit]
        norm_grad = g_ref[0:6, :]
        first, second, value = adam_plain(
            norm_grad, norm_ref[1], norm_ref[2], norm_ref[0], small_rate
        )
        norm_out[0] = norm_grad
        norm_out[1] = first
        norm_out[2] = second
        for row in range(6):
            for side in range(2):
                new[2 * row + side] = value[row : row + 1, side * unit : (side + 1) * unit]
        start = place_ref[4] * pieces
        for k in range(pieces):
            at = bias_count // unit + k
            value_out[at : at + 1, :] = new[start + k]
        for pack in range(packs):
            score_out[pack : pack + 1, :] = g_ref[6:7, pack * queries : (pack + 1) * queries]

    bias_out, norm_out, scores, values = vmem_call(
        kernel,
        "small_update",
        [
            shaped(wide, 3, bias_count),
            shaped(wide, *norm_state.shape),
            shaped(wide, packs, queries),
            shaped(wide, bias_count // unit + pieces, unit),
        ],
        place,
        total,
        bias_state,
        norm_state,
        smem=1,
        scratch=[pltpu.VMEM((12, 1, unit), wide)],
    )
    return bias_out, norm_out, scores, values


def body(
    layer_input,
    output_cot,
    score_cot,
    query_lengths,
    passage_lengths,
    pairing,
    match_offset,
    block_order,
    block_master,
    block_first,
    block_second,
    basis_left,
    basis_right,
    bias_state,
    norm_state,
):
    mp_count = lax.axis_size("mp")
    dp_count = lax.axis_size("dp")
    dp_index = lax.axis_index("dp")
    mp_index = lax.axis_index("mp")
    core, chip = mp_index % 2, mp_index // 2
    half_dp = dp_count // 2
    is_query = dp_index < half_dp
    table_row = dp_index % half_dp
    side = block_master.shape[1]
    owned = block_master.shape[0]
    local_width = H // mp_count * HD
    hidden_local = FF // mp_count
    shapes_list = [(D, 3 * local_width), (local_width, D), (D, hidden_local), (hidden_local, D)]
    half, quarter = ROW // 2, ROW // 4

    core_pairs = [(s, s ^ 1) for s in range(mp_count)]
    chip_pairs = [(s, s ^ 2) for s in range(mp_count)]

    def core_swap(value):
        return lax.ppermute(value, "mp", core_pairs)

    def chip_swap(value):
        return lax.ppermute(value, "mp", chip_pairs)

    ring = ring_order(dp_count)
    ahead = [(ring[k], ring[(k + 1) % dp_count]) for k in range(dp_count)]
    routes = [ahead, [(b, a) for a, b in ahead]]
    bounds = piece_bounds(owned, 4)
    piece_count = len(bounds) - 1
    order_list = block_order[0]
    ring_place = jnp.where(dp_index % 2 == 0, dp_index // 2, dp_count - 1 - dp_index // 2)
    place = jnp.stack(
        [is_query.astype(jnp.int32), table_row, core, chip, mp_index, ring_place]
    )
    link, seg_column, seg_row = pair_tables(
        place, query_lengths, passage_lengths, pairing, score_cot, match_offset
    )

    bias_now = bias_state[0]
    bias_query = bias_now[:local_width]
    bias_value = bias_now[local_width : 2 * local_width]
    bias_up = bias_now[2 * local_width :]
    qkv_bias = jnp.concatenate([bias_query, jnp.zeros_like(bias_query), bias_value])
    vectors = norm_state[0]

    x_rows = in_order(
        place, [layer_input[:half]], [layer_input[half:]]
    )

    master_low = block_master.astype(low)
    arrived = [[master_low[bounds[k] : bounds[k + 1]]] for k in range(piece_count)]
    for step in range(dp_count - 1):
        for k in range(piece_count):
            arrived[k].append(lax.ppermute(arrived[k][-1], "dp", routes[k % 2]))
        if step == 1:
            held = (arrived[0][-1], link, seg_column, seg_row, x_rows, qkv_bias)
            arrived[0][-1], link, seg_column, seg_row, x_rows, qkv_bias = (
                lax.optimization_barrier(held)
            )
    w_qkv, w_out, w_up, w_down = assemble(
        place,
        order_list,
        [piece for k in range(piece_count) for piece in arrived[k]],
        shapes_list,
        side,
        dp_count,
        owned,
        bounds,
    )

    x_mine = x_rows[:half]
    qkv = (mul(x_rows, w_qkv) + qkv_bias).astype(low)
    tiles = ROW // TILE
    half_tiles = tiles // 2

    def cut(value, k):
        return value[k * quarter : (k + 1) * quarter]

    context, lse, mixed = [None] * tiles, [None] * tiles, [None] * half_tiles
    row = seg_row
    for k in range(half_tiles):
        for t in (half_tiles + k, k):
            own = t < half_tiles
            context[t], lse[t], *part = attention_tile(
                qkv, w_out, seg_column, row, t, wide if own else low, 1 if own else 2 + 2 * k
            )
            if not own:
                sent = [core_swap(value) for value in part]
                row = after(seg_row, *part)
        mixed[k] = add_low(part[0], sent)
        row = after(seg_row, mixed[k])
    came = [chip_swap(value) for value in mixed]
    def mix(mine_part, other_part):
        return add_low(mine_part, [core_swap(other_part)])

    normed_one, inverse_one, first_mine, first_other, first_norm = [], [], [], [], []
    hid_mine, hid_other, slope_mine, slope_other = [], [], [], []
    ffn_mixed = []
    up_row = bias_up[None, :]
    ready = mixed[1]
    for k in range(2):
        normed_k, inverse_k, rows_wide, *rows_low = norm_rows(
            place, mixed[k], came[k], cut(x_mine, k), after(vectors, ready), (0, 2, 3), True
        )
        normed_one.append(normed_k)
        inverse_one.append(inverse_k)
        first_norm.append(rows_wide)
        first_mine += rows_low
        rows_other = [core_swap(value) for value in rows_low]
        first_other += rows_other
        mine_part, hid, slope = feed_forward(rows_low, w_up, up_row, w_down)
        hid_mine.append(hid)
        slope_mine.append(slope)
        other_part, hid, slope = feed_forward(
            rows_other, w_up, after(up_row, mine_part), w_down
        )
        hid_other.append(hid)
        slope_other.append(slope)
        ready = other_part
        ffn_mixed.append(mix(mine_part, other_part))
    mixed = ffn_mixed
    came = [chip_swap(value) for value in mixed]
    normed_two, inverse_two, out_mine, out_other, pieces = [], [], [], [], []
    exchange = [(s, s ^ half_dp) for s in range(dp_count)]
    for k in range(2):
        normed_k, inverse_k, out_piece, out_k = norm_rows(
            place, mixed[k], came[k], first_norm[k], vectors, (1, 4, 5), False
        )
        normed_two.append(normed_k)
        inverse_two.append(inverse_k)
        out_mine.append(out_k)
        out_other.append(core_swap(out_k))
        mine = lax.ppermute(out_piece, "dp", exchange)
        pieces += [mine, chip_swap(mine)]

    output_part = in_order(place, out_mine, out_other)
    pieces = pieces + [core_swap(value) for value in pieces]
    linked = link_back(
        place,
        link,
        seg_column,
        output_cot,
        out_mine,
        normed_two,
        inverse_two,
        vectors,
        pieces,
        score_cot.shape[1],
    )
    second_grad, second_mine = list(linked[:2]), list(linked[2:4])
    sums_two, score_part = linked[4], linked[5]
    second_other = [core_swap(value) for value in second_mine]
    pre_mine, pre_other, mixed = [], [], []
    for k in range(2):
        mine_low = after(second_mine[k], other_part) if k else second_mine[k]
        mine_part, pre = feed_back(mine_low, slope_mine[k], w_up, w_down)
        pre_mine.append(pre)
        other_low = after(second_other[k], mine_part)
        other_part, pre = feed_back(other_low, slope_other[k], w_up, w_down)
        pre_other.append(pre)
        mixed.append(mix(mine_part, other_part))
    came = [chip_swap(value) for value in mixed]
    grad_down, grad_up, up_grad = feed_grads(
        hid_mine + hid_other,
        second_mine + second_other,
        first_mine + first_other,
        pre_mine + pre_other,
    )

    rotated_old = rotate_first(after(block_first, mixed[1]), basis_left, basis_right)
    ready = (vectors, grad_down, grad_up, up_grad, rotated_old, output_part)
    late_vectors, grad_down, grad_up, up_grad, rotated_old, output_part = (
        lax.optimization_barrier(ready)
    )

    first_grad, sums_one, attn_mine, attn_other, carried = [], [], [], [], None

    def attention_part(some):
        rows_grads = attn_mine + attn_other
        return attention_backward(
            qkv,
            w_out,
            seg_column,
            seg_row,
            some,
            [context[t] for t in some],
            sum([rows_grads[t] for t in some], []),
            [lse[t] for t in some],
            carried,
        )

    for k in range(2):
        grad_k, sums_k, *low_k = first_back(
            mixed[k],
            came[k],
            second_grad[k],
            normed_one[k],
            inverse_one[k],
            late_vectors if carried is None else after(late_vectors, *carried),
        )
        first_grad.append(grad_k)
        sums_one.append(sums_k)
        attn_mine.append(low_k)
        attn_other.append([core_swap(value) for value in low_k])
        if k == 0:
            attn_mine.append(None)
            carried = attention_part([0, half_tiles])
            attn_mine.pop()
    shared = pack_sums(place, sums_one, sums_two, score_part)
    shared_came = core_swap(shared)
    seg_row = after(seg_row, shared)
    carried = attention_part([1, half_tiles + 1])
    qkv_grad, grad_out, pair_bias = carried
    grad_qkv = mul(x_rows, qkv_grad, TN).astype(low)
    bounds = piece_bounds(owned, 4)
    piece_count = len(bounds) - 1
    staged = spread(
        place,
        order_list,
        [grad_qkv, grad_out, grad_up, grad_down],
        side,
        dp_count,
        owned,
        bounds,
    )

    small = add_biases(shared, shared_came, pair_bias, up_grad)
    stride = 1
    input_stage = 0
    travelling = [staged[k * dp_count] for k in range(piece_count)]
    for step in range(dp_count - 1):
        for k in range(piece_count):
            came = lax.ppermute(travelling[k], "dp", routes[k % 2])
            if step < dp_count - 2:
                local = staged[k * dp_count + step + 1]
                if step or k:
                    local = after(local, travelling[k - 1])
                if k == 0 and step in (2, 4):
                    local = after(local, small_came)
                if step in (2, 3, 4):
                    came = add_low(came, [local])
                else:
                    came = (came.astype(wide) + local.astype(wide)).astype(low)
            travelling[k] = came
        if step >= dp_count - 2:
            continue
        mark = travelling[piece_count - 1]
        if step % 2 == 0 and stride < dp_count:
            if stride > 1:
                small = after(small, mark) + small_came
            else:
                small = after(small, mark)
            pairs = [(s, s ^ stride) for s in range(dp_count)]
            small_came = lax.ppermute(small, "dp", pairs)
            stride *= 2
        if step == 0:
            late_grad = after(qkv_grad, mark)
            other_part = core_swap(mul(late_grad[half:], w_qkv, NT).astype(low))
            mine_part = mul(late_grad[:half], w_qkv, NT)
        if step == 1:
            mine_part = after(mine_part, mark)
            input_mixed = add_low(mine_part, [other_part])
            input_came = chip_swap(input_mixed)
        if step == 4:
            branch_zero = after(input_mixed, mark).astype(wide) + input_came.astype(wide)
            input_mine = (jnp.concatenate(first_grad, axis=0) + branch_zero).astype(low)
            input_other = core_swap(input_mine)
    small = small + small_came
    while stride < dp_count:
        small = small + lax.ppermute(small, "dp", [(s, s ^ stride) for s in range(dp_count)])
        stride *= 2
    bias_out, norm_out, scores, small_values = small_update(
        place, small, bias_state, norm_state, local_width, *score_cot.shape
    )
    local = [staged[(k + 1) * dp_count - 1] for k in range(piece_count)]

    input_grad = in_order(place, [input_mine], [input_other])
    travelling[0] = after(travelling[0], input_grad)
    owned_grad, first_new, second_new, master_new = optimize(
        travelling,
        local,
        rotated_old,
        block_master,
        block_first,
        block_second,
        basis_left,
        basis_right,
    )
    small_values, master_new = lax.optimization_barrier((small_values, master_new))
    small_values = small_values.reshape(-1)
    return (
        output_part,
        scores,
        input_grad,
        owned_grad,
        first_new,
        second_new,
        master_new,
        bias_out,
        norm_out,
        small_values,
    )


def solution(mesh):
    blocks = P(("dp", "mp"), None, None)
    rows = P("dp", None)
    return jax.shard_map(
        body,
        mesh=mesh,
        in_specs=(rows, rows, P(), P(), P(), P(), P(), P("mp", None))
        + (blocks,) * 5
        + (P(None, "mp"), P()),
        out_specs=(rows, P(), rows) + (blocks,) * 4 + (P(None, "mp"), P(), P("mp")),
        check_vma=False,
    )
```

```python
import math

import jax
import jax.numpy as jnp
from jax import lax
from jax.experimental import pallas as pl
from jax.experimental.pallas import tpu as pltpu
from jax.sharding import PartitionSpec as P

D = 1024
H = 16
HD = 64
FF = 4096
ROW = 1024
STEP = 10
TILE = 256

low = jnp.bfloat16
wide = jnp.float32
beta_one = 0.9
beta_two = 0.999
adam_eps = 1e-08
norm_eps = 1e-05
block_rate = 0.05
small_rate = 0.1
mib = 2**20

NN = (((1,), (0,)), ((), ()))
NT = (((1,), (1,)), ((), ()))
TN = (((0,), (0,)), ((), ()))


def mul(left, right, dims=NN):
    return lax.dot_general(left, right, dims, preferred_element_type=wide)


def gelu_parts(values):
    normal_cdf = 0.5 * (1.0 + lax.erf(values * 0.7071067811865476))
    slope = normal_cdf + values * jnp.exp(-0.5 * values * values) * 0.3989422804014327
    return ((values * normal_cdf).astype(low), slope)


def adam_plain(grad_now, first_old, second_old, value_old, rate_now):
    first_new = beta_one * first_old + (1.0 - beta_one) * grad_now
    second_new = beta_two * second_old + (1.0 - beta_two) * grad_now * grad_now
    step_dir = (
        first_new
        / (1.0 - beta_one**STEP)
        / (jnp.sqrt(second_new / (1.0 - beta_two**STEP)) + adam_eps)
    )
    return (first_new, second_new, value_old - rate_now * step_dir)


def after(value, *others):
    return lax.optimization_barrier((value,) + others)[0]


def ring_order(count):
    return [k for k in range(count) if k % 2 == 0] + [k for k in range(count) if k % 2][::-1]


def piece_bounds(owned, pieces):
    pieces = pieces if owned % pieces == 0 else 1
    return [owned * k // pieces for k in range(pieces + 1)]


def vmem_call(kernel, name, outs, *args, smem=0, scratch=(), flops=0, room=4):
    vmem = pl.BlockSpec(memory_space=pltpu.VMEM)
    specs = [pl.BlockSpec(memory_space=pltpu.SMEM)] * smem + [vmem] * (len(args) - smem)
    taken = sum(v.size * v.dtype.itemsize for v in args)
    given = sum(v.size * jnp.dtype(v.dtype).itemsize for v in outs)
    held = sum(
        math.prod(v.shape) * jnp.dtype(v.dtype).itemsize for v in scratch if hasattr(v, "shape")
    )
    moved = taken + given
    return pl.pallas_call(
        kernel,
        in_specs=specs,
        out_specs=[vmem] * len(outs),
        out_shape=outs,
        scratch_shapes=list(scratch),
        compiler_params=pltpu.CompilerParams(vmem_limit_bytes=given + held + room * mib),
        cost_estimate=pl.CostEstimate(flops=0, bytes_accessed=1024, transcendentals=0),
        name=name,
    )(*args)


def shaped(dtype, *shape):
    return jax.ShapeDtypeStruct(shape, dtype)


def matrix_views(refs, side):
    for ref in refs:
        for row in range(0, ref.shape[0], side):
            for column in range(0, ref.shape[1], side):
                yield ref.at[row : row + side, column : column + side]


def ring_member(place, count):
    place = lax.rem(place + 2 * count, count)
    return jnp.where(place < count // 2, 2 * place, 2 * count - 1 - 2 * place)


def each_travelling(place_ref, count, owned, bounds, first, visit):
    for k in range(len(bounds) - 1):
        sign = 1 if k % 2 == 0 else -1
        for step in range(count):
            owner = ring_member(place_ref[5] - sign * (first + step), count)
            start = owner * owned + bounds[k]
            for w in range(bounds[k + 1] - bounds[k]):
                visit(k * count + step, w, start + w)


def assemble(place, order, pieces, shapes_list, side, count, owned, bounds):
    def kernel(place_ref, order_ref, *refs):
        parts, outs, blocks = refs[: len(pieces)], refs[len(pieces) : -1], refs[-1]

        def visit(at, w, slot):
            blocks[order_ref[slot]] = parts[at][w]

        each_travelling(place_ref, count, owned, bounds, 0, visit)
        for k, view in enumerate(matrix_views(outs, side)):
            view[...] = blocks[k]

    return vmem_call(
        kernel,
        "assemble",
        [shaped(low, *shape) for shape in shapes_list],
        place,
        order,
        *pieces,
        smem=2,
        scratch=[pltpu.VMEM((count * owned, side, side), low)],
    )


def spread(place, order, matrices, side, count, owned, bounds):
    def kernel(place_ref, order_ref, *refs):
        sources, outs, blocks = refs[: len(matrices)], refs[len(matrices) : -1], refs[-1]
        for k, view in enumerate(matrix_views(sources, side)):
            blocks[k] = view[...]

        def visit(at, w, slot):
            outs[at][w] = blocks[order_ref[slot]]

        each_travelling(place_ref, count, owned, bounds, 1, visit)

    return vmem_call(
        kernel,
        "spread",
        [
            shaped(low, bounds[k + 1] - bounds[k], side, side)
            for k in range(len(bounds) - 1)
            for _ in range(count)
        ],
        place,
        order,
        *matrices,
        smem=2,
        scratch=[pltpu.VMEM((count * owned, side, side), low)],
    )


def joined(refs):
    values = [ref[...] for ref in refs]
    return values[0] if len(values) == 1 else jnp.concatenate(values, axis=0)


def add_low(left, right):
    def kernel(a_ref, *refs):
        refs[-1][...] = (a_ref[...].astype(wide) + joined(refs[:-1]).astype(wide)).astype(low)

    return vmem_call(kernel, "add_low", [shaped(low, *left.shape)], left, *right)[0]


def in_order(place, mine, other):
    rows = mine[0].shape[0]
    count = len(mine)

    def kernel(place_ref, *refs):
        out = refs[-1]
        core = place_ref[2]
        for k in range(count):
            for ref, turn in ((refs[k], core), (refs[count + k], 1 - core)):
                start = pl.multiple_of((turn * count + k) * rows, rows)
                out[pl.ds(start, rows), :] = ref[...]

    return vmem_call(
        kernel, "in_order", [shaped(low, 2 * count * rows, D)], place, *mine, *other, smem=1
    )[0]


def feed_grads(hidden, second_rows, first_rows, pre_rows):
    count, rows = len(hidden), hidden[0].shape[0]
    inner = hidden[0].shape[1]
    pieces = 3 * count + len(first_rows)

    def kernel(*refs):
        down_ref, up_ref, bias_ref, left, right = refs[pieces:]

        def fill(target, sources):
            start = 0
            for ref in sources:
                target[start : start + ref.shape[0], :] = ref[...]
                start += ref.shape[0]

        fill(left, refs[:count])
        fill(right, refs[count : 2 * count])
        down_ref[...] = mul(left[...], right[...], TN).astype(low)
        fill(left, refs[2 * count : pieces - count])
        fill(right, refs[pieces - count : pieces])
        up_ref[...] = mul(left[...], right[...], TN).astype(low)
        bias_ref[...] = jnp.sum(right[...].astype(wide), axis=0, keepdims=True)

    return vmem_call(
        kernel,
        "feed_grads",
        [shaped(low, inner, D), shaped(low, D, inner), shaped(wide, 1, inner)],
        *hidden,
        *second_rows,
        *first_rows,
        *pre_rows,
        scratch=[pltpu.VMEM((count * rows, D), low), pltpu.VMEM((count * rows, D), low)],
        flops=4 * count * rows * D * inner,
        room=12,
    )


def pair_tables(place, query_lengths, passage_lengths, pairing, score_cot, match_offset):
    queries, passages = query_lengths.shape[1], passage_lengths.shape[1]
    half = ROW // 2
    pair_scale = D ** (-0.5)

    def kernel(place_ref, ql_ref, pl_ref, pair_ref, cot_ref, offset_ref, link_ref, col_ref, row_ref):
        is_query = place_ref[0] == 1
        row = place_ref[1]
        first_core = place_ref[2] == 0
        token = lax.broadcasted_iota(jnp.int32, (1, ROW), 1)
        zero = jnp.zeros((1, ROW), jnp.int32)
        segment, start_at, length_at = zero, zero, zero
        cot = jnp.zeros((1, ROW), wide)
        start = jnp.int32(0)
        for e in range(queries):
            end = start + ql_ref[row, e]
            inside = (token >= start) & (token < end)
            chosen = pair_ref[row, e]
            before = jnp.int32(0)
            length = jnp.int32(1)
            for m in range(passages):
                span = pl_ref[row, m]
                before = before + jnp.where(m < chosen, span, 0)
                length = jnp.where(m == chosen, span, length)
            segment = jnp.where(inside, e, segment)
            start_at = jnp.where(inside, before, start_at)
            length_at = jnp.where(inside, length, length_at)
            cot = jnp.where(inside, cot_ref[row, e] * pair_scale, cot)
            start = end
        passage = zero
        start = jnp.int32(0)
        for m in range(passages):
            start = start + pl_ref[row, m]
            passage = passage + (token >= start).astype(jnp.int32)
        length_at = jnp.maximum(length_at, 1)
        target = start_at + lax.rem(offset_ref[pl.ds(row, 1), :], length_at)
        own = jnp.where(is_query, segment, passage)

        def turn(value):
            swapped = jnp.concatenate([value[:, half:], value[:, :half]], axis=1)
            return jnp.where(first_core, value, swapped)

        token = turn(token)
        target, cot, segment, own = turn(target), turn(cot), turn(segment), turn(own)
        stacked = jnp.concatenate(
            [target.astype(wide), cot, segment.astype(wide), own.astype(wide)]
            + [token.astype(wide)]
            + [jnp.zeros((3, ROW), wide)],
            axis=0,
        )
        columns = stacked.T
        col_ref[...] = columns
        row_ref[...] = own.astype(wide)
        left = jnp.where(is_query, columns[:half, 0:1], columns[:half, 4:5])
        right = jnp.where(is_query, token, target).astype(wide)
        value = jnp.where(is_query, jnp.ones_like(cot), cot)
        link_ref[...] = jnp.where(left == right, value, 0.0).astype(low)

    smem = pl.BlockSpec(memory_space=pltpu.SMEM)
    vmem = pl.BlockSpec(memory_space=pltpu.VMEM)
    return pl.pallas_call(
        kernel,
        in_specs=[smem] * 5 + [vmem],
        out_specs=[vmem] * 3,
        out_shape=[
            jax.ShapeDtypeStruct((half, ROW), low),
            jax.ShapeDtypeStruct((ROW, 8), wide),
            jax.ShapeDtypeStruct((1, ROW), wide),
        ],
        compiler_params=pltpu.CompilerParams(vmem_limit_bytes=16 * mib),
        name="pair_tables",
    )(place, query_lengths, passage_lengths, pairing, score_cot, match_offset)


def halves(value):
    top = value.astype(low)
    return (top, (value - top.astype(wide)).astype(low))


def left_parts(value):
    top, rest = halves(value)
    return jnp.concatenate([top, rest, top], axis=1)


def right_parts(value, axis=0):
    top, rest = halves(value)
    return jnp.concatenate([top, top, rest], axis=axis)


def rotate_first(blocks, left_basis, right_basis):
    count, side = blocks.shape[0], blocks.shape[1]
    group = count // (4 if count % 4 == 0 else 1)

    def kernel(m_ref, l_ref, r_ref, out_ref):
        every = range(group)
        inner = [mul(left_parts(l_ref[b].T), right_parts(m_ref[b])) for b in every]
        for b in every:
            out_ref[b] = mul(left_parts(inner[b]), right_parts(r_ref[b]))

    spec = pl.BlockSpec((group, side, side), lambda t: (t, 0, 0))
    return pl.pallas_call(
        kernel,
        grid=(count // group,),
        in_specs=[spec] * 3,
        out_specs=spec,
        out_shape=jax.ShapeDtypeStruct(blocks.shape, wide),
        compiler_params=pltpu.CompilerParams(vmem_limit_bytes=16 * mib),
        cost_estimate=pl.CostEstimate(
            flops=0, bytes_accessed=1024, transcendentals=0
        ),
        name="rotate_first",
    )(blocks, left_basis, right_basis)


def optimize(came, local, rotated_old, master, first, second, left_basis, right_basis):
    count, side = master.shape[0], master.shape[1]
    pieces = len(came)
    group = count // pieces

    def kernel(*refs):
        came_refs, refs = refs[:pieces], refs[pieces:]
        local_refs, refs = refs[:pieces], refs[pieces:]
        c_ref, w_ref, m_ref, v_ref, l_ref, r_ref, g_out, m_out, v_out, w_out = refs
        for k in range(pieces):

            @pl.when(pl.program_id(0) == k)
            def _():
                g_out[...] = came_refs[k][...].astype(wide) + local_refs[k][...].astype(wide)

        every = range(group)
        for b in every:
            m_out[b] = beta_one * m_ref[b] + (1.0 - beta_one) * g_out[b]
        inner = [mul(left_parts(l_ref[b].T), right_parts(g_out[b])) for b in every]
        turned = [mul(left_parts(inner[b]), right_parts(r_ref[b])) for b in every]
        steps = []
        for b in every:
            second_new = beta_two * v_ref[b] + (1.0 - beta_two) * turned[b] * turned[b]
            v_out[b] = second_new
            first_turned = beta_one * c_ref[b] + (1.0 - beta_one) * turned[b]
            steps.append(
                (first_turned / (1.0 - beta_one**STEP))
                / (jnp.sqrt(second_new / (1.0 - beta_two**STEP)) + adam_eps)
            )
        inner = [mul(left_parts(l_ref[b]), right_parts(steps[b])) for b in every]
        for b in every:
            back = mul(left_parts(inner[b]), right_parts(r_ref[b], 1), NT)
            w_out[b] = w_ref[b] - block_rate * back

    spec = pl.BlockSpec((group, side, side), lambda t: (t, 0, 0))
    vmem = pl.BlockSpec(memory_space=pltpu.VMEM)
    return pl.pallas_call(
        kernel,
        grid=(pieces,),
        in_specs=[vmem] * (2 * pieces) + [spec] * 6,
        out_specs=[spec] * 4,
        out_shape=[jax.ShapeDtypeStruct(master.shape, wide)] * 4,
        compiler_params=pltpu.CompilerParams(vmem_limit_bytes=20 * mib),
        cost_estimate=pl.CostEstimate(
            flops=0, bytes_accessed=1024, transcendentals=0
        ),
        name="optimize",
    )(*came, *local, rotated_old, master, first, second, left_basis, right_basis)


def head_mask(head):
    lane = lax.broadcasted_iota(jnp.int32, (1, 2 * HD), 1)
    return ((lane // HD) == head).astype(low)


def attention_tile(qkv, w_out, table, seg_row, tile, kind, pieces):
    width = qkv.shape[1] // 3
    pairs = width // (2 * HD)
    rows = qkv.shape[0]
    span = slice(tile * TILE, (tile + 1) * TILE)

    def kernel(qkv_ref, w_ref, sk_ref, sq_ref, *refs):
        ctx_ref, lse_ref, *part_refs = refs
        same = sk_ref[:, 3:4] == sq_ref[:, span]
        for pair in range(pairs):
            place = pair * 2 * HD
            lanes = slice(place, place + 2 * HD)
            q = qkv_ref[span, lanes] * jnp.asarray(HD**-0.5, low)
            k = qkv_ref[:, width + place : width + place + 2 * HD]
            v_t = qkv_ref[:, 2 * width + place : 2 * width + place + 2 * HD].T
            parts = []
            for head in range(2):
                s = jnp.where(same, mul(k, q * head_mask(head), NT), -1e30)
                peak = jnp.max(s, axis=0, keepdims=True)
                e = jnp.exp(s - peak)
                total = jnp.sum(e, axis=0, keepdims=True)
                part = mul(v_t[head * HD : (head + 1) * HD], e.astype(low))
                parts.append(part * (1.0 / total))
                lse_ref[pair * 2 + head : pair * 2 + head + 1, :] = peak + jnp.log(total)
            ctx_ref[:, lanes] = jnp.concatenate(parts, axis=0).T.astype(low)
        part = mul(ctx_ref[...], w_ref[...]).astype(kind)
        size = TILE // len(part_refs)
        for k, part_ref in enumerate(part_refs):
            part_ref[...] = part[k * size : (k + 1) * size]

    return vmem_call(
        kernel,
        "attention_tile",
        [shaped(low, TILE, width), shaped(wide, 2 * pairs, TILE)]
        + [shaped(kind, TILE // pieces, D)] * pieces,
        qkv,
        w_out,
        table,
        seg_row,
        flops=16 * TILE * rows * width,
        room=8,
    )


def norm_rows(place, mixed, came, residual, vectors, which, keep):
    bias_row, gain_row, shift_row = which
    rows = mixed.shape[0]

    pieces = 2 if keep else 1

    def kernel(place_ref, a_ref, b_ref, x_ref, v_ref, normed_ref, inverse_ref, last_ref, *low_refs):
        total = a_ref[...].astype(wide) + b_ref[...].astype(wide)
        z = x_ref[...].astype(wide) + total + v_ref[bias_row : bias_row + 1, :]
        center = z - jnp.mean(z, axis=1, keepdims=True)
        inverse = lax.rsqrt(jnp.mean(center * center, axis=1, keepdims=True) + norm_eps)
        normed = center * inverse
        out = v_ref[gain_row : gain_row + 1, :] * normed + v_ref[shift_row : shift_row + 1, :]
        out_low = out.astype(low)
        for k, low_ref in enumerate(low_refs):
            low_ref[...] = out_low[k * rows // pieces : (k + 1) * rows // pieces]
        normed_ref[...] = normed
        inverse_ref[...] = inverse
        if keep:
            last_ref[...] = out
        else:
            first_chip = place_ref[3] == 0
            last_ref[...] = jnp.where(first_chip, out[: rows // 2], out[rows // 2 :]).astype(low)

    outs = [shaped(wide, rows, D), shaped(wide, rows, 1)]
    outs += [shaped(wide, rows, D) if keep else shaped(low, rows // 2, D)]
    outs += [shaped(low, rows // pieces, D)] * pieces
    return vmem_call(
        kernel,
        "norm_rows",
        outs,
        place,
        mixed,
        came,
        residual,
        vectors,
        smem=1,
        flops=20 * rows * D,
    )


def norm_back(grad_rows, norm_gain, normed, inverse):
    scaled = grad_rows * norm_gain
    first_mean = jnp.mean(scaled, axis=1, keepdims=True)
    second_mean = jnp.mean(scaled * normed, axis=1, keepdims=True)
    return inverse * (scaled - first_mean - normed * second_mean)


def column_sums(grad_z, grad_rows, normed):
    return jnp.concatenate(
        [
            jnp.sum(grad_z, axis=0, keepdims=True),
            jnp.sum(grad_rows * normed, axis=0, keepdims=True),
            jnp.sum(grad_rows, axis=0, keepdims=True),
        ],
        axis=0,
    )


def feed_forward(rows_low, w_up, bias_up, w_down):
    rows, hidden = sum(value.shape[0] for value in rows_low), w_up.shape[1]

    def kernel(up_ref, b_ref, down_ref, *refs):
        part_ref, hid_ref, slope_ref = refs[-3:]
        u = mul(joined(refs[:-3]), up_ref[...]) + b_ref[...]
        hid, slope = gelu_parts(u)
        hid_ref[...] = hid
        slope_ref[...] = slope
        part_ref[...] = mul(hid, down_ref[...]).astype(part_ref.dtype)

    return vmem_call(
        kernel,
        "feed_forward",
        [shaped(low, rows, D), shaped(low, rows, hidden), shaped(wide, rows, hidden)],
        w_up,
        bias_up,
        w_down,
        *rows_low,
        flops=4 * rows * D * hidden,
    )


def feed_back(grad_low, slope, w_up, w_down):
    rows, hidden = grad_low.shape[0], w_up.shape[1]

    def kernel(g_ref, slope_ref, up_ref, down_ref, part_ref, pre_ref):
        pre = (mul(g_ref[...], down_ref[...], NT) * slope_ref[...]).astype(low)
        pre_ref[...] = pre
        part_ref[...] = mul(pre, up_ref[...], NT).astype(part_ref.dtype)

    return vmem_call(
        kernel,
        "feed_back",
        [shaped(low, rows, D), shaped(low, rows, hidden)],
        grad_low,
        slope,
        w_up,
        w_down,
        flops=4 * rows * D * hidden,
    )


def link_back(place, link, table, cot_rows, out_rows, normed, inverse, vectors, pieces, queries):
    rows = out_rows[0].shape[0]
    count = len(out_rows)
    piece_rows = pieces[0].shape[0]

    def kernel(place_ref, link_ref, table_ref, cot_ref, *refs):
        outs, refs = refs[:count], refs[count:]
        norms, refs = refs[:count], refs[count:]
        scales, refs = refs[:count], refs[count:]
        v_ref, refs = refs[0], refs[1:]
        parts, refs = refs[: len(pieces)], refs[len(pieces) :]
        grads, refs = refs[:count], refs[count:]
        lows, refs = refs[:count], refs[count:]
        sums_ref, score_ref, partner = refs
        is_query = place_ref[0] == 1
        chip = place_ref[3]
        for k, part in enumerate(parts):
            turn = chip if k % 2 == 0 else 1 - chip
            start = (k // 2 * 2 + turn) * piece_rows
            partner[pl.ds(pl.multiple_of(start, piece_rows), piece_rows), :] = part[...]
        gain = v_ref[4:5, :]
        sums = jnp.zeros((3, D), wide)
        score = jnp.zeros((1, queries), wide)
        for k in range(count):
            span = slice(k * rows, (k + 1) * rows)
            linked = mul(link_ref[span, :], partner[...])
            token = jnp.sum(outs[k][...].astype(wide) * linked, axis=1, keepdims=True)
            kinds = lax.broadcasted_iota(jnp.int32, (1, queries), 1).astype(wide)
            hot = table_ref[span, 2:3] == kinds
            score = score + jnp.sum(jnp.where(hot, token, 0.0), axis=0, keepdims=True)
            scale = jnp.where(is_query, table_ref[span, 1:2], 1.0)
            start = pl.multiple_of(place_ref[2] * count * rows + k * rows, rows)
            grad_rows = cot_ref[pl.ds(start, rows), :].astype(wide) + scale * linked
            normed_k = norms[k][...]
            grad_z = norm_back(grad_rows, gain, normed_k, scales[k][...])
            grads[k][...] = grad_z
            lows[k][...] = grad_z.astype(low)
            sums = sums + column_sums(grad_z, grad_rows, normed_k)
        sums_ref[...] = sums
        score_ref[...] = jnp.where(is_query, score * D ** (-0.5), 0.0)

    return vmem_call(
        kernel,
        "link_back",
        [shaped(wide, rows, D)] * count
        + [shaped(low, rows, D)] * count
        + [shaped(wide, 3, D), shaped(wide, 1, queries)],
        place,
        link,
        table,
        cot_rows,
        *out_rows,
        *normed,
        *inverse,
        vectors,
        *pieces,
        smem=1,
        scratch=[pltpu.VMEM((ROW, D), low)],
        flops=2 * count * rows * ROW * D,
    )


def first_back(mixed, came, second_grad, normed, inverse, vectors):
    rows = mixed.shape[0]

    def kernel(a_ref, b_ref, g_ref, n_ref, i_ref, v_ref, grad_ref, sums_ref, *low_refs):
        total = a_ref[...].astype(wide) + b_ref[...].astype(wide)
        grad_rows = g_ref[...] + total
        normed_k = n_ref[...]
        grad_z = norm_back(grad_rows, v_ref[2:3, :], normed_k, i_ref[...])
        grad_ref[...] = grad_z
        grad_low = grad_z.astype(low)
        for k, low_ref in enumerate(low_refs):
            low_ref[...] = grad_low[k * rows // 2 : (k + 1) * rows // 2]
        sums_ref[...] = column_sums(grad_z, grad_rows, normed_k)

    return vmem_call(
        kernel,
        "first_back",
        [shaped(wide, rows, D), shaped(wide, 3, D)] + [shaped(low, rows // 2, D)] * 2,
        mixed,
        came,
        second_grad,
        normed,
        inverse,
        vectors,
        flops=20 * rows * D,
    )


def attention_backward(qkv, w_out, table, seg_row, tiles, contexts, rows_grads, lses, carried):
    width = qkv.shape[1] // 3
    pairs = width // (2 * HD)
    rows = qkv.shape[0]
    count = len(tiles)
    last = carried is not None
    before = [t for t in range(rows // TILE) if t not in tiles]

    def kernel(qkv_ref, w_ref, sk_ref, sq_ref, *refs):
        ctx_refs, refs = refs[:count], refs[count:]
        g_refs, refs = refs[: len(rows_grads)], refs[len(rows_grads) :]
        lse_refs, refs = refs[:count], refs[count:]
        if last:
            (old_q, old_k, old_v, old_w, old_b), refs = refs[:5], refs[5:]
            out_ref, wgrad_ref, bias_ref, ctx, grad_rows, ctx_grad, lse, gk, gv, sums = refs
        else:
            out_ref, gk, gv, wgrad_ref, sums, ctx, grad_rows, ctx_grad, lse = refs
        for t in range(count):
            span = slice(t * TILE, (t + 1) * TILE)
            ctx[span, :] = ctx_refs[t][...]
            lse[:, span] = lse_refs[t][...]
        for k, ref in enumerate(g_refs):
            grad_rows[k * ref.shape[0] : (k + 1) * ref.shape[0], :] = ref[...]
        ctx_grad[...] = mul(grad_rows[...], w_ref[...], NT).astype(low)
        wgrad = mul(ctx[...], grad_rows[...], TN)
        if last:
            wgrad_ref[...] = (wgrad + old_w[...]).astype(low)
            gk[...] = old_k[...]
            gv[...] = old_v[...]
            sums[...] = old_b[...]
        else:
            wgrad_ref[...] = wgrad
            gk[...] = jnp.zeros_like(gk)
            gv[...] = jnp.zeros_like(gv)
            sums[...] = jnp.zeros_like(sums)

        def step(index, carry):
            tile = tiles[0] + (tiles[1] - tiles[0]) * index
            span = pl.ds(pl.multiple_of(tile * TILE, TILE), TILE)
            here = pl.ds(pl.multiple_of(index * TILE, TILE), TILE)
            same = sk_ref[:, 3:4] == sq_ref[:, span]
            for pair in range(pairs):
                place = pair * 2 * HD
                lanes = slice(place, place + 2 * HD)
                q = qkv_ref[span, lanes] * jnp.asarray(HD**-0.5, low)
                k = qkv_ref[:, width + place : width + place + 2 * HD]
                v = qkv_ref[:, 2 * width + place : 2 * width + place + 2 * HD]
                k_t = k.T
                grad = ctx_grad[here, lanes]
                dots = (grad.astype(wide) * ctx[here, lanes].astype(wide)).T
                parts = []
                for head in range(2):
                    mask = head_mask(head)
                    row = pair * 2 + head
                    q_head = q * mask
                    grad_head = grad * mask
                    features = slice(head * HD, (head + 1) * HD)
                    delta = jnp.sum(dots[features], axis=0, keepdims=True)
                    s = jnp.where(same, mul(k, q_head, NT), -1e30)
                    p = jnp.exp(s - lse[row : row + 1, here])
                    gs = (p * (mul(v, grad_head, NT) - delta)).astype(low)
                    gv[:, lanes] += mul(p.astype(low), grad_head)
                    gk[:, lanes] += mul(gs, q_head)
                    parts.append(mul(k_t[features], gs))
                gq = (jnp.concatenate(parts, axis=0).T * HD**-0.5).astype(low)
                out_ref[span if last else here, lanes] = gq
                sums[:, lanes] += jnp.sum(gq.astype(wide), axis=0, keepdims=True)
            return carry

        lax.fori_loop(0, count, step, 0)
        if last:
            for k, t in enumerate(before):
                out_ref[t * TILE : (t + 1) * TILE, :width] = old_q[k * TILE : (k + 1) * TILE, :]
            out_ref[:, width : 2 * width] = gk[...].astype(low)
            gv_low = gv[...].astype(low)
            out_ref[:, 2 * width :] = gv_low
            bias_ref[:, :width] = sums[...]
            bias_ref[:, width:] = jnp.sum(gv_low.astype(wide), axis=0, keepdims=True)

    scratch = [
        pltpu.VMEM((count * TILE, width), low),
        pltpu.VMEM((count * TILE, D), low),
        pltpu.VMEM((count * TILE, width), low),
        pltpu.VMEM((2 * pairs, count * TILE), wide),
    ]
    if last:
        outs = [shaped(low, rows, 3 * width), shaped(low, width, D), shaped(wide, 1, 2 * width)]
        scratch += [pltpu.VMEM((rows, width), wide)] * 2 + [pltpu.VMEM((1, width), wide)]
    else:
        outs = [shaped(low, count * TILE, width)] + [shaped(wide, rows, width)] * 2
        outs += [shaped(wide, width, D), shaped(wide, 1, width)]
    return vmem_call(
        kernel,
        "attention_backward",
        outs,
        qkv,
        w_out,
        table,
        seg_row,
        *contexts,
        *rows_grads,
        *lses,
        *(carried or []),
        scratch=scratch,
        flops=40 * rows * count * TILE * width,
        room=10,
    )


def pack_sums(place, sums_one, sums_two, score_part):
    queries = score_part.shape[1]

    def kernel(place_ref, one_a, one_b, two_ref, score_ref, out_ref):
        one = one_a[...] + one_b[...]
        two = two_ref[...]
        out_ref[0:1, :] = one[0:1]
        out_ref[1:2, :] = two[0:1]
        out_ref[2:4, :] = one[1:3]
        out_ref[4:6, :] = two[1:3]
        lane = lax.broadcasted_iota(jnp.int32, (1, D), 1)
        first = place_ref[1] * queries
        row = jnp.zeros((1, D), wide)
        score = score_ref[...]
        for e in range(queries):
            row = jnp.where(lane == first + e, score[:, e : e + 1], row)
        out_ref[6:7, :] = row
        out_ref[7:8, :] = jnp.zeros((1, D), wide)

    return vmem_call(
        kernel, "pack_sums", [shaped(wide, 8, D)], place, *sums_one, sums_two, score_part, smem=1
    )[0]


def add_biases(shared, came, pair_bias, up_grad):
    def kernel(a_ref, b_ref, pair_ref, up_ref, out_ref):
        out_ref[0:8, :] = a_ref[...] + b_ref[...]
        zero = jnp.zeros((1, D - pair_ref.shape[1]), wide)
        out_ref[8:9, :] = jnp.concatenate([pair_ref[...], zero], axis=1)
        out_ref[9:10, :] = up_ref[...]
        out_ref[10:16, :] = jnp.zeros((6, D), wide)

    return vmem_call(
        kernel, "add_biases", [shaped(wide, 16, D)], shared, came, pair_bias, up_grad
    )[0]


def small_update(place, total, bias_state, norm_state, local_width, packs, queries):
    bias_count = bias_state.shape[1]
    hidden = bias_count - 2 * local_width
    unit = D // 2
    pieces = norm_state.shape[1] * 2 // 4

    def kernel(place_ref, g_ref, bias_ref, norm_ref, bias_out, norm_out, score_out, value_out, new):
        bias_grad = jnp.concatenate([g_ref[8:9, : 2 * local_width], g_ref[9:10, :hidden]], axis=1)
        first, second, value = adam_plain(
            bias_grad, bias_ref[1:2], bias_ref[2:3], bias_ref[0:1], small_rate
        )
        bias_out[0:1, :] = bias_grad
        bias_out[1:2, :] = first
        bias_out[2:3, :] = second
        for k in range(bias_count // unit):
            value_out[k : k + 1, :] = value[:, k * unit : (k + 1) * unit]
        norm_grad = g_ref[0:6, :]
        first, second, value = adam_plain(
            norm_grad, norm_ref[1], norm_ref[2], norm_ref[0], small_rate
        )
        norm_out[0] = norm_grad
        norm_out[1] = first
        norm_out[2] = second
        for row in range(6):
            for side in range(2):
                new[2 * row + side] = value[row : row + 1, side * unit : (side + 1) * unit]
        start = place_ref[4] * pieces
        for k in range(pieces):
            at = bias_count // unit + k
            value_out[at : at + 1, :] = new[start + k]
        for pack in range(packs):
            score_out[pack : pack + 1, :] = g_ref[6:7, pack * queries : (pack + 1) * queries]

    bias_out, norm_out, scores, values = vmem_call(
        kernel,
        "small_update",
        [
            shaped(wide, 3, bias_count),
            shaped(wide, *norm_state.shape),
            shaped(wide, packs, queries),
            shaped(wide, bias_count // unit + pieces, unit),
        ],
        place,
        total,
        bias_state,
        norm_state,
        smem=1,
        scratch=[pltpu.VMEM((12, 1, unit), wide)],
    )
    return bias_out, norm_out, scores, values


def body(
    layer_input,
    output_cot,
    score_cot,
    query_lengths,
    passage_lengths,
    pairing,
    match_offset,
    block_order,
    block_master,
    block_first,
    block_second,
    basis_left,
    basis_right,
    bias_state,
    norm_state,
):
    mp_count = lax.axis_size("mp")
    dp_count = lax.axis_size("dp")
    dp_index = lax.axis_index("dp")
    mp_index = lax.axis_index("mp")
    core, chip = mp_index % 2, mp_index // 2
    half_dp = dp_count // 2
    is_query = dp_index < half_dp
    table_row = dp_index % half_dp
    side = block_master.shape[1]
    owned = block_master.shape[0]
    local_width = H // mp_count * HD
    hidden_local = FF // mp_count
    shapes_list = [(D, 3 * local_width), (local_width, D), (D, hidden_local), (hidden_local, D)]
    half, quarter = ROW // 2, ROW // 4

    core_pairs = [(s, s ^ 1) for s in range(mp_count)]
    chip_pairs = [(s, s ^ 2) for s in range(mp_count)]

    def core_swap(value):
        return lax.ppermute(value, "mp", core_pairs)

    def chip_swap(value):
        return lax.ppermute(value, "mp", chip_pairs)

    ring = ring_order(dp_count)
    ahead = [(ring[k], ring[(k + 1) % dp_count]) for k in range(dp_count)]
    routes = [ahead, [(b, a) for a, b in ahead]]
    bounds = piece_bounds(owned, 4)
    piece_count = len(bounds) - 1
    order_list = block_order[0]
    ring_place = jnp.where(dp_index % 2 == 0, dp_index // 2, dp_count - 1 - dp_index // 2)
    place = jnp.stack(
        [is_query.astype(jnp.int32), table_row, core, chip, mp_index, ring_place]
    )
    link, seg_column, seg_row = pair_tables(
        place, query_lengths, passage_lengths, pairing, score_cot, match_offset
    )

    bias_now = bias_state[0]
    bias_query = bias_now[:local_width]
    bias_value = bias_now[local_width : 2 * local_width]
    bias_up = bias_now[2 * local_width :]
    qkv_bias = jnp.concatenate([bias_query, jnp.zeros_like(bias_query), bias_value])
    vectors = norm_state[0]

    x_rows = in_order(
        place, [layer_input[:half]], [layer_input[half:]]
    )

    master_low = block_master.astype(low)
    arrived = [[master_low[bounds[k] : bounds[k + 1]]] for k in range(piece_count)]
    for step in range(dp_count - 1):
        for k in range(piece_count):
            arrived[k].append(lax.ppermute(arrived[k][-1], "dp", routes[k % 2]))
        if step == 1:
            held = (arrived[0][-1], link, seg_column, seg_row, x_rows, qkv_bias)
            arrived[0][-1], link, seg_column, seg_row, x_rows, qkv_bias = (
                lax.optimization_barrier(held)
            )
    w_qkv, w_out, w_up, w_down = assemble(
        place,
        order_list,
        [piece for k in range(piece_count) for piece in arrived[k]],
        shapes_list,
        side,
        dp_count,
        owned,
        bounds,
    )

    x_mine = x_rows[:half]
    qkv = (mul(x_rows, w_qkv) + qkv_bias).astype(low)
    tiles = ROW // TILE
    half_tiles = tiles // 2

    def cut(value, k):
        return value[k * quarter : (k + 1) * quarter]

    context, lse, mixed = [None] * tiles, [None] * tiles, [None] * half_tiles
    row = seg_row
    for k in range(half_tiles):
        for t in (half_tiles + k, k):
            own = t < half_tiles
            context[t], lse[t], *part = attention_tile(
                qkv, w_out, seg_column, row, t, wide if own else low, 1 if own else 2 + 2 * k
            )
            if not own:
                sent = [core_swap(value) for value in part]
                row = after(seg_row, *part)
        mixed[k] = add_low(part[0], sent)
        row = after(seg_row, mixed[k])
    came = [chip_swap(value) for value in mixed]
    def mix(mine_part, other_part):
        return add_low(mine_part, [core_swap(other_part)])

    normed_one, inverse_one, first_mine, first_other, first_norm = [], [], [], [], []
    hid_mine, hid_other, slope_mine, slope_other = [], [], [], []
    ffn_mixed = []
    up_row = bias_up[None, :]
    ready = mixed[1]
    for k in range(2):
        normed_k, inverse_k, rows_wide, *rows_low = norm_rows(
            place, mixed[k], came[k], cut(x_mine, k), after(vectors, ready), (0, 2, 3), True
        )
        normed_one.append(normed_k)
        inverse_one.append(inverse_k)
        first_norm.append(rows_wide)
        first_mine += rows_low
        rows_other = [core_swap(value) for value in rows_low]
        first_other += rows_other
        mine_part, hid, slope = feed_forward(rows_low, w_up, up_row, w_down)
        hid_mine.append(hid)
        slope_mine.append(slope)
        other_part, hid, slope = feed_forward(
            rows_other, w_up, after(up_row, mine_part), w_down
        )
        hid_other.append(hid)
        slope_other.append(slope)
        ready = other_part
        ffn_mixed.append(mix(mine_part, other_part))
    mixed = ffn_mixed
    came = [chip_swap(value) for value in mixed]
    normed_two, inverse_two, out_mine, out_other, pieces = [], [], [], [], []
    exchange = [(s, s ^ half_dp) for s in range(dp_count)]
    for k in range(2):
        normed_k, inverse_k, out_piece, out_k = norm_rows(
            place, mixed[k], came[k], first_norm[k], vectors, (1, 4, 5), False
        )
        normed_two.append(normed_k)
        inverse_two.append(inverse_k)
        out_mine.append(out_k)
        out_other.append(core_swap(out_k))
        mine = lax.ppermute(out_piece, "dp", exchange)
        pieces += [mine, chip_swap(mine)]

    output_part = in_order(place, out_mine, out_other)
    pieces = pieces + [core_swap(value) for value in pieces]
    linked = link_back(
        place,
        link,
        seg_column,
        output_cot,
        out_mine,
        normed_two,
        inverse_two,
        vectors,
        pieces,
        score_cot.shape[1],
    )
    second_grad, second_mine = list(linked[:2]), list(linked[2:4])
    sums_two, score_part = linked[4], linked[5]
    second_other = [core_swap(value) for value in second_mine]
    pre_mine, pre_other, mixed = [], [], []
    for k in range(2):
        mine_low = after(second_mine[k], other_part) if k else second_mine[k]
        mine_part, pre = feed_back(mine_low, slope_mine[k], w_up, w_down)
        pre_mine.append(pre)
        other_low = after(second_other[k], mine_part)
        other_part, pre = feed_back(other_low, slope_other[k], w_up, w_down)
        pre_other.append(pre)
        mixed.append(mix(mine_part, other_part))
    came = [chip_swap(value) for value in mixed]
    grad_down, grad_up, up_grad = feed_grads(
        hid_mine + hid_other,
        second_mine + second_other,
        first_mine + first_other,
        pre_mine + pre_other,
    )

    rotated_old = rotate_first(after(block_first, mixed[1]), basis_left, basis_right)
    ready = (vectors, grad_down, grad_up, up_grad, rotated_old, output_part)
    late_vectors, grad_down, grad_up, up_grad, rotated_old, output_part = (
        lax.optimization_barrier(ready)
    )

    first_grad, sums_one, attn_mine, attn_other, carried = [], [], [], [], None

    def attention_part(some):
        rows_grads = attn_mine + attn_other
        return attention_backward(
            qkv,
            w_out,
            seg_column,
            seg_row,
            some,
            [context[t] for t in some],
            sum([rows_grads[t] for t in some], []),
            [lse[t] for t in some],
            carried,
        )

    for k in range(2):
        grad_k, sums_k, *low_k = first_back(
            mixed[k],
            came[k],
            second_grad[k],
            normed_one[k],
            inverse_one[k],
            late_vectors if carried is None else after(late_vectors, *carried),
        )
        first_grad.append(grad_k)
        sums_one.append(sums_k)
        attn_mine.append(low_k)
        attn_other.append([core_swap(value) for value in low_k])
        if k == 0:
            attn_mine.append(None)
            carried = attention_part([0, half_tiles])
            attn_mine.pop()
    shared = pack_sums(place, sums_one, sums_two, score_part)
    shared_came = core_swap(shared)
    seg_row = after(seg_row, shared)
    carried = attention_part([1, half_tiles + 1])
    qkv_grad, grad_out, pair_bias = carried
    grad_qkv = mul(x_rows, qkv_grad, TN).astype(low)
    bounds = piece_bounds(owned, 4)
    piece_count = len(bounds) - 1
    staged = spread(
        place,
        order_list,
        [grad_qkv, grad_out, grad_up, grad_down],
        side,
        dp_count,
        owned,
        bounds,
    )

    small = add_biases(shared, shared_came, pair_bias, up_grad)
    stride = 1
    input_stage = 0
    travelling = [staged[k * dp_count] for k in range(piece_count)]
    for step in range(dp_count - 1):
        for k in range(piece_count):
            came = lax.ppermute(travelling[k], "dp", routes[k % 2])
            if step < dp_count - 2:
                local = staged[k * dp_count + step + 1]
                if step or k:
                    local = after(local, travelling[k - 1])
                if k == 0 and step in (2, 4):
                    local = after(local, small_came)
                if step in (3, 4):
                    came = add_low(came, [local])
                else:
                    came = (came.astype(wide) + local.astype(wide)).astype(low)
            travelling[k] = came
        if step >= dp_count - 2:
            continue
        mark = travelling[piece_count - 1]
        if step % 2 == 0 and stride < dp_count:
            if stride > 1:
                small = after(small, mark) + small_came
            else:
                small = after(small, mark)
            pairs = [(s, s ^ stride) for s in range(dp_count)]
            small_came = lax.ppermute(small, "dp", pairs)
            stride *= 2
        if step == 0:
            late_grad = after(qkv_grad, mark)
            other_part = core_swap(mul(late_grad[half:], w_qkv, NT).astype(low))
            mine_part = mul(late_grad[:half], w_qkv, NT)
        if step == 1:
            mine_part = after(mine_part, mark)
            input_mixed = add_low(mine_part, [other_part])
            input_came = chip_swap(input_mixed)
        if step == 4:
            branch_zero = after(input_mixed, mark).astype(wide) + input_came.astype(wide)
            input_mine = (jnp.concatenate(first_grad, axis=0) + branch_zero).astype(low)
            input_other = core_swap(input_mine)
    small = small + small_came
    while stride < dp_count:
        small = small + lax.ppermute(small, "dp", [(s, s ^ stride) for s in range(dp_count)])
        stride *= 2
    bias_out, norm_out, scores, small_values = small_update(
        place, small, bias_state, norm_state, local_width, *score_cot.shape
    )
    local = [staged[(k + 1) * dp_count - 1] for k in range(piece_count)]

    input_grad = in_order(place, [input_mine], [input_other])
    travelling[0] = after(travelling[0], input_grad)
    owned_grad, first_new, second_new, master_new = optimize(
        travelling,
        local,
        rotated_old,
        block_master,
        block_first,
        block_second,
        basis_left,
        basis_right,
    )
    small_values, master_new = lax.optimization_barrier((small_values, master_new))
    small_values = small_values.reshape(-1)
    return (
        output_part,
        scores,
        input_grad,
        owned_grad,
        first_new,
        second_new,
        master_new,
        bias_out,
        norm_out,
        small_values,
    )


def solution(mesh):
    blocks = P(("dp", "mp"), None, None)
    rows = P("dp", None)
    return jax.shard_map(
        body,
        mesh=mesh,
        in_specs=(rows, rows, P(), P(), P(), P(), P(), P("mp", None))
        + (blocks,) * 5
        + (P(None, "mp"), P()),
        out_specs=(rows, P(), rows) + (blocks,) * 4 + (P(None, "mp"), P(), P("mp")),
        check_vma=False,
    )
```

```python
import math

import jax
import jax.numpy as jnp
from jax import lax
from jax.experimental import pallas as pl
from jax.experimental.pallas import tpu as pltpu
from jax.sharding import PartitionSpec as P

D = 1024
H = 16
HD = 64
FF = 4096
ROW = 1024
STEP = 10
TILE = 256

low = jnp.bfloat16
wide = jnp.float32
beta_one = 0.9
beta_two = 0.999
adam_eps = 1e-08
norm_eps = 1e-05
block_rate = 0.05
small_rate = 0.1
mib = 2**20

NN = (((1,), (0,)), ((), ()))
NT = (((1,), (1,)), ((), ()))
TN = (((0,), (0,)), ((), ()))


def mul(left, right, dims=NN):
    return lax.dot_general(left, right, dims, preferred_element_type=wide)


def gelu_parts(values):
    normal_cdf = 0.5 * (1.0 + lax.erf(values * 0.7071067811865476))
    slope = normal_cdf + values * jnp.exp(-0.5 * values * values) * 0.3989422804014327
    return ((values * normal_cdf).astype(low), slope)


def adam_plain(grad_now, first_old, second_old, value_old, rate_now):
    first_new = beta_one * first_old + (1.0 - beta_one) * grad_now
    second_new = beta_two * second_old + (1.0 - beta_two) * grad_now * grad_now
    step_dir = (
        first_new
        / (1.0 - beta_one**STEP)
        / (jnp.sqrt(second_new / (1.0 - beta_two**STEP)) + adam_eps)
    )
    return (first_new, second_new, value_old - rate_now * step_dir)


def after(value, *others):
    return lax.optimization_barrier((value,) + others)[0]


def ring_order(count):
    return [k for k in range(count) if k % 2 == 0] + [k for k in range(count) if k % 2][::-1]


def piece_bounds(owned, pieces):
    pieces = pieces if owned % pieces == 0 else 1
    return [owned * k // pieces for k in range(pieces + 1)]


def vmem_call(kernel, name, outs, *args, smem=0, scratch=(), flops=0, room=4):
    vmem = pl.BlockSpec(memory_space=pltpu.VMEM)
    specs = [pl.BlockSpec(memory_space=pltpu.SMEM)] * smem + [vmem] * (len(args) - smem)
    taken = sum(v.size * v.dtype.itemsize for v in args)
    given = sum(v.size * jnp.dtype(v.dtype).itemsize for v in outs)
    held = sum(
        math.prod(v.shape) * jnp.dtype(v.dtype).itemsize for v in scratch if hasattr(v, "shape")
    )
    moved = taken + given
    return pl.pallas_call(
        kernel,
        in_specs=specs,
        out_specs=[vmem] * len(outs),
        out_shape=outs,
        scratch_shapes=list(scratch),
        compiler_params=pltpu.CompilerParams(vmem_limit_bytes=given + held + room * mib),
        cost_estimate=pl.CostEstimate(flops=0, bytes_accessed=1024, transcendentals=0),
        name=name,
    )(*args)


def shaped(dtype, *shape):
    return jax.ShapeDtypeStruct(shape, dtype)


def matrix_views(refs, side):
    for ref in refs:
        for row in range(0, ref.shape[0], side):
            for column in range(0, ref.shape[1], side):
                yield ref.at[row : row + side, column : column + side]


def ring_member(place, count):
    place = lax.rem(place + 2 * count, count)
    return jnp.where(place < count // 2, 2 * place, 2 * count - 1 - 2 * place)


def each_travelling(place_ref, count, owned, bounds, first, visit):
    for k in range(len(bounds) - 1):
        sign = 1 if k % 2 == 0 else -1
        for step in range(count):
            owner = ring_member(place_ref[5] - sign * (first + step), count)
            start = owner * owned + bounds[k]
            for w in range(bounds[k + 1] - bounds[k]):
                visit(k * count + step, w, start + w)


def assemble(place, order, pieces, shapes_list, side, count, owned, bounds):
    def kernel(place_ref, order_ref, *refs):
        parts, outs, blocks = refs[: len(pieces)], refs[len(pieces) : -1], refs[-1]

        def visit(at, w, slot):
            blocks[order_ref[slot]] = parts[at][w]

        each_travelling(place_ref, count, owned, bounds, 0, visit)
        for k, view in enumerate(matrix_views(outs, side)):
            view[...] = blocks[k]

    return vmem_call(
        kernel,
        "assemble",
        [shaped(low, *shape) for shape in shapes_list],
        place,
        order,
        *pieces,
        smem=2,
        scratch=[pltpu.VMEM((count * owned, side, side), low)],
    )


def spread(place, order, matrices, side, count, owned, bounds):
    def kernel(place_ref, order_ref, *refs):
        sources, outs, blocks = refs[: len(matrices)], refs[len(matrices) : -1], refs[-1]
        for k, view in enumerate(matrix_views(sources, side)):
            blocks[k] = view[...]

        def visit(at, w, slot):
            outs[at][w] = blocks[order_ref[slot]]

        each_travelling(place_ref, count, owned, bounds, 1, visit)

    return vmem_call(
        kernel,
        "spread",
        [
            shaped(low, bounds[k + 1] - bounds[k], side, side)
            for k in range(len(bounds) - 1)
            for _ in range(count)
        ],
        place,
        order,
        *matrices,
        smem=2,
        scratch=[pltpu.VMEM((count * owned, side, side), low)],
    )


def joined(refs):
    values = [ref[...] for ref in refs]
    return values[0] if len(values) == 1 else jnp.concatenate(values, axis=0)


def add_low(left, right):
    def kernel(a_ref, *refs):
        refs[-1][...] = (a_ref[...].astype(wide) + joined(refs[:-1]).astype(wide)).astype(low)

    return vmem_call(kernel, "add_low", [shaped(low, *left.shape)], left, *right)[0]


def in_order(place, mine, other):
    rows = mine[0].shape[0]
    count = len(mine)

    def kernel(place_ref, *refs):
        out = refs[-1]
        core = place_ref[2]
        for k in range(count):
            for ref, turn in ((refs[k], core), (refs[count + k], 1 - core)):
                start = pl.multiple_of((turn * count + k) * rows, rows)
                out[pl.ds(start, rows), :] = ref[...]

    return vmem_call(
        kernel, "in_order", [shaped(low, 2 * count * rows, D)], place, *mine, *other, smem=1
    )[0]


def feed_grads(hidden, second_rows, first_rows, pre_rows):
    count, rows = len(hidden), hidden[0].shape[0]
    inner = hidden[0].shape[1]
    pieces = 3 * count + len(first_rows)

    def kernel(*refs):
        down_ref, up_ref, bias_ref, left, right = refs[pieces:]

        def fill(target, sources):
            start = 0
            for ref in sources:
                target[start : start + ref.shape[0], :] = ref[...]
                start += ref.shape[0]

        fill(left, refs[:count])
        fill(right, refs[count : 2 * count])
        down_ref[...] = mul(left[...], right[...], TN).astype(low)
        fill(left, refs[2 * count : pieces - count])
        fill(right, refs[pieces - count : pieces])
        up_ref[...] = mul(left[...], right[...], TN).astype(low)
        bias_ref[...] = jnp.sum(right[...].astype(wide), axis=0, keepdims=True)

    return vmem_call(
        kernel,
        "feed_grads",
        [shaped(low, inner, D), shaped(low, D, inner), shaped(wide, 1, inner)],
        *hidden,
        *second_rows,
        *first_rows,
        *pre_rows,
        scratch=[pltpu.VMEM((count * rows, D), low), pltpu.VMEM((count * rows, D), low)],
        flops=4 * count * rows * D * inner,
        room=12,
    )


def pair_tables(place, query_lengths, passage_lengths, pairing, score_cot, match_offset):
    queries, passages = query_lengths.shape[1], passage_lengths.shape[1]
    half = ROW // 2
    pair_scale = D ** (-0.5)

    def kernel(place_ref, ql_ref, pl_ref, pair_ref, cot_ref, offset_ref, link_ref, col_ref, row_ref):
        is_query = place_ref[0] == 1
        row = place_ref[1]
        first_core = place_ref[2] == 0
        token = lax.broadcasted_iota(jnp.int32, (1, ROW), 1)
        zero = jnp.zeros((1, ROW), jnp.int32)
        segment, start_at, length_at = zero, zero, zero
        cot = jnp.zeros((1, ROW), wide)
        start = jnp.int32(0)
        for e in range(queries):
            end = start + ql_ref[row, e]
            inside = (token >= start) & (token < end)
            chosen = pair_ref[row, e]
            before = jnp.int32(0)
            length = jnp.int32(1)
            for m in range(passages):
                span = pl_ref[row, m]
                before = before + jnp.where(m < chosen, span, 0)
                length = jnp.where(m == chosen, span, length)
            segment = jnp.where(inside, e, segment)
            start_at = jnp.where(inside, before, start_at)
            length_at = jnp.where(inside, length, length_at)
            cot = jnp.where(inside, cot_ref[row, e] * pair_scale, cot)
            start = end
        passage = zero
        start = jnp.int32(0)
        for m in range(passages):
            start = start + pl_ref[row, m]
            passage = passage + (token >= start).astype(jnp.int32)
        length_at = jnp.maximum(length_at, 1)
        target = start_at + lax.rem(offset_ref[pl.ds(row, 1), :], length_at)
        own = jnp.where(is_query, segment, passage)

        def turn(value):
            swapped = jnp.concatenate([value[:, half:], value[:, :half]], axis=1)
            return jnp.where(first_core, value, swapped)

        token = turn(token)
        target, cot, segment, own = turn(target), turn(cot), turn(segment), turn(own)
        stacked = jnp.concatenate(
            [target.astype(wide), cot, segment.astype(wide), own.astype(wide)]
            + [token.astype(wide)]
            + [jnp.zeros((3, ROW), wide)],
            axis=0,
        )
        columns = stacked.T
        col_ref[...] = columns
        row_ref[...] = own.astype(wide)
        left = jnp.where(is_query, columns[:half, 0:1], columns[:half, 4:5])
        right = jnp.where(is_query, token, target).astype(wide)
        value = jnp.where(is_query, jnp.ones_like(cot), cot)
        link_ref[...] = jnp.where(left == right, value, 0.0).astype(low)

    smem = pl.BlockSpec(memory_space=pltpu.SMEM)
    vmem = pl.BlockSpec(memory_space=pltpu.VMEM)
    return pl.pallas_call(
        kernel,
        in_specs=[smem] * 5 + [vmem],
        out_specs=[vmem] * 3,
        out_shape=[
            jax.ShapeDtypeStruct((half, ROW), low),
            jax.ShapeDtypeStruct((ROW, 8), wide),
            jax.ShapeDtypeStruct((1, ROW), wide),
        ],
        compiler_params=pltpu.CompilerParams(vmem_limit_bytes=16 * mib),
        name="pair_tables",
    )(place, query_lengths, passage_lengths, pairing, score_cot, match_offset)


def halves(value):
    top = value.astype(low)
    return (top, (value - top.astype(wide)).astype(low))


def left_parts(value):
    top, rest = halves(value)
    return jnp.concatenate([top, rest, top], axis=1)


def right_parts(value, axis=0):
    top, rest = halves(value)
    return jnp.concatenate([top, top, rest], axis=axis)


def rotate_first(blocks, left_basis, right_basis):
    count, side = blocks.shape[0], blocks.shape[1]
    group = count // (4 if count % 4 == 0 else 1)

    def kernel(m_ref, l_ref, r_ref, out_ref):
        every = range(group)
        inner = [mul(left_parts(l_ref[b].T), right_parts(m_ref[b])) for b in every]
        for b in every:
            out_ref[b] = mul(left_parts(inner[b]), right_parts(r_ref[b]))

    spec = pl.BlockSpec((group, side, side), lambda t: (t, 0, 0))
    return pl.pallas_call(
        kernel,
        grid=(count // group,),
        in_specs=[spec] * 3,
        out_specs=spec,
        out_shape=jax.ShapeDtypeStruct(blocks.shape, wide),
        compiler_params=pltpu.CompilerParams(vmem_limit_bytes=16 * mib),
        cost_estimate=pl.CostEstimate(
            flops=0, bytes_accessed=1024, transcendentals=0
        ),
        name="rotate_first",
    )(blocks, left_basis, right_basis)


def optimize(came, local, rotated_old, master, first, second, left_basis, right_basis):
    count, side = master.shape[0], master.shape[1]
    pieces = len(came)
    group = count // pieces

    def kernel(*refs):
        came_refs, refs = refs[:pieces], refs[pieces:]
        local_refs, refs = refs[:pieces], refs[pieces:]
        c_ref, w_ref, m_ref, v_ref, l_ref, r_ref, g_out, m_out, v_out, w_out = refs
        for k in range(pieces):

            @pl.when(pl.program_id(0) == k)
            def _():
                g_out[...] = came_refs[k][...].astype(wide) + local_refs[k][...].astype(wide)

        every = range(group)
        for b in every:
            m_out[b] = beta_one * m_ref[b] + (1.0 - beta_one) * g_out[b]
        inner = [mul(left_parts(l_ref[b].T), right_parts(g_out[b])) for b in every]
        turned = [mul(left_parts(inner[b]), right_parts(r_ref[b])) for b in every]
        steps = []
        for b in every:
            second_new = beta_two * v_ref[b] + (1.0 - beta_two) * turned[b] * turned[b]
            v_out[b] = second_new
            first_turned = beta_one * c_ref[b] + (1.0 - beta_one) * turned[b]
            steps.append(
                (first_turned / (1.0 - beta_one**STEP))
                / (jnp.sqrt(second_new / (1.0 - beta_two**STEP)) + adam_eps)
            )
        inner = [mul(left_parts(l_ref[b]), right_parts(steps[b])) for b in every]
        for b in every:
            back = mul(left_parts(inner[b]), right_parts(r_ref[b], 1), NT)
            w_out[b] = w_ref[b] - block_rate * back

    spec = pl.BlockSpec((group, side, side), lambda t: (t, 0, 0))
    vmem = pl.BlockSpec(memory_space=pltpu.VMEM)
    return pl.pallas_call(
        kernel,
        grid=(pieces,),
        in_specs=[vmem] * (2 * pieces) + [spec] * 6,
        out_specs=[spec] * 4,
        out_shape=[jax.ShapeDtypeStruct(master.shape, wide)] * 4,
        compiler_params=pltpu.CompilerParams(vmem_limit_bytes=20 * mib),
        cost_estimate=pl.CostEstimate(
            flops=0, bytes_accessed=1024, transcendentals=0
        ),
        name="optimize",
    )(*came, *local, rotated_old, master, first, second, left_basis, right_basis)


def head_mask(head):
    lane = lax.broadcasted_iota(jnp.int32, (1, 2 * HD), 1)
    return ((lane // HD) == head).astype(low)


def attention_tile(qkv, w_out, table, seg_row, tile, kind, pieces):
    width = qkv.shape[1] // 3
    pairs = width // (2 * HD)
    rows = qkv.shape[0]
    span = slice(tile * TILE, (tile + 1) * TILE)

    def kernel(qkv_ref, w_ref, sk_ref, sq_ref, *refs):
        ctx_ref, lse_ref, *part_refs = refs
        same = sk_ref[:, 3:4] == sq_ref[:, span]
        for pair in range(pairs):
            place = pair * 2 * HD
            lanes = slice(place, place + 2 * HD)
            q = qkv_ref[span, lanes] * jnp.asarray(HD**-0.5, low)
            k = qkv_ref[:, width + place : width + place + 2 * HD]
            v_t = qkv_ref[:, 2 * width + place : 2 * width + place + 2 * HD].T
            parts = []
            for head in range(2):
                s = jnp.where(same, mul(k, q * head_mask(head), NT), -1e30)
                peak = jnp.max(s, axis=0, keepdims=True)
                e = jnp.exp(s - peak)
                total = jnp.sum(e, axis=0, keepdims=True)
                part = mul(v_t[head * HD : (head + 1) * HD], e.astype(low))
                parts.append(part * (1.0 / total))
                lse_ref[pair * 2 + head : pair * 2 + head + 1, :] = peak + jnp.log(total)
            ctx_ref[:, lanes] = jnp.concatenate(parts, axis=0).T.astype(low)
        part = mul(ctx_ref[...], w_ref[...]).astype(kind)
        size = TILE // len(part_refs)
        for k, part_ref in enumerate(part_refs):
            part_ref[...] = part[k * size : (k + 1) * size]

    return vmem_call(
        kernel,
        "attention_tile",
        [shaped(low, TILE, width), shaped(wide, 2 * pairs, TILE)]
        + [shaped(kind, TILE // pieces, D)] * pieces,
        qkv,
        w_out,
        table,
        seg_row,
        flops=16 * TILE * rows * width,
        room=8,
    )


def norm_rows(place, mixed, came, residual, vectors, which, keep):
    bias_row, gain_row, shift_row = which
    rows = mixed.shape[0]

    pieces = 2 if keep else 1

    def kernel(place_ref, a_ref, b_ref, x_ref, v_ref, normed_ref, inverse_ref, last_ref, *low_refs):
        total = a_ref[...].astype(wide) + b_ref[...].astype(wide)
        z = x_ref[...].astype(wide) + total + v_ref[bias_row : bias_row + 1, :]
        center = z - jnp.mean(z, axis=1, keepdims=True)
        inverse = lax.rsqrt(jnp.mean(center * center, axis=1, keepdims=True) + norm_eps)
        normed = center * inverse
        out = v_ref[gain_row : gain_row + 1, :] * normed + v_ref[shift_row : shift_row + 1, :]
        out_low = out.astype(low)
        for k, low_ref in enumerate(low_refs):
            low_ref[...] = out_low[k * rows // pieces : (k + 1) * rows // pieces]
        normed_ref[...] = normed
        inverse_ref[...] = inverse
        if keep:
            last_ref[...] = out
        else:
            first_chip = place_ref[3] == 0
            last_ref[...] = jnp.where(first_chip, out[: rows // 2], out[rows // 2 :]).astype(low)

    outs = [shaped(wide, rows, D), shaped(wide, rows, 1)]
    outs += [shaped(wide, rows, D) if keep else shaped(low, rows // 2, D)]
    outs += [shaped(low, rows // pieces, D)] * pieces
    return vmem_call(
        kernel,
        "norm_rows",
        outs,
        place,
        mixed,
        came,
        residual,
        vectors,
        smem=1,
        flops=20 * rows * D,
    )


def norm_back(grad_rows, norm_gain, normed, inverse):
    scaled = grad_rows * norm_gain
    first_mean = jnp.mean(scaled, axis=1, keepdims=True)
    second_mean = jnp.mean(scaled * normed, axis=1, keepdims=True)
    return inverse * (scaled - first_mean - normed * second_mean)


def column_sums(grad_z, grad_rows, normed):
    return jnp.concatenate(
        [
            jnp.sum(grad_z, axis=0, keepdims=True),
            jnp.sum(grad_rows * normed, axis=0, keepdims=True),
            jnp.sum(grad_rows, axis=0, keepdims=True),
        ],
        axis=0,
    )


def feed_forward(rows_low, w_up, bias_up, w_down):
    rows, hidden = sum(value.shape[0] for value in rows_low), w_up.shape[1]

    def kernel(up_ref, b_ref, down_ref, *refs):
        part_ref, hid_ref, slope_ref = refs[-3:]
        u = mul(joined(refs[:-3]), up_ref[...]) + b_ref[...]
        hid, slope = gelu_parts(u)
        hid_ref[...] = hid
        slope_ref[...] = slope
        part_ref[...] = mul(hid, down_ref[...]).astype(part_ref.dtype)

    return vmem_call(
        kernel,
        "feed_forward",
        [shaped(low, rows, D), shaped(low, rows, hidden), shaped(wide, rows, hidden)],
        w_up,
        bias_up,
        w_down,
        *rows_low,
        flops=4 * rows * D * hidden,
    )


def feed_back(grad_low, slope, w_up, w_down):
    rows, hidden = grad_low.shape[0], w_up.shape[1]

    def kernel(g_ref, slope_ref, up_ref, down_ref, part_ref, pre_ref):
        pre = (mul(g_ref[...], down_ref[...], NT) * slope_ref[...]).astype(low)
        pre_ref[...] = pre
        part_ref[...] = mul(pre, up_ref[...], NT).astype(part_ref.dtype)

    return vmem_call(
        kernel,
        "feed_back",
        [shaped(low, rows, D), shaped(low, rows, hidden)],
        grad_low,
        slope,
        w_up,
        w_down,
        flops=4 * rows * D * hidden,
    )


def link_back(place, link, table, cot_rows, out_rows, normed, inverse, vectors, pieces, queries):
    rows = out_rows[0].shape[0]
    count = len(out_rows)
    piece_rows = pieces[0].shape[0]

    def kernel(place_ref, link_ref, table_ref, cot_ref, *refs):
        outs, refs = refs[:count], refs[count:]
        norms, refs = refs[:count], refs[count:]
        scales, refs = refs[:count], refs[count:]
        v_ref, refs = refs[0], refs[1:]
        parts, refs = refs[: len(pieces)], refs[len(pieces) :]
        grads, refs = refs[:count], refs[count:]
        lows, refs = refs[:count], refs[count:]
        sums_ref, score_ref, partner = refs
        is_query = place_ref[0] == 1
        chip = place_ref[3]
        for k, part in enumerate(parts):
            turn = chip if k % 2 == 0 else 1 - chip
            start = (k // 2 * 2 + turn) * piece_rows
            partner[pl.ds(pl.multiple_of(start, piece_rows), piece_rows), :] = part[...]
        gain = v_ref[4:5, :]
        sums = jnp.zeros((3, D), wide)
        score = jnp.zeros((1, queries), wide)
        for k in range(count):
            span = slice(k * rows, (k + 1) * rows)
            linked = mul(link_ref[span, :], partner[...])
            token = jnp.sum(outs[k][...].astype(wide) * linked, axis=1, keepdims=True)
            kinds = lax.broadcasted_iota(jnp.int32, (1, queries), 1).astype(wide)
            hot = table_ref[span, 2:3] == kinds
            score = score + jnp.sum(jnp.where(hot, token, 0.0), axis=0, keepdims=True)
            scale = jnp.where(is_query, table_ref[span, 1:2], 1.0)
            start = pl.multiple_of(place_ref[2] * count * rows + k * rows, rows)
            grad_rows = cot_ref[pl.ds(start, rows), :].astype(wide) + scale * linked
            normed_k = norms[k][...]
            grad_z = norm_back(grad_rows, gain, normed_k, scales[k][...])
            grads[k][...] = grad_z
            lows[k][...] = grad_z.astype(low)
            sums = sums + column_sums(grad_z, grad_rows, normed_k)
        sums_ref[...] = sums
        score_ref[...] = jnp.where(is_query, score * D ** (-0.5), 0.0)

    return vmem_call(
        kernel,
        "link_back",
        [shaped(wide, rows, D)] * count
        + [shaped(low, rows, D)] * count
        + [shaped(wide, 3, D), shaped(wide, 1, queries)],
        place,
        link,
        table,
        cot_rows,
        *out_rows,
        *normed,
        *inverse,
        vectors,
        *pieces,
        smem=1,
        scratch=[pltpu.VMEM((ROW, D), low)],
        flops=2 * count * rows * ROW * D,
    )


def first_back(mixed, came, second_grad, normed, inverse, vectors):
    rows = mixed.shape[0]

    def kernel(a_ref, b_ref, g_ref, n_ref, i_ref, v_ref, grad_ref, sums_ref, *low_refs):
        total = a_ref[...].astype(wide) + b_ref[...].astype(wide)
        grad_rows = g_ref[...] + total
        normed_k = n_ref[...]
        grad_z = norm_back(grad_rows, v_ref[2:3, :], normed_k, i_ref[...])
        grad_ref[...] = grad_z
        grad_low = grad_z.astype(low)
        for k, low_ref in enumerate(low_refs):
            low_ref[...] = grad_low[k * rows // 2 : (k + 1) * rows // 2]
        sums_ref[...] = column_sums(grad_z, grad_rows, normed_k)

    return vmem_call(
        kernel,
        "first_back",
        [shaped(wide, rows, D), shaped(wide, 3, D)] + [shaped(low, rows // 2, D)] * 2,
        mixed,
        came,
        second_grad,
        normed,
        inverse,
        vectors,
        flops=20 * rows * D,
    )


def attention_backward(qkv, w_out, table, seg_row, tiles, contexts, rows_grads, lses, carried):
    width = qkv.shape[1] // 3
    pairs = width // (2 * HD)
    rows = qkv.shape[0]
    count = len(tiles)
    last = carried is not None
    before = [t for t in range(rows // TILE) if t not in tiles]

    def kernel(qkv_ref, w_ref, sk_ref, sq_ref, *refs):
        ctx_refs, refs = refs[:count], refs[count:]
        g_refs, refs = refs[: len(rows_grads)], refs[len(rows_grads) :]
        lse_refs, refs = refs[:count], refs[count:]
        if last:
            (old_q, old_k, old_v, old_w, old_b), refs = refs[:5], refs[5:]
            out_ref, wgrad_ref, bias_ref, ctx, grad_rows, ctx_grad, lse, gk, gv, sums = refs
        else:
            out_ref, gk, gv, wgrad_ref, sums, ctx, grad_rows, ctx_grad, lse = refs
        for t in range(count):
            span = slice(t * TILE, (t + 1) * TILE)
            ctx[span, :] = ctx_refs[t][...]
            lse[:, span] = lse_refs[t][...]
        for k, ref in enumerate(g_refs):
            grad_rows[k * ref.shape[0] : (k + 1) * ref.shape[0], :] = ref[...]
        ctx_grad[...] = mul(grad_rows[...], w_ref[...], NT).astype(low)
        wgrad = mul(ctx[...], grad_rows[...], TN)
        if last:
            wgrad_ref[...] = (wgrad + old_w[...]).astype(low)
            gk[...] = old_k[...]
            gv[...] = old_v[...]
            sums[...] = old_b[...]
        else:
            wgrad_ref[...] = wgrad
            gk[...] = jnp.zeros_like(gk)
            gv[...] = jnp.zeros_like(gv)
            sums[...] = jnp.zeros_like(sums)

        def step(index, carry):
            tile = tiles[0] + (tiles[1] - tiles[0]) * index
            span = pl.ds(pl.multiple_of(tile * TILE, TILE), TILE)
            here = pl.ds(pl.multiple_of(index * TILE, TILE), TILE)
            same = sk_ref[:, 3:4] == sq_ref[:, span]
            for pair in range(pairs):
                place = pair * 2 * HD
                lanes = slice(place, place + 2 * HD)
                q = qkv_ref[span, lanes] * jnp.asarray(HD**-0.5, low)
                k = qkv_ref[:, width + place : width + place + 2 * HD]
                v = qkv_ref[:, 2 * width + place : 2 * width + place + 2 * HD]
                k_t = k.T
                grad = ctx_grad[here, lanes]
                dots = (grad.astype(wide) * ctx[here, lanes].astype(wide)).T
                parts = []
                for head in range(2):
                    mask = head_mask(head)
                    row = pair * 2 + head
                    q_head = q * mask
                    grad_head = grad * mask
                    features = slice(head * HD, (head + 1) * HD)
                    delta = jnp.sum(dots[features], axis=0, keepdims=True)
                    s = jnp.where(same, mul(k, q_head, NT), -1e30)
                    p = jnp.exp(s - lse[row : row + 1, here])
                    gs = (p * (mul(v, grad_head, NT) - delta)).astype(low)
                    gv[:, lanes] += mul(p.astype(low), grad_head)
                    gk[:, lanes] += mul(gs, q_head)
                    parts.append(mul(k_t[features], gs))
                gq = (jnp.concatenate(parts, axis=0).T * HD**-0.5).astype(low)
                out_ref[span if last else here, lanes] = gq
                sums[:, lanes] += jnp.sum(gq.astype(wide), axis=0, keepdims=True)
            return carry

        lax.fori_loop(0, count, step, 0)
        if last:
            for k, t in enumerate(before):
                out_ref[t * TILE : (t + 1) * TILE, :width] = old_q[k * TILE : (k + 1) * TILE, :]
            out_ref[:, width : 2 * width] = gk[...].astype(low)
            gv_low = gv[...].astype(low)
            out_ref[:, 2 * width :] = gv_low
            bias_ref[:, :width] = sums[...]
            bias_ref[:, width:] = jnp.sum(gv_low.astype(wide), axis=0, keepdims=True)

    scratch = [
        pltpu.VMEM((count * TILE, width), low),
        pltpu.VMEM((count * TILE, D), low),
        pltpu.VMEM((count * TILE, width), low),
        pltpu.VMEM((2 * pairs, count * TILE), wide),
    ]
    if last:
        outs = [shaped(low, rows, 3 * width), shaped(low, width, D), shaped(wide, 1, 2 * width)]
        scratch += [pltpu.VMEM((rows, width), wide)] * 2 + [pltpu.VMEM((1, width), wide)]
    else:
        outs = [shaped(low, count * TILE, width)] + [shaped(wide, rows, width)] * 2
        outs += [shaped(wide, width, D), shaped(wide, 1, width)]
    return vmem_call(
        kernel,
        "attention_backward",
        outs,
        qkv,
        w_out,
        table,
        seg_row,
        *contexts,
        *rows_grads,
        *lses,
        *(carried or []),
        scratch=scratch,
        flops=40 * rows * count * TILE * width,
        room=10,
    )


def pack_sums(place, sums_one, sums_two, score_part):
    queries = score_part.shape[1]

    def kernel(place_ref, one_a, one_b, two_ref, score_ref, out_ref):
        one = one_a[...] + one_b[...]
        two = two_ref[...]
        out_ref[0:1, :] = one[0:1]
        out_ref[1:2, :] = two[0:1]
        out_ref[2:4, :] = one[1:3]
        out_ref[4:6, :] = two[1:3]
        lane = lax.broadcasted_iota(jnp.int32, (1, D), 1)
        first = place_ref[1] * queries
        row = jnp.zeros((1, D), wide)
        score = score_ref[...]
        for e in range(queries):
            row = jnp.where(lane == first + e, score[:, e : e + 1], row)
        out_ref[6:7, :] = row
        out_ref[7:8, :] = jnp.zeros((1, D), wide)

    return vmem_call(
        kernel, "pack_sums", [shaped(wide, 8, D)], place, *sums_one, sums_two, score_part, smem=1
    )[0]


def add_biases(shared, came, pair_bias, up_grad):
    def kernel(a_ref, b_ref, pair_ref, up_ref, out_ref):
        out_ref[0:8, :] = a_ref[...] + b_ref[...]
        zero = jnp.zeros((1, D - pair_ref.shape[1]), wide)
        out_ref[8:9, :] = jnp.concatenate([pair_ref[...], zero], axis=1)
        out_ref[9:10, :] = up_ref[...]
        out_ref[10:16, :] = jnp.zeros((6, D), wide)

    return vmem_call(
        kernel, "add_biases", [shaped(wide, 16, D)], shared, came, pair_bias, up_grad
    )[0]


def small_update(place, total, bias_state, norm_state, local_width, packs, queries):
    bias_count = bias_state.shape[1]
    hidden = bias_count - 2 * local_width
    unit = D // 2
    pieces = norm_state.shape[1] * 2 // 4

    def kernel(place_ref, g_ref, bias_ref, norm_ref, bias_out, norm_out, score_out, value_out, new):
        bias_grad = jnp.concatenate([g_ref[8:9, : 2 * local_width], g_ref[9:10, :hidden]], axis=1)
        first, second, value = adam_plain(
            bias_grad, bias_ref[1:2], bias_ref[2:3], bias_ref[0:1], small_rate
        )
        bias_out[0:1, :] = bias_grad
        bias_out[1:2, :] = first
        bias_out[2:3, :] = second
        for k in range(bias_count // unit):
            value_out[k : k + 1, :] = value[:, k * unit : (k + 1) * unit]
        norm_grad = g_ref[0:6, :]
        first, second, value = adam_plain(
            norm_grad, norm_ref[1], norm_ref[2], norm_ref[0], small_rate
        )
        norm_out[0] = norm_grad
        norm_out[1] = first
        norm_out[2] = second
        for row in range(6):
            for side in range(2):
                new[2 * row + side] = value[row : row + 1, side * unit : (side + 1) * unit]
        start = place_ref[4] * pieces
        for k in range(pieces):
            at = bias_count // unit + k
            value_out[at : at + 1, :] = new[start + k]
        for pack in range(packs):
            score_out[pack : pack + 1, :] = g_ref[6:7, pack * queries : (pack + 1) * queries]

    bias_out, norm_out, scores, values = vmem_call(
        kernel,
        "small_update",
        [
            shaped(wide, 3, bias_count),
            shaped(wide, *norm_state.shape),
            shaped(wide, packs, queries),
            shaped(wide, bias_count // unit + pieces, unit),
        ],
        place,
        total,
        bias_state,
        norm_state,
        smem=1,
        scratch=[pltpu.VMEM((12, 1, unit), wide)],
    )
    return bias_out, norm_out, scores, values


def body(
    layer_input,
    output_cot,
    score_cot,
    query_lengths,
    passage_lengths,
    pairing,
    match_offset,
    block_order,
    block_master,
    block_first,
    block_second,
    basis_left,
    basis_right,
    bias_state,
    norm_state,
):
    mp_count = lax.axis_size("mp")
    dp_count = lax.axis_size("dp")
    dp_index = lax.axis_index("dp")
    mp_index = lax.axis_index("mp")
    core, chip = mp_index % 2, mp_index // 2
    half_dp = dp_count // 2
    is_query = dp_index < half_dp
    table_row = dp_index % half_dp
    side = block_master.shape[1]
    owned = block_master.shape[0]
    local_width = H // mp_count * HD
    hidden_local = FF // mp_count
    shapes_list = [(D, 3 * local_width), (local_width, D), (D, hidden_local), (hidden_local, D)]
    half, quarter = ROW // 2, ROW // 4

    core_pairs = [(s, s ^ 1) for s in range(mp_count)]
    chip_pairs = [(s, s ^ 2) for s in range(mp_count)]

    def core_swap(value):
        return lax.ppermute(value, "mp", core_pairs)

    def chip_swap(value):
        return lax.ppermute(value, "mp", chip_pairs)

    ring = ring_order(dp_count)
    ahead = [(ring[k], ring[(k + 1) % dp_count]) for k in range(dp_count)]
    routes = [ahead, [(b, a) for a, b in ahead]]
    bounds = piece_bounds(owned, 4)
    piece_count = len(bounds) - 1
    order_list = block_order[0]
    ring_place = jnp.where(dp_index % 2 == 0, dp_index // 2, dp_count - 1 - dp_index // 2)
    place = jnp.stack(
        [is_query.astype(jnp.int32), table_row, core, chip, mp_index, ring_place]
    )
    link, seg_column, seg_row = pair_tables(
        place, query_lengths, passage_lengths, pairing, score_cot, match_offset
    )

    bias_now = bias_state[0]
    bias_query = bias_now[:local_width]
    bias_value = bias_now[local_width : 2 * local_width]
    bias_up = bias_now[2 * local_width :]
    qkv_bias = jnp.concatenate([bias_query, jnp.zeros_like(bias_query), bias_value])
    vectors = norm_state[0]

    x_rows = in_order(
        place, [layer_input[:half]], [layer_input[half:]]
    )

    master_low = block_master.astype(low)
    arrived = [[master_low[bounds[k] : bounds[k + 1]]] for k in range(piece_count)]
    for step in range(dp_count - 1):
        for k in range(piece_count):
            arrived[k].append(lax.ppermute(arrived[k][-1], "dp", routes[k % 2]))
        if step == 1:
            held = (arrived[0][-1], link, seg_column, seg_row, x_rows, qkv_bias)
            arrived[0][-1], link, seg_column, seg_row, x_rows, qkv_bias = (
                lax.optimization_barrier(held)
            )
    w_qkv, w_out, w_up, w_down = assemble(
        place,
        order_list,
        [piece for k in range(piece_count) for piece in arrived[k]],
        shapes_list,
        side,
        dp_count,
        owned,
        bounds,
    )

    x_mine = x_rows[:half]
    qkv = (mul(x_rows, w_qkv) + qkv_bias).astype(low)
    tiles = ROW // TILE
    half_tiles = tiles // 2

    def cut(value, k):
        return value[k * quarter : (k + 1) * quarter]

    context, lse, mixed = [None] * tiles, [None] * tiles, [None] * half_tiles
    row = seg_row
    for k in range(half_tiles):
        for t in (half_tiles + k, k):
            own = t < half_tiles
            context[t], lse[t], *part = attention_tile(
                qkv, w_out, seg_column, row, t, wide if own else low, 1 if own else 2 + 2 * k
            )
            if not own:
                sent = [core_swap(value) for value in part]
                row = after(seg_row, *part)
        mixed[k] = add_low(part[0], sent)
        row = after(seg_row, mixed[k])
    came = [chip_swap(value) for value in mixed]
    def mix(mine_part, other_part):
        return add_low(mine_part, [core_swap(other_part)])

    normed_one, inverse_one, first_mine, first_other, first_norm = [], [], [], [], []
    hid_mine, hid_other, slope_mine, slope_other = [], [], [], []
    ffn_mixed = []
    up_row = bias_up[None, :]
    ready = mixed[1]
    for k in range(2):
        normed_k, inverse_k, rows_wide, *rows_low = norm_rows(
            place, mixed[k], came[k], cut(x_mine, k), after(vectors, ready), (0, 2, 3), True
        )
        normed_one.append(normed_k)
        inverse_one.append(inverse_k)
        first_norm.append(rows_wide)
        first_mine += rows_low
        rows_other = [core_swap(value) for value in rows_low]
        first_other += rows_other
        mine_part, hid, slope = feed_forward(rows_low, w_up, up_row, w_down)
        hid_mine.append(hid)
        slope_mine.append(slope)
        other_part, hid, slope = feed_forward(
            rows_other, w_up, after(up_row, mine_part), w_down
        )
        hid_other.append(hid)
        slope_other.append(slope)
        ready = other_part
        ffn_mixed.append(mix(mine_part, other_part))
    mixed = ffn_mixed
    came = [chip_swap(value) for value in mixed]
    normed_two, inverse_two, out_mine, out_other, pieces = [], [], [], [], []
    exchange = [(s, s ^ half_dp) for s in range(dp_count)]
    for k in range(2):
        normed_k, inverse_k, out_piece, out_k = norm_rows(
            place, mixed[k], came[k], first_norm[k], vectors, (1, 4, 5), False
        )
        normed_two.append(normed_k)
        inverse_two.append(inverse_k)
        out_mine.append(out_k)
        out_other.append(core_swap(out_k))
        mine = lax.ppermute(out_piece, "dp", exchange)
        pieces += [mine, chip_swap(mine)]

    output_part = in_order(place, out_mine, out_other)
    pieces = pieces + [core_swap(value) for value in pieces]
    linked = link_back(
        place,
        link,
        seg_column,
        output_cot,
        out_mine,
        normed_two,
        inverse_two,
        vectors,
        pieces,
        score_cot.shape[1],
    )
    second_grad, second_mine = list(linked[:2]), list(linked[2:4])
    sums_two, score_part = linked[4], linked[5]
    second_other = [core_swap(value) for value in second_mine]
    pre_mine, pre_other, mixed = [], [], []
    for k in range(2):
        mine_low = after(second_mine[k], other_part) if k else second_mine[k]
        mine_part, pre = feed_back(mine_low, slope_mine[k], w_up, w_down)
        pre_mine.append(pre)
        other_low = after(second_other[k], mine_part)
        other_part, pre = feed_back(other_low, slope_other[k], w_up, w_down)
        pre_other.append(pre)
        mixed.append(mix(mine_part, other_part))
    came = [chip_swap(value) for value in mixed]
    grad_down, grad_up, up_grad = feed_grads(
        hid_mine + hid_other,
        second_mine + second_other,
        first_mine + first_other,
        pre_mine + pre_other,
    )

    rotated_old = rotate_first(after(block_first, mixed[1]), basis_left, basis_right)
    ready = (vectors, grad_down, grad_up, up_grad, rotated_old, output_part)
    late_vectors, grad_down, grad_up, up_grad, rotated_old, output_part = (
        lax.optimization_barrier(ready)
    )

    first_grad, sums_one, attn_mine, attn_other, carried = [], [], [], [], None

    def attention_part(some):
        rows_grads = attn_mine + attn_other
        return attention_backward(
            qkv,
            w_out,
            seg_column,
            seg_row,
            some,
            [context[t] for t in some],
            sum([rows_grads[t] for t in some], []),
            [lse[t] for t in some],
            carried,
        )

    for k in range(2):
        grad_k, sums_k, *low_k = first_back(
            mixed[k],
            came[k],
            second_grad[k],
            normed_one[k],
            inverse_one[k],
            late_vectors if carried is None else after(late_vectors, *carried),
        )
        first_grad.append(grad_k)
        sums_one.append(sums_k)
        attn_mine.append(low_k)
        attn_other.append([core_swap(value) for value in low_k])
        if k == 0:
            attn_mine.append(None)
            carried = attention_part([0, half_tiles])
            attn_mine.pop()
    shared = pack_sums(place, sums_one, sums_two, score_part)
    shared_came = core_swap(shared)
    seg_row = after(seg_row, shared)
    carried = attention_part([1, half_tiles + 1])
    qkv_grad, grad_out, pair_bias = carried
    grad_qkv = mul(x_rows, qkv_grad, TN).astype(low)
    bounds = piece_bounds(owned, 4)
    piece_count = len(bounds) - 1
    staged = spread(
        place,
        order_list,
        [grad_qkv, grad_out, grad_up, grad_down],
        side,
        dp_count,
        owned,
        bounds,
    )

    small = add_biases(shared, shared_came, pair_bias, up_grad)
    stride = 1
    input_stage = 0
    travelling = [staged[k * dp_count] for k in range(piece_count)]
    for step in range(dp_count - 1):
        for k in range(piece_count):
            came = lax.ppermute(travelling[k], "dp", routes[k % 2])
            if step < dp_count - 2:
                local = staged[k * dp_count + step + 1]
                if step or k:
                    local = after(local, travelling[k - 1])
                if k == 0 and step in (2, 4):
                    local = after(local, small_came)
                if step == 4:
                    came = add_low(came, [local])
                else:
                    came = (came.astype(wide) + local.astype(wide)).astype(low)
            travelling[k] = came
        if step >= dp_count - 2:
            continue
        mark = travelling[piece_count - 1]
        if step % 2 == 0 and stride < dp_count:
            if stride > 1:
                small = after(small, mark) + small_came
            else:
                small = after(small, mark)
            pairs = [(s, s ^ stride) for s in range(dp_count)]
            small_came = lax.ppermute(small, "dp", pairs)
            stride *= 2
        if step == 0:
            late_grad = after(qkv_grad, mark)
            other_part = core_swap(mul(late_grad[half:], w_qkv, NT).astype(low))
            mine_part = mul(late_grad[:half], w_qkv, NT)
        if step == 1:
            mine_part = after(mine_part, mark)
            input_mixed = add_low(mine_part, [other_part])
            input_came = chip_swap(input_mixed)
        if step == 4:
            branch_zero = after(input_mixed, mark).astype(wide) + input_came.astype(wide)
            input_mine = (jnp.concatenate(first_grad, axis=0) + branch_zero).astype(low)
            input_other = core_swap(input_mine)
    small = small + small_came
    while stride < dp_count:
        small = small + lax.ppermute(small, "dp", [(s, s ^ stride) for s in range(dp_count)])
        stride *= 2
    bias_out, norm_out, scores, small_values = small_update(
        place, small, bias_state, norm_state, local_width, *score_cot.shape
    )
    local = [staged[(k + 1) * dp_count - 1] for k in range(piece_count)]

    input_grad = in_order(place, [input_mine], [input_other])
    travelling[0] = after(travelling[0], input_grad)
    owned_grad, first_new, second_new, master_new = optimize(
        travelling,
        local,
        rotated_old,
        block_master,
        block_first,
        block_second,
        basis_left,
        basis_right,
    )
    small_values, master_new = lax.optimization_barrier((small_values, master_new))
    small_values = small_values.reshape(-1)
    return (
        output_part,
        scores,
        input_grad,
        owned_grad,
        first_new,
        second_new,
        master_new,
        bias_out,
        norm_out,
        small_values,
    )


def solution(mesh):
    blocks = P(("dp", "mp"), None, None)
    rows = P("dp", None)
    return jax.shard_map(
        body,
        mesh=mesh,
        in_specs=(rows, rows, P(), P(), P(), P(), P(), P("mp", None))
        + (blocks,) * 5
        + (P(None, "mp"), P()),
        out_specs=(rows, P(), rows) + (blocks,) * 4 + (P(None, "mp"), P(), P("mp")),
        check_vma=False,
    )
```
